32 devices in a mesh: dp: 16 (over z, y, x), tensor: 2 (over core).
Axes of the slice: x: 2, y: 2, z: 4, core: 2. Of those that a mesh axis runs over, the one named last changes fastest.
Arguments:
- tokens: bfloat16 [16384, 768], P('dp'), may hold values from -6 to 6
- lengths: int32 [16, 6], P('dp'), may hold values from 1 to 768, 1024 in all within a row
- gene_ids: int32 [16384], P('dp'), may hold values from 0 to 35999
- norm1_gain: float32 [768], replicated, may hold values from 0.5 to 1.5
- norm1_shift: float32 [768], replicated, may hold values from -1.75 to 1.75
- qkv_weight: bfloat16 [768, 3, 768], P(None, None, 'tensor'), may hold values from -0.21875 to 0.21875
- qv_bias: float32 [2, 768], P(None, 'tensor'), may hold values from -1.75 to 1.75
- out_weight: bfloat16 [768, 768], P('tensor'), may hold values from -0.625 to 0.625
- out_bias: float32 [768], replicated, may hold values from -1.75 to 1.75
- norm2_gain: float32 [768], replicated, may hold values from 0.5 to 1.5
- norm2_shift: float32 [768], replicated, may hold values from -1.75 to 1.75
- up_weight: bfloat16 [768, 3072], P(None, 'tensor'), may hold values from -0.21875 to 0.21875
- up_bias: float32 [3072], P('tensor'), may hold values from -1.75 to 1.75
- down_weight: bfloat16 [3072, 768], P('tensor'), may hold values from -0.109375 to 0.109375
- down_bias: float32 [768], replicated, may hold values from -1.75 to 1.75
- cotangent: bfloat16 [16384, 768], P('dp'), may hold values from -6 to 6
Outputs:
- output: bfloat16 [16384, 768], P('dp')
- input_grad: bfloat16 [16384, 768], P('dp')
- norm1_gain_grad: float32 [768], replicated
- norm1_shift_grad: float32 [768], replicated
- qkv_grad: float32 [768, 3, 768], P(None, None, 'tensor')
- qv_bias_grad: float32 [2, 768], P(None, 'tensor')
- out_grad: float32 [768, 768], P('tensor')
- out_bias_grad: float32 [768], replicated
- norm2_gain_grad: float32 [768], replicated
- norm2_shift_grad: float32 [768], replicated
- up_grad: float32 [768, 3072], P(None, 'tensor')
- up_bias_grad: float32 [3072], P('tensor')
- down_grad: float32 [3072, 768], P('tensor')
- down_bias_grad: float32 [768], replicated
- gene_counts: int32 [36000], P('tensor')
The draws below stay inside these ranges and needn't reach their ends.
Inputs may be any that keep to these rules, and one draw needn't show every extreme that they name: The lengths of one row fill the 1024 token slots of one device.
All inputs are finite; a program needn't handle non-finite values.
Results may differ from the reference program's by a relative error of at most 0.01.
Values sent between devices are 32-bit elements; how exact they have to be, the bound alone decides.
A program may use at most 192 MiB of HBM per device.

```python
import math
import jax
import jax.numpy as jnp
import numpy as np
from jax import lax

D = 768
HEADS = 12
HEAD = 64
FF = 3072
VOCAB = 36000
TOK_DEV = 1024
CELLS_DEV = 6
MOST_LEN = 768
PACKS = 16
TOKENS = 16384


def touch_ends(values, stream_key, smallest, top_value):
    longest = values.shape.index(max(values.shape))
    spots = []
    for shift in (0, 1):
        where = [jax.random.randint(jax.random.fold_in(stream_key, axis), (), 0, length) for axis, length in enumerate(values.shape)]
        where[longest] = (where[longest] + shift) % values.shape[longest]
        spots.append(tuple(where))
    return values.at[spots[0]].set(smallest).at[spots[1]].set(top_value)


def shard_levels(own_key, extent, pieces, least, high):
    factor_of, own = 1.0, jax.random.fold_in(own_key, 6)
    for axis_at, parts in pieces:
        heights = jnp.exp(jax.random.uniform(jax.random.fold_in(own, axis_at), (parts,), jnp.float32, least / len(pieces), high / len(pieces)))
        factor_of = factor_of * jnp.repeat(heights, extent[axis_at] // parts).reshape([-1 if axis == axis_at else 1 for axis in range(len(extent))])
    return factor_of


def rank_bounds(amount, slope):
    loads = [(1 << 20) // math.isqrt(rank ** slope) + 1 for rank in range(1, amount + 1)]
    deviation = 1 + sum(loads) // (1 << 30)
    return np.cumsum(np.array([max(1, weight // deviation) for weight in loads]))


def ranked(key, shape, number_of, skew):
    grid = rank_bounds(number_of, skew)
    lot = jax.random.randint(jax.random.fold_in(key, 1), shape, 0, int(grid[number_of - 1]))
    standing = jnp.searchsorted(jnp.asarray(grid, jnp.int32), lot, side="right")
    return jax.random.permutation(jax.random.fold_in(key, 2), number_of)[standing].astype(jnp.int32)


def profile(count, total, limit, skew):
    weights = [(1 << 20) // math.isqrt(standing ** skew) + 1 for standing in range(2, count + 1)]
    rest, given = total - limit - (count - 1), [1] * (count - 1)
    while rest > 0:
        movable = [i for i in range(count - 1) if given[i] < limit]
        whole, budget = sum([weights[i] for i in movable]), rest
        for i in movable:
            extra = min(limit - given[i], max(1, budget * weights[i] // whole), rest)
            given[i] = given[i] + extra
            rest = rest - extra
    return np.array([limit] + given)


def ragged_sizes(stream_key, count, total, reach, skew):
    if count == 2:
        one = jax.random.randint(stream_key, (), max(1, total - reach), min(reach, total - 1) + 1)
        return jnp.stack([one, total - one])
    tallies = jnp.asarray(profile(count, total, reach, skew), jnp.int32)
    pairs = (count - 1) // 2
    donor, sink = tallies[1:1 + 2 * pairs:2], tallies[2:2 + 2 * pairs:2]
    margin = jnp.minimum(donor - 1, reach - sink)
    moved = jax.random.randint(jax.random.fold_in(stream_key, 1), (pairs,), 0, 1 << 20) % (margin + 1)
    tallies = tallies.at[1:1 + 2 * pairs:2].set(donor - moved).at[2:2 + 2 * pairs:2].set(sink + moved)
    return tallies[jax.random.permutation(jax.random.fold_in(stream_key, 2), count)]


def noise(own_key, extent, width, most, shards=(), kind=jnp.bfloat16):
    drawn = jax.random.normal(own_key, extent, jnp.float32) * width
    if len(shards) > 0:
        drawn = shard_levels(own_key, extent, shards, -0.22, 0.18) * drawn
    return jnp.clip(drawn, min=-most, max=most).astype(kind)


def setup_inputs(seed: int = 0) -> dict:
    streams_of = jax.random.split(jax.random.key(seed), 17)
    tokens = noise(streams_of[0], (TOKENS, D), 1.0, 6.0, ((0, 16),))
    lengths = jax.vmap(lambda own: ragged_sizes(own, CELLS_DEV, TOK_DEV, MOST_LEN, 2))(jax.random.split(streams_of[1], PACKS)).reshape((PACKS, CELLS_DEV)).astype(jnp.int32)
    gene_ids = touch_ends(ranked(streams_of[2], (TOKENS,), VOCAB, 2), jax.random.fold_in(streams_of[2], 3), 0, VOCAB - 1).astype(jnp.int32)
    norm1_gain = jnp.clip(1.0 + 0.1 * jax.random.normal(streams_of[3], (D,), jnp.float32), 0.5, 1.5)
    norm1_shift = noise(streams_of[4], (D,), 0.3, 1.75, (), jnp.float32)
    qkv_weight = noise(streams_of[5], (D, 3, D), D ** -0.5, 0.21875, ((2, 2),))
    qv_bias = noise(streams_of[6], (2, D), 0.3, 1.75, ((1, 2),), jnp.float32)
    out_weight = noise(streams_of[7], (D, D), (D // 8) ** -0.5, 0.625, ((0, 2),))
    out_bias = noise(streams_of[8], (D,), 0.3, 1.75, (), jnp.float32)
    norm2_gain = jnp.clip(1.0 + 0.1 * jax.random.normal(streams_of[9], (D,), jnp.float32), 0.5, 1.5)
    norm2_shift = noise(streams_of[10], (D,), 0.3, 1.75, (), jnp.float32)
    up_weight = noise(streams_of[11], (D, FF), D ** -0.5, 0.21875, ((1, 2),))
    up_bias = noise(streams_of[12], (FF,), 0.3, 1.75, ((0, 2),), jnp.float32)
    down_weight = noise(streams_of[13], (FF, D), FF ** -0.5, 0.109375, ((0, 2),))
    down_bias = noise(streams_of[14], (D,), 0.3, 1.75, (), jnp.float32)
    cotangent = noise(streams_of[15], (TOKENS, D), 1.0, 6.0, ((0, 16),))
    return {"tokens": tokens, "lengths": lengths, "gene_ids": gene_ids, "norm1_gain": norm1_gain, "norm1_shift": norm1_shift, "qkv_weight": qkv_weight, "qv_bias": qv_bias, "out_weight": out_weight, "out_bias": out_bias, "norm2_gain": norm2_gain, "norm2_shift": norm2_shift, "up_weight": up_weight, "up_bias": up_bias, "down_weight": down_weight, "down_bias": down_bias, "cotangent": cotangent}


highest = lax.Precision.HIGHEST

@jax.custom_vjp
def low(v):
    return lax.optimization_barrier(v.astype(jnp.bfloat16)).astype(jnp.float32)

@jax.custom_vjp
def low_back(v):
    return v

def low_keep(v):
    return (low(v), None)

def low_pass(kept, grad):
    return (grad,)

def back_keep(v):
    return (v, None)

def back_low(kept, grad):
    return (low(grad),)
low.defvjp(low_keep, low_pass)
low_back.defvjp(back_keep, back_low)

def layer_norm(field, norm_gain, norm_shift):
    row_mean = lax.optimization_barrier(jnp.mean(field, axis=-1, keepdims=True))
    centred = field - row_mean
    variance = lax.optimization_barrier(jnp.mean(centred * centred, axis=-1, keepdims=True))
    return centred * lax.rsqrt(variance + 1e-05) * norm_gain + norm_shift

def gelu_erf(upper_pre):
    return 0.5 * upper_pre * (1.0 + jax.scipy.special.erf(upper_pre * 0.7071067811865476))

def cell_mask(length_row):
    position = jnp.arange(TOK_DEV, dtype=jnp.int32)
    cell_ends = jnp.cumsum(length_row).astype(jnp.int32)
    segment = lax.optimization_barrier(jnp.sum((position[:, None] >= cell_ends[None, :]).astype(jnp.int32), axis=1))
    return segment[:, None] == segment[None, :]

def encoder_block(inputs, same_cell, params):
    gain_one, shift_one, qkv_w, qv_b, out_w, out_b, gain_two, shift_two, up_w, up_b, down_w, down_b = params
    normed1 = low(layer_norm(inputs, gain_one, shift_one))
    qkv_all = jnp.einsum('td,dcf->tcf', normed1, qkv_w, precision=highest)
    queries = low(low_back(qkv_all[:, 0] + qv_b[0])).reshape(TOK_DEV, HEADS, HEAD)
    key_rows = low(low_back(qkv_all[:, 1])).reshape(TOK_DEV, HEADS, HEAD)
    values = low(low_back(qkv_all[:, 2] + qv_b[1])).reshape(TOK_DEV, HEADS, HEAD)
    scores = jnp.einsum('qhe,khe->hqk', queries, key_rows, precision=highest) * HEAD ** (-0.5)
    scores = low_back(jnp.where(same_cell[None], scores, -1000000000.0))
    row_peak = lax.optimization_barrier(jnp.max(scores, axis=-1, keepdims=True))
    exponent = jnp.exp(scores - row_peak)
    probabilities = exponent / lax.optimization_barrier(jnp.sum(exponent, axis=-1, keepdims=True))
    context = jnp.einsum('hqk,khe->qhe', low(probabilities), values, precision=highest)
    context = low(low_back(context)).reshape(TOK_DEV, D)
    branch = low_back(jnp.dot(context, out_w, precision=highest) + out_b)
    hidden = inputs + branch
    normed2 = low(layer_norm(hidden, gain_two, shift_two))
    upper_pre = low_back(jnp.dot(normed2, up_w, precision=highest) + up_b)
    active = low(gelu_erf(upper_pre))
    ffn_out = low_back(jnp.dot(active, down_w, precision=highest) + down_b)
    return hidden + ffn_out

def reference(tokens, lengths, gene_ids, norm1_gain, norm1_shift, qkv_weight, qv_bias, out_weight, out_bias, norm2_gain, norm2_shift, up_weight, up_bias, down_weight, down_bias, cotangent):
    params = tuple((arr.astype(jnp.float32) for arr in (norm1_gain, norm1_shift, qkv_weight, qv_bias, out_weight, out_bias, norm2_gain, norm2_shift, up_weight, up_bias, down_weight, down_bias)))
    packed_in = tokens.astype(jnp.float32).reshape(PACKS, TOK_DEV, D)
    packed_cot = cotangent.astype(jnp.float32).reshape(PACKS, TOK_DEV, D)

    def one_pack(carried, packed):
        inputs, length_row, cot_rows = packed
        same_cell = cell_mask(length_row)

        def forward(inputs_now, params_now):
            return encoder_block(inputs_now, same_cell, params_now)
        result, pull = jax.vjp(forward, inputs, params)
        grad_in, grad_params = pull(cot_rows)
        carried = jax.tree.map(lambda left, right: left + right, carried, grad_params)
        return (carried, (result.astype(jnp.bfloat16), grad_in.astype(jnp.bfloat16)))
    zeros_start = jax.tree.map(jnp.zeros_like, params)
    grads, (outputs, input_grads) = lax.scan(one_pack, zeros_start, (packed_in, lengths, packed_cot))
    gene_counts = jnp.zeros((VOCAB,), jnp.int32).at[gene_ids].add(1)
    return (outputs.reshape(TOKENS, D), input_grads.reshape(TOKENS, D), grads[0], grads[1], grads[2], grads[3], grads[4], grads[5], grads[6], grads[7], grads[8], grads[9], grads[10], grads[11], gene_counts)
```

```python
import functools

import jax
import jax.numpy as jnp
from jax import lax
from jax.experimental import pallas as pl
from jax.experimental.pallas import tpu as pltpu
from jax.sharding import PartitionSpec as P

HEAD = 64
VOCAB = 36000
MESH = pl.DeviceIdType.MESH


def bit_of(dp, m):
    return lax.rem(lax.div(dp, m), 2)

class Engine:
    def __init__(self, n_dp, rows, n_chunks, g, r, o, ssem, rsem, osem):
        self.g, self.r, self.o, self.ssem, self.rsem, self.osem = g, r, o, ssem, rsem, osem
        self.bits = n_dp.bit_length() - 1
        self.half = min(self.bits, 4)
        self.rows = rows
        self.n = n_chunks
        self.dp = lax.axis_index("dp"); self.t = lax.axis_index("tensor")
        self.flat = self.bits - self.half
        self.stages = 2 * self.half + self.flat

    def order(self, c, p, k):
        if p == 0: o = [0, 1, 2]
        elif p == 1: o = [1, 0, 2]
        else: o = [2, None, None]
        if self.bits < 3: return 1 << k
        if k >= 3: return 1 << k
        if o[k] is not None: return 1 << o[k]
        odd = lax.rem(c, 2)
        return 1 + odd if k == 1 else 2 - odd

    def region(self, c, p, depth):
        off = 0
        for k in range(depth):
            off = off + bit_of(self.dp, self.order(c, p, k)) * (self.rows >> (k + 1))
        return off

    def copy(self, c, p, s):
        g, r, rows, H = self.g, self.r, self.rows, self.half
        if s < H:
            k = s; h = rows >> (s + 1)
            m = self.order(c, p, k); b = bit_of(self.dp, m)
            src = g.at[c, p, pl.ds(pl.multiple_of(self.region(c, p, k) + (1 - b) * h, 8), h)]
            base = rows - (rows >> s)
            dst = r.at[c, p, pl.ds(base, h)]
        elif s < H + self.flat:
            k = s; h = rows >> H
            m = self.order(c, p, k); b = bit_of(self.dp, m)
            src = g.at[c, p, pl.ds(pl.multiple_of(self.region(c, p, H), 8), h)]
            dst = r.at[c, p, pl.ds(rows - h + (s - H) * h, h)]
        else:
            k = self.stages - 1 - s; h = rows >> (k + 1)
            m = self.order(c, p, k); b = bit_of(self.dp, m)
            at = pl.ds(pl.multiple_of(self.region(c, p, k + 1), 8), h)
            dst = self.o.at[c, p, at]; src = g.at[c, p, at] if s == self.stages - self.half else dst
        partner = self.dp + m * (1 - 2 * b)
        return pltpu.make_async_remote_copy(src, dst, self.ssem.at[c, p, s], self.rsem.at[c, p, s],
                                            device_id=(partner, self.t), device_id_type=MESH)

    def add(self, c, p, s):
        g, r, rows, H = self.g, self.r, self.rows, self.half
        if s < H:
            h = rows >> (s + 1); base = rows - (rows >> s)
            at = pl.ds(pl.multiple_of(self.region(c, p, s + 1), 8), h)
        elif s < H + self.flat:
            h = rows >> H; base = rows - h + (s - H) * h
            at = pl.ds(pl.multiple_of(self.region(c, p, H), 8), h)
        else:
            return
        g[c, p, at] = g[c, p, at] + r[c, p, pl.ds(base, h)]

    def keep(self, c, p):
        at = pl.ds(pl.multiple_of(self.region(c, p, self.half), 8), self.rows >> self.half)
        return pltpu.make_async_copy(self.g.at[c, p, at], self.o.at[c, p, at], self.osem.at[c, p])

    def tick(self, tau, parts, done=None):
        for s in range(self.stages + 1):
            c = tau - s
            @pl.when((c >= 0) & (c < self.n))
            def _():
                if s > 0:
                    for p in range(parts):
                        self.copy(c, p, s - 1).wait()
                        self.add(c, p, s - 1)
                        if s == self.stages - self.half:
                            self.keep(c, p).start()
                        if s == self.stages - self.half + 1:
                            self.keep(c, p).wait()
                        if s < self.stages:
                            self.copy(c, p, s).start()
                else:
                    for p in range(parts):
                        self.copy(c, p, s).start()
                if s == self.stages and done is not None:
                    done(c)

    def r_rows(self):
        return self.rows - (self.rows >> self.half) + self.flat * (self.rows >> self.half)

def barrier(n_dp, with_core=True):
    dp = lax.axis_index("dp"); t = lax.axis_index("tensor")
    bar = pltpu.get_barrier_semaphore()
    n = 0
    for k in range(n_dp.bit_length() - 1):
        m = 1 << k
        b = bit_of(dp, m)
        pl.semaphore_signal(bar, inc=1, device_id=(dp + m * (1 - 2 * b), t), device_id_type=MESH); n += 1
    pl.semaphore_wait(bar, n)

def kern(n_dp, n_chunks, rows, parts, x, o, g, r, ssem, rsem, lsem, osem):
    ld = pltpu.make_async_copy(x, g, lsem); ld.start()
    barrier(n_dp)
    ld.wait()
    e = Engine(n_dp, rows, n_chunks, g, r, o, ssem, rsem, osem)
    def body(tau, carry):
        e.tick(tau, parts); return carry
    lax.fori_loop(0, n_chunks + e.stages, body, 0)

def allreduce(n_dp, n_chunks=18, rows=256, parts=3, cols=256):
    bits = n_dp.bit_length()-1; half=min(bits,4); stages = 2*half + bits-half
    rr = rows - (rows >> half) + (bits-half) * (rows >> half)
    def f(x):
        return pl.pallas_call(functools.partial(kern, n_dp, n_chunks, rows, parts),
            out_shape=jax.ShapeDtypeStruct((n_chunks, parts, rows, cols), jnp.float32),
            in_specs=[pl.BlockSpec(memory_space=pl.ANY)],
            out_specs=pl.BlockSpec(memory_space=pl.ANY),
            scratch_shapes=[pltpu.VMEM((n_chunks, parts, rows, cols), jnp.float32), pltpu.VMEM((n_chunks, parts, rr, cols), jnp.float32),
              pltpu.SemaphoreType.DMA((n_chunks, parts, stages)), pltpu.SemaphoreType.DMA((n_chunks, parts, stages)), pltpu.SemaphoreType.DMA, pltpu.SemaphoreType.DMA((n_chunks, parts))],
            compiler_params=pltpu.CompilerParams(collective_id=0, has_side_effects=True, vmem_limit_bytes=60<<20),
        )(x)
    return f


def pack(down, up, out, qkv):
    return jnp.concatenate(
        [
            down.reshape(6, 256, 3, 256).transpose(0, 2, 1, 3),
            up.reshape(3, 256, 6, 256).transpose(2, 0, 1, 3),
            jnp.concatenate([out.reshape(-1), qkv.reshape(-1)]).reshape(6, 3, 256, 256),
        ]
    )


def unpack(packed, down, up, out, qkv):
    rest = packed[12:].reshape(-1)
    return (
        packed[:6].transpose(0, 2, 1, 3).reshape(down.shape),
        packed[6:12].transpose(1, 2, 0, 3).reshape(up.shape),
        rest[: out.size].reshape(out.shape),
        rest[out.size :].reshape(qkv.shape),
    )


def layer_norm(field, norm_gain, norm_shift):
    row_mean = jnp.mean(field, axis=-1, keepdims=True)
    centred = field - row_mean
    variance = jnp.mean(centred * centred, axis=-1, keepdims=True)
    return centred * lax.rsqrt(variance + 1e-05) * norm_gain + norm_shift


def gelu_erf(upper_pre):
    return 0.5 * upper_pre * (1.0 + jax.scipy.special.erf(upper_pre * 0.7071067811865476))


def cell_mask(length_row, tok_rows):
    position = jnp.arange(tok_rows, dtype=jnp.int32)
    cell_ends = jnp.cumsum(length_row)
    segment = jnp.sum((position[:, None] >= cell_ends[None, :]).astype(jnp.int32), axis=1)
    return segment[:, None] == segment[None, :]


def over_rows(left, right):
    return lax.dot_general(
        left, right, (((0,), (0,)), ((), ())), preferred_element_type=jnp.float32
    )


def by_transpose(left, right):
    return lax.dot_general(
        left, right, (((1,), (1,)), ((), ())), preferred_element_type=jnp.float32
    )


def count_genes(gene_ids, vocab_start, vocab_local):
    tok_rows = gene_ids.shape[0]
    block_rows = min(128, tok_rows)
    shifted = (gene_ids - vocab_start).reshape(tok_rows // block_rows, block_rows)
    column_ids = jnp.arange(vocab_local, dtype=jnp.int32)
    ones_row = jnp.ones((1, block_rows), jnp.bfloat16)

    def add_block(counted, block_ids):
        onehot = (block_ids[:, None] == column_ids[None, :]).astype(jnp.bfloat16)
        return (counted + jnp.dot(ones_row, onehot, preferred_element_type=jnp.float32)[0], None)

    counted, unused = lax.scan(add_block, jnp.zeros((vocab_local,), jnp.float32), shifted)
    return counted


def attention_scores(queries, key_rows, same_cell):
    scores = jnp.einsum(
        "qhe,khe->hqk", queries, key_rows, preferred_element_type=jnp.float32
    ) * HEAD ** (-0.5)
    return jnp.where(same_cell[None], scores, -1000000000.0)


def on_device(
    tokens,
    lengths,
    gene_ids,
    norm1_gain,
    norm1_shift,
    qkv_weight,
    qv_bias,
    out_weight,
    out_bias,
    norm2_gain,
    norm2_shift,
    up_weight,
    up_bias,
    down_weight,
    down_bias,
    cotangent,
):
    tok_rows = tokens.shape[0]
    features = tokens.shape[1]
    head_cols = qkv_weight.shape[2]
    local_heads = head_cols // HEAD
    vocab_local = VOCAB // lax.axis_size("tensor")
    gene_total = count_genes(gene_ids, lax.axis_index("tensor") * vocab_local, vocab_local)
    same_cell = cell_mask(lengths[0], tok_rows)
    inputs = tokens.astype(jnp.float32)
    normed1_f, norm1_pull = jax.vjp(layer_norm, inputs, norm1_gain, norm1_shift)
    normed1 = normed1_f.astype(jnp.bfloat16)
    qkv_flat = qkv_weight.reshape(features, 3 * head_cols)
    qkv_all = jnp.dot(normed1, qkv_flat, preferred_element_type=jnp.float32)
    queries = (
        (qkv_all[:, :head_cols] + qv_bias[0])
        .astype(jnp.bfloat16)
        .reshape(tok_rows, local_heads, HEAD)
    )
    key_rows = (
        qkv_all[:, head_cols : 2 * head_cols]
        .astype(jnp.bfloat16)
        .reshape(tok_rows, local_heads, HEAD)
    )
    values = (
        (qkv_all[:, 2 * head_cols :] + qv_bias[1])
        .astype(jnp.bfloat16)
        .reshape(tok_rows, local_heads, HEAD)
    )
    scores = attention_scores(queries, key_rows, same_cell)
    row_peak = jnp.max(scores, axis=-1, keepdims=True)
    exponent = jnp.exp(scores - row_peak)
    row_sum = jnp.sum(exponent, axis=-1, keepdims=True)
    log_total = row_peak + jnp.log(row_sum)
    probs_low = (exponent / row_sum).astype(jnp.bfloat16)
    context = jnp.einsum("hqk,khe->qhe", probs_low, values, preferred_element_type=jnp.float32)
    context = context.astype(jnp.bfloat16).reshape(tok_rows, head_cols)
    attn_terms = jnp.dot(context, out_weight, preferred_element_type=jnp.float32)
    hidden = inputs + lax.psum(attn_terms, "tensor") + out_bias
    normed2_f, norm2_pull = jax.vjp(layer_norm, hidden, norm2_gain, norm2_shift)
    normed2 = normed2_f.astype(jnp.bfloat16)
    upper_pre = jnp.dot(normed2, up_weight, preferred_element_type=jnp.float32) + up_bias
    active_f, gelu_pull = jax.vjp(gelu_erf, upper_pre)
    active = active_f.astype(jnp.bfloat16)
    ffn_terms = jnp.dot(active, down_weight, preferred_element_type=jnp.float32)
    output = (hidden + lax.psum(ffn_terms, "tensor") + down_bias).astype(jnp.bfloat16)
    grad_output = cotangent.astype(jnp.float32)
    down_bias_grad = jnp.sum(grad_output, axis=0)
    down_grad = over_rows(active, cotangent)
    grad_active = by_transpose(cotangent, down_weight)
    grad_upper = gelu_pull(grad_active)[0].astype(jnp.bfloat16)
    up_bias_grad = jnp.sum(grad_upper.astype(jnp.float32), axis=0)
    up_grad = over_rows(normed2, grad_upper)
    grad_normed2 = lax.psum(by_transpose(grad_upper, up_weight), "tensor")
    grad_hidden_norm, norm2_gain_grad, norm2_shift_grad = norm2_pull(grad_normed2)
    grad_hidden = grad_output + grad_hidden_norm
    grad_branch = grad_hidden.astype(jnp.bfloat16)
    out_bias_grad = jnp.sum(grad_branch.astype(jnp.float32), axis=0)
    out_grad = over_rows(context, grad_branch)
    grad_context = (
        by_transpose(grad_branch, out_weight)
        .astype(jnp.bfloat16)
        .reshape(tok_rows, local_heads, HEAD)
    )
    again = attention_scores(queries, key_rows, same_cell)
    probabilities = jnp.exp(again - log_total)
    probs_again = probabilities.astype(jnp.bfloat16)
    grad_values = jnp.einsum(
        "hqk,qhe->khe", probs_again, grad_context, preferred_element_type=jnp.float32
    )
    grad_probs = jnp.einsum(
        "qhe,khe->hqk", grad_context, values, preferred_element_type=jnp.float32
    )
    grad_scores = probabilities * (
        grad_probs - jnp.sum(probabilities * grad_probs, axis=-1, keepdims=True)
    )
    grad_scores = grad_scores.astype(jnp.bfloat16)
    grad_query = jnp.einsum(
        "hqk,khe->qhe", grad_scores, key_rows, preferred_element_type=jnp.float32
    ) * HEAD ** (-0.5)
    grad_keys = jnp.einsum(
        "hqk,qhe->khe", grad_scores, queries, preferred_element_type=jnp.float32
    ) * HEAD ** (-0.5)
    grad_qkv = jnp.concatenate(
        [
            grad_query.reshape(tok_rows, head_cols),
            grad_keys.reshape(tok_rows, head_cols),
            grad_values.reshape(tok_rows, head_cols),
        ],
        axis=1,
    ).astype(jnp.bfloat16)
    grad_qkv_f = grad_qkv.astype(jnp.float32)
    qv_bias_grad = jnp.stack(
        [
            jnp.sum(grad_qkv_f[:, :head_cols], axis=0),
            jnp.sum(grad_qkv_f[:, 2 * head_cols :], axis=0),
        ]
    )
    qkv_grad = over_rows(normed1, grad_qkv).reshape(features, 3, head_cols)
    grad_normed1 = lax.psum(by_transpose(grad_qkv, qkv_flat), "tensor")
    grad_input_norm, norm1_gain_grad, norm1_shift_grad = norm1_pull(grad_normed1)
    input_grad = (grad_hidden + grad_input_norm).astype(jnp.bfloat16)
    packed = pack(down_grad, up_grad, out_grad, qkv_grad)
    packed = allreduce(lax.axis_size("dp"), packed.shape[0])(packed)
    down_grad, up_grad, out_grad, qkv_grad = unpack(packed, down_grad, up_grad, out_grad, qkv_grad)
    (
        norm1_gain_grad,
        norm1_shift_grad,
        qv_bias_grad,
        out_bias_grad,
        norm2_gain_grad,
        norm2_shift_grad,
        up_bias_grad,
        down_bias_grad,
        gene_total,
    ) = lax.psum(
        (
            norm1_gain_grad,
            norm1_shift_grad,
            qv_bias_grad,
            out_bias_grad,
            norm2_gain_grad,
            norm2_shift_grad,
            up_bias_grad,
            down_bias_grad,
            gene_total,
        ),
        "dp",
    )
    gene_counts = gene_total.astype(jnp.int32)
    return (
        output,
        input_grad,
        norm1_gain_grad,
        norm1_shift_grad,
        qkv_grad,
        qv_bias_grad,
        out_grad,
        out_bias_grad,
        norm2_gain_grad,
        norm2_shift_grad,
        up_grad,
        up_bias_grad,
        down_grad,
        down_bias_grad,
        gene_counts,
    )


def solution(mesh):
    return jax.shard_map(
        on_device,
        mesh=mesh,
        in_specs=(
            P("dp", None),
            P("dp", None),
            P("dp"),
            P(),
            P(),
            P(None, None, "tensor"),
            P(None, "tensor"),
            P("tensor", None),
            P(),
            P(),
            P(),
            P(None, "tensor"),
            P("tensor"),
            P("tensor", None),
            P(),
            P("dp", None),
        ),
        out_specs=(
            P("dp", None),
            P("dp", None),
            P(),
            P(),
            P(None, None, "tensor"),
            P(None, "tensor"),
            P("tensor", None),
            P(),
            P(),
            P(),
            P(None, "tensor"),
            P("tensor"),
            P("tensor", None),
            P(),
            P("tensor"),
        ),
        check_vma=False,
    )
```

```python
import functools

import jax
import jax.numpy as jnp
from jax import lax
from jax.experimental import pallas as pl
from jax.experimental.pallas import tpu as pltpu
from jax.sharding import PartitionSpec as P

HEAD = 64
VOCAB = 36000
MESH = pl.DeviceIdType.MESH
F32, BF16 = jnp.float32, jnp.bfloat16
BLK = 256
PARTS = 3
SLOTS = 6
LANES = 128


def mm(left, right):
    return jnp.dot(left, right, preferred_element_type=F32)


def mm_t(left, right):
    return lax.dot_general(left, right, (((1,), (1,)), ((), ())), preferred_element_type=F32)


def bit_of(index, mask):
    return lax.rem(lax.div(index, mask), 2)


def rows_at(index, size):
    return pl.ds(pl.multiple_of(index * size, size), size)


class Exchange:
    def __init__(self, n_dp, chunks, parts, slots, g, r, o, ssem, rsem, osem):
        self.chunks, self.parts, self.slots = chunks, parts, slots
        self.g, self.r, self.o = g, r, o
        self.ssem, self.rsem, self.osem = ssem, rsem, osem
        self.rows = g.shape[2]
        self.bits, self.half, self.stages = stage_counts(n_dp)
        self.dp, self.core = lax.axis_index("dp"), lax.axis_index("tensor")

    def mask(self, c, p, k):
        if k >= 3 or self.bits < 3 or p == 0:
            return 1 << k
        if p == 1:
            return 1 << (1, 0, 2)[k]
        if k == 0:
            return 4
        odd = lax.rem(c, 2)
        return 1 + odd if k == 1 else 2 - odd

    def first(self, c, p, depth):
        at = 0
        for k in range(depth):
            at = at + bit_of(self.dp, self.mask(c, p, k)) * (self.rows >> (k + 1))
        return at

    def slot(self, s):
        if s < self.half:
            return pl.ds(self.rows - (self.rows >> s), self.rows >> (s + 1))
        size = self.rows >> self.half
        return pl.ds(self.rows - size + (s - self.half) * size, size)

    def own(self, c, p, depth):
        return pl.ds(pl.multiple_of(self.first(c, p, depth), 8), self.rows >> depth)

    def copy(self, c, p, s):
        flat_end = self.stages - self.half
        k = s if s < flat_end else self.stages - 1 - s
        mask = self.mask(c, p, k)
        bit = bit_of(self.dp, mask)
        if s < self.half:
            size = self.rows >> (s + 1)
            away = pl.ds(pl.multiple_of(self.first(c, p, s) + (1 - bit) * size, 8), size)
            src = self.g.at[c, p, away]
        elif s < flat_end:
            src = self.g.at[c, p, self.own(c, p, self.half)]
        if s < flat_end:
            dst = self.r.at[lax.rem(c, self.slots), p, self.slot(s)]
        else:
            mine = self.own(c, p, k + 1)
            dst = self.o.at[c, p, mine]
            src = self.g.at[c, p, mine] if s == flat_end else dst
        return pltpu.make_async_remote_copy(
            src,
            dst,
            self.ssem.at[c, p, s],
            self.rsem.at[c, p, s],
            device_id=(self.dp + mask * (1 - 2 * bit), self.core),
            device_id_type=MESH,
        )

    def keep(self, c, p):
        mine = self.own(c, p, self.half)
        return pltpu.make_async_copy(self.g.at[c, p, mine], self.o.at[c, p, mine], self.osem.at[c, p])

    def tick(self, tau):
        flat_end = self.stages - self.half
        for s in range(self.stages + 1):
            c = tau - s

            @pl.when((c >= 0) & (c < self.chunks))
            def _():
                for p in range(self.parts):
                    if s > 0:
                        self.copy(c, p, s - 1).wait()
                    if 0 < s <= flat_end:
                        mine = self.own(c, p, min(s, self.half))
                        got = self.r[lax.rem(c, self.slots), p, self.slot(s - 1)]
                        self.g[c, p, mine] = self.g[c, p, mine] + got
                    if s == flat_end:
                        self.keep(c, p).start()
                    if s == flat_end + 1:
                        self.keep(c, p).wait()
                    if s < self.stages:
                        self.copy(c, p, s).start()


def stage_counts(n_dp):
    bits = n_dp.bit_length() - 1
    half = min(bits, 4)
    return bits, half, bits + half


def slot_rows(n_dp, rows):
    bits, half, _ = stage_counts(n_dp)
    return rows - (rows >> half) + (bits - half) * (rows >> half)


def normalise(x):
    c = x - jnp.mean(x, axis=-1, keepdims=True)
    scale = lax.rsqrt(jnp.mean(c * c, axis=-1, keepdims=True) + 1e-05)
    return c * scale, scale


def norm_back(x_hat, scale, grad):
    middle = jnp.mean(grad, axis=-1, keepdims=True)
    along = jnp.mean(grad * x_hat, axis=-1, keepdims=True)
    return (grad - middle - x_hat * along) * scale


def total(x):
    return jnp.sum(x.astype(F32), axis=0, keepdims=True)


def put_rows(ref, row, vector):
    for i in range(vector.shape[1] // LANES):
        ref[0, 0, row + i : row + i + 1, :] = vector[:, i * LANES : (i + 1) * LANES]


def add_rows(ref, row, vector):
    for i in range(vector.shape[1] // LANES):
        at = slice(row + i, row + i + 1)
        ref[0, 0, at, :] = ref[0, 0, at, :] + vector[:, i * LANES : (i + 1) * LANES]


def small_plan(features, head_cols, units, vocab_local):
    plan, at = {}, 0
    for name, size in (
        ("genes", vocab_local),
        ("gain1", features),
        ("shift1", features),
        ("qbias", head_cols),
        ("vbias", head_cols),
        ("obias", features),
        ("gain2", features),
        ("shift2", features),
        ("ubias", units),
        ("dbias", features),
    ):
        count = -(-size // LANES)
        if name == "genes":
            count = -(-count // 8) * 8
        plan[name] = (at, count, size)
        at += count
    return plan, -(-at // 128) * 128


def leftover(j):
    block = 9 + j // 2
    return 13 + block // 3, block % 3, j % 2


def layer(
    n_dp,
    plan,
    lengths,
    genes,
    tok_h,
    cot_h,
    gain1,
    shift1,
    qkvw_h,
    qvb,
    outw_h,
    obias,
    gain2,
    shift2,
    upw_h,
    ubias,
    dnw_h,
    dbias,
    out_h,
    ing_h,
    o,
    o_small,
    tok,
    cot,
    qkvw,
    outw,
    upw,
    dnw,
    norm,
    norm_t,
    qs,
    ks,
    vs,
    x_t,
    ctx,
    dctx,
    dq_t,
    t1,
    t2,
    t3,
    v,
    g,
    r,
    act,
    act_t,
    gu,
    slope,
    dk_sum,
    dv_sum,
    seg,
    sg,
    sr,
    lsem,
    esend,
    erecv,
    ssem,
    rsem,
    osem,
    sssem,
    srsem,
    sosem,
    vfree,
):
    tokens, features = tok.shape
    head_cols = qs.shape[1]
    units = dnw.shape[0]
    rbs = tokens // BLK
    dp, core = lax.axis_index("dp"), lax.axis_index("tensor")
    other = (dp, 1 - core)

    loads = [
        pltpu.make_async_copy(src, dst, lsem.at[i])
        for i, (src, dst) in enumerate(
            ((tok_h, tok), (qkvw_h, qkvw), (outw_h, outw), (upw_h, upw), (cot_h, cot), (dnw_h, dnw))
        )
    ]
    for load in loads:
        load.start()

    bar = pltpu.get_barrier_semaphore()
    bits = n_dp.bit_length() - 1
    for k in range(bits):
        bit = bit_of(dp, 1 << k)
        to = (dp + (1 << k) * (1 - 2 * bit), core)
        pl.semaphore_signal(bar, inc=1, device_id=to, device_id_type=MESH)
    pl.semaphore_signal(bar, inc=1, device_id=other, device_id_type=MESH)

    big = Exchange(n_dp, g.shape[0], PARTS, SLOTS, g, r, o, ssem, rsem, osem)
    small = Exchange(n_dp, 1, 1, 1, sg, sr, o_small, sssem, srsem, sosem)

    def swap(e, src, rb):
        at = rows_at(rb, BLK)
        return pltpu.make_async_remote_copy(
            src.at[at], v.at[at], esend.at[e, rb], erecv.at[e, rb], device_id=other, device_id_type=MESH
        )

    def freed():
        pl.semaphore_signal(vfree, inc=1, device_id=other, device_id_type=MESH)

    def each(body, count=rbs):
        def step(i, carry):
            body(i)
            return carry

        lax.fori_loop(0, count, step, 0)

    def segment(position):
        ends, seg_now = 0, jnp.zeros(position.shape, jnp.int32)
        for i in range(lengths.shape[1]):
            ends = ends + lengths[0, i]
            seg_now = seg_now + (position >= ends).astype(jnp.int32)
        return seg_now

    seg[...] = segment(lax.broadcasted_iota(jnp.int32, (tokens, LANES), 0))
    sg[...] = jnp.zeros_like(sg)

    loads[0].wait()

    def first_norm(rb):
        at = rows_at(rb, BLK)
        x_hat, _ = normalise(tok[at, :].astype(F32))
        norm[at, :] = (x_hat * gain1[...] + shift1[...]).astype(BF16)

    each(first_norm)
    loads[1].wait()

    def project(rb):
        at = rows_at(rb, BLK)
        x = norm[at, :]
        qs[at, :] = (mm(x, qkvw[0]) + qvb[0:1, :]).astype(BF16) * BF16(HEAD**-0.5)
        ks[at, :] = mm(x, qkvw[1]).astype(BF16)
        vs[at, :] = (mm(x, qkvw[2]) + qvb[1:2, :]).astype(BF16)

    each(project)
    loads[2].wait()
    pl.semaphore_wait(bar, bits + 1)

    def attend(rb):
        at = rows_at(rb, BLK)
        seg_row = segment(lax.broadcasted_iota(jnp.int32, (1, tokens), 1))
        same = jnp.concatenate([seg[at, :]] * (tokens // LANES), axis=1) == seg_row
        for pair in range(head_cols // LANES):
            sides = []
            for side in range(2):
                cols = slice(pair * LANES + side * HEAD, pair * LANES + (side + 1) * HEAD)
                scores = jnp.where(same, mm_t(qs[at, cols], ks[:, cols]), -1000000000.0)
                e = jnp.exp(scores - jnp.max(scores, axis=-1, keepdims=True))
                inverse = 1.0 / jnp.sum(e, axis=-1, keepdims=True)
                sides.append(mm((e * inverse).astype(BF16), vs[:, cols]))
            ctx[at, pair * LANES : (pair + 1) * LANES] = jnp.concatenate(sides, axis=1).astype(BF16)
        t1[at, :] = mm(ctx[at, :], outw[...])
        swap(0, t1, rb).start()

    each(attend)
    loads[3].wait()
    loads[4].wait()
    loads[5].wait()

    def second_norm(rb):
        at = rows_at(rb, BLK)
        swap(0, t1, rb).wait()
        hidden = tok[at, :].astype(F32) + (t1[at, :] + v[at, :]) + obias[...]
        t1[at, :] = hidden
        x_hat, _ = normalise(hidden)
        norm[at, :] = (x_hat * gain2[...] + shift2[...]).astype(BF16)
        t2[at, :] = jnp.zeros((BLK, features), F32)
        t3[at, :] = jnp.zeros((BLK, features), F32)

    each(second_norm)
    freed()

    def feed_forward(u):
        ucols = rows_at(u, BLK)

        def upper(rb):
            at = rows_at(rb, BLK)
            up = mm(norm[at, :], upw[:, ucols]) + ubias[:, ucols]
            cdf = 0.5 * (1.0 + lax.erf(up * 0.7071067811865476))
            act[at, :] = (up * cdf).astype(BF16)
            slope[at, :] = cdf + up * (jnp.exp(-0.5 * up * up) * 0.3989422804014327)

        each(upper)
        act_t[...] = act[...].T
        for p in range(PARTS):
            g[2 * u, p] = mm(act_t[...], cot[:, p * BLK : (p + 1) * BLK])
        big.tick(u + jnp.minimum(u, 1))

        @pl.when(u == 0)
        def _():
            norm_t[...] = norm[...].T

        def lower(rb, sums):
            at = rows_at(rb, BLK)
            down_rows = dnw[ucols, :]
            grad = (mm_t(cot[at, :], down_rows) * slope[at, :]).astype(BF16)
            gu[at, :] = grad
            t2[at, :] = t2[at, :] + mm(act[at, :], down_rows)
            t3[at, :] = t3[at, :] + mm_t(grad, upw[:, ucols])
            return sums + total(grad)

        sums = lax.fori_loop(0, rbs, lower, jnp.zeros((1, BLK), F32))
        row = plan["ubias"][0] + u * (BLK // LANES)
        for i in range(BLK // LANES):
            sg[0, 0, pl.ds(row + i, 1), :] = sums[:, i * LANES : (i + 1) * LANES]
        for p in range(PARTS):
            g[2 * u + 1, p] = mm(norm_t[p * BLK : (p + 1) * BLK, :], gu[...])

        @pl.when(u == 0)
        def _():
            big.tick(1)

    each(feed_forward, units // BLK)
    tau = units // BLK + 1

    pl.semaphore_wait(vfree, 1)
    each(lambda rb: swap(1, t3, rb).start())
    big.tick(tau)
    tau += 1

    def second_norm_back(rb):
        at = rows_at(rb, BLK)
        swap(1, t3, rb).wait()
        grad = t3[at, :] + v[at, :]
        x_hat, scale = normalise(t1[at, :])
        add_rows(sg, plan["gain2"][0], total(grad * x_hat))
        add_rows(sg, plan["shift2"][0], total(grad))
        given = cot[at, :].astype(F32)
        add_rows(sg, plan["dbias"][0], total(given))
        grad = given + norm_back(x_hat, scale, grad * gain2[...])
        t3[at, :] = grad
        norm[at, :] = grad.astype(BF16)
        add_rows(sg, plan["obias"][0], total(norm[at, :]))
        dctx[at, :] = mm_t(norm[at, :], outw[...]).astype(BF16)

    each(second_norm_back)
    freed()
    pl.semaphore_wait(vfree, 1)
    each(lambda rb: swap(2, t2, rb).start())

    x_t[...] = ctx[...].T
    for p in range(PARTS):
        branch = norm[:, p * BLK : (p + 1) * BLK]
        g[12, p] = mm(x_t[:BLK, :], branch)
        rest = mm(x_t[BLK:, :], branch)
        if p < 2:
            g[17, 1, p * LANES : (p + 1) * LANES] = rest
        else:
            g[17, 2, :LANES] = rest
    big.tick(tau)
    tau += 1

    def result(rb):
        at = rows_at(rb, BLK)
        swap(2, t2, rb).wait()
        norm[at, :] = (t1[at, :] + (t2[at, :] + v[at, :]) + dbias[...]).astype(BF16)

    each(result)
    freed()
    to_out = pltpu.make_async_copy(norm, out_h, lsem.at[0])
    to_out.start()

    x_t[...] = ks[...].T

    def attend_back(step):
        pair, qb = lax.div(step, rbs), lax.rem(step, rbs)
        at = rows_at(qb, BLK)
        cols = rows_at(pair, LANES)
        position = lax.broadcasted_iota(jnp.int32, (1, BLK), 1) + qb * BLK
        seg_row = segment(position)
        same = jnp.concatenate([seg[...]] * (BLK // LANES), axis=1) == seg_row
        dks, dvs = [], []
        for side in range(2):
            lanes = slice(side * HEAD, (side + 1) * HEAD)
            q_now, d_now = qs[at, cols][:, lanes], dctx[at, cols][:, lanes]
            scores = jnp.where(same, mm_t(ks[:, cols][:, lanes], q_now), -1000000000.0)
            e = jnp.exp(scores - jnp.max(scores, axis=0, keepdims=True))
            probs = e * (1.0 / jnp.sum(e, axis=0, keepdims=True))
            grad = mm_t(vs[:, cols][:, lanes], d_now)
            inner = jnp.sum(probs * grad, axis=0, keepdims=True)
            grad = (probs * (grad - inner)).astype(BF16)
            dvs.append(mm(probs.astype(BF16), d_now))
            dks.append(mm(grad, q_now))
            hrows = pl.ds(pl.multiple_of(pair * LANES + side * HEAD, HEAD), HEAD)
            dq_t[hrows, at] = (mm(x_t[hrows, :], grad) * HEAD**-0.5).astype(BF16)
        dk_now, dv_now = jnp.concatenate(dks, axis=1), jnp.concatenate(dvs, axis=1)

        @pl.when(qb == 0)
        def _():
            dk_sum[...] = dk_now
            dv_sum[...] = dv_now

        @pl.when(qb > 0)
        def _():
            dk_sum[...] = dk_sum[...] + dk_now
            dv_sum[...] = dv_sum[...] + dv_now

        @pl.when(qb == rbs - 1)
        def _():
            ks[:, cols] = dk_sum[...].astype(BF16)
            vs[:, cols] = dv_sum[...].astype(BF16)

        @pl.when(lax.rem(step, 3) == 1)
        def _():
            big.tick(tau + lax.div(step, 3))

    steps = rbs * (head_cols // LANES)
    each(attend_back, steps)
    tau += steps // 3

    qs[...] = dq_t[...].T
    put_rows(sg, plan["qbias"][0], total(qs[...]))
    put_rows(sg, plan["vbias"][0], total(vs[...]))
    to_out.wait()
    each(first_norm)
    norm_t[...] = norm[...].T
    for i, grads in enumerate((qs, ks, vs)):
        for j in range(PARTS):
            made = mm(norm_t[j * BLK : (j + 1) * BLK, :], grads[...])
            g[13 + i, j] = made[:, :BLK]
            if i * 3 + j < 8:
                c, p, side = leftover(i * 3 + j)
                g[c, p, :, side * LANES : (side + 1) * LANES] = made[:, BLK:]
            else:
                g[17, 2, LANES:, :LANES] = made[:LANES, BLK:]
                g[17, 2, LANES:, LANES:] = made[LANES:, BLK:]
    big.tick(tau)
    tau += 1

    pl.semaphore_wait(vfree, 1)

    def to_norm(rb):
        at = rows_at(rb, BLK)
        t2[at, :] = mm_t(qs[at, :], qkvw[0]) + mm_t(ks[at, :], qkvw[1]) + mm_t(vs[at, :], qkvw[2])
        swap(3, t2, rb).start()

    each(to_norm)

    def first_norm_back(rb):
        at = rows_at(rb, BLK)
        swap(3, t2, rb).wait()
        grad = t2[at, :] + v[at, :]
        x_hat, scale = normalise(tok[at, :].astype(F32))
        add_rows(sg, plan["gain1"][0], total(grad * x_hat))
        add_rows(sg, plan["shift1"][0], total(grad))
        norm[at, :] = (t3[at, :] + norm_back(x_hat, scale, grad * gain1[...])).astype(BF16)

    each(first_norm_back)
    to_ing = pltpu.make_async_copy(norm, ing_h, lsem.at[1])
    to_ing.start()

    rows = plan["genes"][1]
    local = genes[...] - core * plan["genes"][2]
    high = lax.shift_right_arithmetic(local, 7)
    low = local - high * LANES
    high = (lax.broadcasted_iota(jnp.int32, (rows, tokens), 0) == high).astype(F32).astype(BF16)
    low = (lax.broadcasted_iota(jnp.int32, (LANES, tokens), 0) == low).astype(F32).astype(BF16)
    sg[0, 0, :rows, :] = mm_t(high, low)

    def finish(i, carry):
        big.tick(tau + i)
        small.tick(i)
        return carry

    left = g.shape[0] + big.stages - tau
    lax.fori_loop(0, max(left, small.stages + 1), finish, 0)
    to_ing.wait()


def run_layer(n_dp, plan, small_rows, *args):
    (lengths, genes, tok, cot, gain1, shift1, qkvw, qvb, outw, obias, gain2, shift2, upw, ubias, dnw, dbias) = args
    tokens, features = tok.shape
    units, head_cols = dnw.shape[0], outw.shape[0]
    chunks = (features * (2 * units + 4 * head_cols)) // (PARTS * BLK * BLK)
    _, _, stages = stage_counts(n_dp)
    vmem = pl.BlockSpec(memory_space=pltpu.VMEM)
    smem = pl.BlockSpec(memory_space=pltpu.SMEM)
    hbm = pl.BlockSpec(memory_space=pl.ANY)
    dma = pltpu.SemaphoreType.DMA
    wide = (tokens, features)
    return pl.pallas_call(
        functools.partial(layer, n_dp, plan),
        out_shape=(
            jax.ShapeDtypeStruct(wide, BF16),
            jax.ShapeDtypeStruct(wide, BF16),
            jax.ShapeDtypeStruct((chunks, PARTS, BLK, BLK), F32),
            jax.ShapeDtypeStruct((1, 1, small_rows, LANES), F32),
        ),
        in_specs=[smem, vmem, hbm, hbm, vmem, vmem, hbm, vmem, hbm, vmem, vmem, vmem, hbm, vmem, hbm, vmem],
        out_specs=(hbm, hbm, hbm, hbm),
        scratch_shapes=[
            pltpu.VMEM(wide, BF16),
            pltpu.VMEM(wide, BF16),
            pltpu.VMEM(qkvw.shape, BF16),
            pltpu.VMEM(outw.shape, BF16),
            pltpu.VMEM(upw.shape, BF16),
            pltpu.VMEM(dnw.shape, BF16),
            pltpu.VMEM(wide, BF16),
            pltpu.VMEM((features, tokens), BF16),
            pltpu.VMEM((tokens, head_cols), BF16),
            pltpu.VMEM((tokens, head_cols), BF16),
            pltpu.VMEM((tokens, head_cols), BF16),
            pltpu.VMEM((head_cols, tokens), BF16),
            pltpu.VMEM((tokens, head_cols), BF16),
            pltpu.VMEM((tokens, head_cols), BF16),
            pltpu.VMEM((head_cols, tokens), BF16),
            pltpu.VMEM(wide, F32),
            pltpu.VMEM(wide, F32),
            pltpu.VMEM(wide, F32),
            pltpu.VMEM(wide, F32),
            pltpu.VMEM((chunks, PARTS, BLK, BLK), F32),
            pltpu.VMEM((SLOTS, PARTS, slot_rows(n_dp, BLK), BLK), F32),
            pltpu.VMEM((tokens, BLK), BF16),
            pltpu.VMEM((BLK, tokens), BF16),
            pltpu.VMEM((tokens, BLK), BF16),
            pltpu.VMEM((tokens, BLK), F32),
            pltpu.VMEM((tokens, LANES), F32),
            pltpu.VMEM((tokens, LANES), F32),
            pltpu.VMEM((tokens, LANES), jnp.int32),
            pltpu.VMEM((1, 1, small_rows, LANES), F32),
            pltpu.VMEM((1, 1, slot_rows(n_dp, small_rows), LANES), F32),
            dma((6,)),
            dma((4, tokens // BLK)),
            dma((4, tokens // BLK)),
            dma((chunks, PARTS, stages)),
            dma((chunks, PARTS, stages)),
            dma((chunks, PARTS)),
            dma((1, 1, stages)),
            dma((1, 1, stages)),
            dma((1, 1)),
            pltpu.SemaphoreType.REGULAR,
        ],
        compiler_params=pltpu.CompilerParams(
            collective_id=0, has_side_effects=True, vmem_limit_bytes=63 << 20
        ),
    )(*args)


def unpack(packed, features, units, head_cols):
    down = packed[0:12:2].transpose(0, 2, 1, 3).reshape(units, features)
    up = packed[1:12:2].transpose(1, 2, 0, 3).reshape(features, units)
    out = jnp.concatenate(
        [
            packed[12].transpose(1, 0, 2).reshape(BLK, features),
            jnp.concatenate([packed[17, 1, :LANES], packed[17, 1, LANES:], packed[17, 2, :LANES]], axis=1),
        ],
        axis=0,
    )
    pieces = []
    for i in range(3):
        rows = []
        for j in range(3):
            if i * 3 + j < 8:
                c, p, side = leftover(i * 3 + j)
                rest = packed[c, p, :, side * LANES : (side + 1) * LANES]
            else:
                rest = jnp.concatenate([packed[17, 2, LANES:, :LANES], packed[17, 2, LANES:, LANES:]], axis=0)
            rows.append(jnp.concatenate([packed[13 + i, j], rest], axis=1))
        pieces.append(jnp.concatenate(rows, axis=0))
    return down, up, out, jnp.stack(pieces, axis=1)


def on_device(
    n_dp,
    tokens,
    lengths,
    gene_ids,
    norm1_gain,
    norm1_shift,
    qkv_weight,
    qv_bias,
    out_weight,
    out_bias,
    norm2_gain,
    norm2_shift,
    up_weight,
    up_bias,
    down_weight,
    down_bias,
    cotangent,
):
    features = tokens.shape[1]
    head_cols, units = out_weight.shape[0], down_weight.shape[0]
    plan, small_rows = small_plan(features, head_cols, units, VOCAB // lax.axis_size("tensor"))
    output, input_grad, packed, sums = run_layer(
        n_dp,
        plan,
        small_rows,
        lengths,
        gene_ids[None],
        tokens,
        cotangent,
        norm1_gain[None],
        norm1_shift[None],
        qkv_weight.transpose(1, 0, 2),
        qv_bias,
        out_weight,
        out_bias[None],
        norm2_gain[None],
        norm2_shift[None],
        up_weight,
        up_bias[None],
        down_weight,
        down_bias[None],
    )
    down_grad, up_grad, out_grad, qkv_grad = unpack(packed, features, units, head_cols)

    def take(name):
        at, count, size = plan[name]
        return sums[0, 0, at : at + count].reshape(-1)[:size]

    return (
        output,
        input_grad,
        take("gain1"),
        take("shift1"),
        qkv_grad,
        jnp.stack([take("qbias"), take("vbias")]),
        out_grad,
        take("obias"),
        take("gain2"),
        take("shift2"),
        up_grad,
        take("ubias"),
        down_grad,
        take("dbias"),
        take("genes").astype(jnp.int32),
    )


def solution(mesh):
    return jax.shard_map(
        functools.partial(on_device, mesh.shape["dp"]),
        mesh=mesh,
        in_specs=(
            P("dp", None),
            P("dp", None),
            P("dp"),
            P(),
            P(),
            P(None, None, "tensor"),
            P(None, "tensor"),
            P("tensor", None),
            P(),
            P(),
            P(),
            P(None, "tensor"),
            P("tensor"),
            P("tensor", None),
            P(),
            P("dp", None),
        ),
        out_specs=(
            P("dp", None),
            P("dp", None),
            P(),
            P(),
            P(None, None, "tensor"),
            P(None, "tensor"),
            P("tensor", None),
            P(),
            P(),
            P(),
            P(None, "tensor"),
            P("tensor"),
            P("tensor", None),
            P(),
            P("tensor"),
        ),
        check_vma=False,
    )
```

```python
import functools

import jax
import jax.numpy as jnp
from jax import lax
from jax.experimental import pallas as pl
from jax.experimental.pallas import tpu as pltpu
from jax.sharding import PartitionSpec as P

HEAD = 64
VOCAB = 36000
MESH = pl.DeviceIdType.MESH
F32, BF16 = jnp.float32, jnp.bfloat16
BLK = 256
PARTS = 3
SLOTS = 6
LANES = 128


def mm(left, right):
    return jnp.dot(left, right, preferred_element_type=F32)


def mm_t(left, right):
    return lax.dot_general(left, right, (((1,), (1,)), ((), ())), preferred_element_type=F32)


def bit_of(index, mask):
    return lax.rem(lax.div(index, mask), 2)


def rows_at(index, size):
    return pl.ds(pl.multiple_of(index * size, size), size)


class Exchange:
    def __init__(self, n_dp, chunks, parts, slots, g, r, o, ssem, rsem, osem):
        self.chunks, self.parts, self.slots = chunks, parts, slots
        self.g, self.r, self.o = g, r, o
        self.ssem, self.rsem, self.osem = ssem, rsem, osem
        self.rows = g.shape[2]
        self.bits, self.half, self.stages = stage_counts(n_dp)
        self.dp, self.core = lax.axis_index("dp"), lax.axis_index("tensor")

    def mask(self, c, p, k):
        if k >= 3 or self.bits < 3 or p == 0:
            return 1 << k
        if p == 1:
            return 1 << (1, 0, 2)[k]
        if k == 0:
            return 4
        odd = lax.rem(c, 2)
        return 1 + odd if k == 1 else 2 - odd

    def first(self, c, p, depth):
        at = 0
        for k in range(depth):
            at = at + bit_of(self.dp, self.mask(c, p, k)) * (self.rows >> (k + 1))
        return at

    def slot(self, s):
        if s < self.half:
            return pl.ds(self.rows - (self.rows >> s), self.rows >> (s + 1))
        size = self.rows >> self.half
        return pl.ds(self.rows - size + (s - self.half) * size, size)

    def own(self, c, p, depth):
        return pl.ds(pl.multiple_of(self.first(c, p, depth), 8), self.rows >> depth)

    def copy(self, c, p, s):
        flat_end = self.stages - self.half
        k = s if s < flat_end else self.stages - 1 - s
        mask = self.mask(c, p, k)
        bit = bit_of(self.dp, mask)
        if s < self.half:
            size = self.rows >> (s + 1)
            away = pl.ds(pl.multiple_of(self.first(c, p, s) + (1 - bit) * size, 8), size)
            src = self.g.at[c, p, away]
        elif s < flat_end:
            src = self.g.at[c, p, self.own(c, p, self.half)]
        if s < flat_end:
            dst = self.r.at[lax.rem(c, self.slots), p, self.slot(s)]
        else:
            mine = self.own(c, p, k + 1)
            dst = self.o.at[c, p, mine]
            src = self.g.at[c, p, mine] if s == flat_end else dst
        return pltpu.make_async_remote_copy(
            src,
            dst,
            self.ssem.at[c, p, s],
            self.rsem.at[c, p, s],
            device_id=(self.dp + mask * (1 - 2 * bit), self.core),
            device_id_type=MESH,
        )

    def keep(self, c, p):
        mine = self.own(c, p, self.half)
        return pltpu.make_async_copy(self.g.at[c, p, mine], self.o.at[c, p, mine], self.osem.at[c, p])

    def tick(self, tau):
        flat_end = self.stages - self.half
        for s in range(self.stages + 1):
            c = tau - s

            @pl.when((c >= 0) & (c < self.chunks))
            def _():
                for p in range(self.parts):
                    if s > 0:
                        self.copy(c, p, s - 1).wait()
                    if 0 < s <= flat_end:
                        mine = self.own(c, p, min(s, self.half))
                        got = self.r[lax.rem(c, self.slots), p, self.slot(s - 1)]
                        self.g[c, p, mine] = self.g[c, p, mine] + got
                    if s == flat_end:
                        self.keep(c, p).start()
                    if s == flat_end + 1:
                        self.keep(c, p).wait()
                    if s < self.stages:
                        self.copy(c, p, s).start()


def stage_counts(n_dp):
    bits = n_dp.bit_length() - 1
    half = min(bits, 4)
    return bits, half, bits + half


def slot_rows(n_dp, rows):
    bits, half, _ = stage_counts(n_dp)
    return rows - (rows >> half) + (bits - half) * (rows >> half)


def normalise(x):
    c = x - jnp.mean(x, axis=-1, keepdims=True)
    scale = lax.rsqrt(jnp.mean(c * c, axis=-1, keepdims=True) + 1e-05)
    return c * scale, scale


def norm_back(x_hat, scale, grad):
    middle = jnp.mean(grad, axis=-1, keepdims=True)
    along = jnp.mean(grad * x_hat, axis=-1, keepdims=True)
    return (grad - middle - x_hat * along) * scale


def total(x):
    return jnp.sum(x.astype(F32), axis=0, keepdims=True)


def put_rows(ref, row, vector):
    for i in range(vector.shape[1] // LANES):
        ref[0, 0, row + i : row + i + 1, :] = vector[:, i * LANES : (i + 1) * LANES]


def add_rows(ref, row, vector):
    for i in range(vector.shape[1] // LANES):
        at = slice(row + i, row + i + 1)
        ref[0, 0, at, :] = ref[0, 0, at, :] + vector[:, i * LANES : (i + 1) * LANES]


def small_plan(features, head_cols, units, vocab_local):
    plan, at = {}, 0
    for name, size in (
        ("genes", vocab_local),
        ("gain1", features),
        ("shift1", features),
        ("qbias", head_cols),
        ("vbias", head_cols),
        ("obias", features),
        ("gain2", features),
        ("shift2", features),
        ("ubias", units),
        ("dbias", features),
    ):
        count = -(-size // LANES)
        if name == "genes":
            count = -(-count // 8) * 8
        plan[name] = (at, count, size)
        at += count
    return plan, -(-at // 128) * 128


def leftover(j):
    block = 9 + j // 2
    return 13 + block // 3, block % 3, j % 2


def layer(
    n_dp,
    plan,
    lengths,
    genes,
    tok_h,
    cot_h,
    gain1,
    shift1,
    qkvw_h,
    qvb,
    outw_h,
    obias,
    gain2,
    shift2,
    upw_h,
    ubias,
    dnw_h,
    dbias,
    out_h,
    ing_h,
    o,
    o_small,
    tok,
    cot,
    qkvw,
    outw,
    upw,
    dnw,
    norm,
    norm_t,
    qs,
    ks,
    vs,
    x_t,
    ctx,
    dctx,
    dq_t,
    t1,
    t2,
    t3,
    v,
    g,
    r,
    act,
    act_t,
    gu,
    slope,
    dk_sum,
    dv_sum,
    seg,
    sg,
    sr,
    lsem,
    esend,
    erecv,
    ssem,
    rsem,
    osem,
    sssem,
    srsem,
    sosem,
    vfree,
):
    tokens, features = tok.shape
    head_cols = qs.shape[1]
    units = dnw.shape[0]
    rbs = tokens // BLK
    dp, core = lax.axis_index("dp"), lax.axis_index("tensor")
    other = (dp, 1 - core)

    loads = [
        pltpu.make_async_copy(src, dst, lsem.at[i])
        for i, (src, dst) in enumerate(
            ((tok_h, tok), (qkvw_h, qkvw), (outw_h, outw), (upw_h, upw), (cot_h, cot), (dnw_h, dnw))
        )
    ]
    for load in loads:
        load.start()

    bar = pltpu.get_barrier_semaphore()
    bits = n_dp.bit_length() - 1
    for k in range(bits):
        bit = bit_of(dp, 1 << k)
        to = (dp + (1 << k) * (1 - 2 * bit), core)
        pl.semaphore_signal(bar, inc=1, device_id=to, device_id_type=MESH)
    pl.semaphore_signal(bar, inc=1, device_id=other, device_id_type=MESH)

    big = Exchange(n_dp, g.shape[0], PARTS, SLOTS, g, r, o, ssem, rsem, osem)
    small = Exchange(n_dp, 1, 1, 1, sg, sr, o_small, sssem, srsem, sosem)

    def swap(e, src, rb):
        at = rows_at(rb, BLK)
        return pltpu.make_async_remote_copy(
            src.at[at], v.at[at], esend.at[e, rb], erecv.at[e, rb], device_id=other, device_id_type=MESH
        )

    def freed():
        pl.semaphore_signal(vfree, inc=1, device_id=other, device_id_type=MESH)

    def each(body, count=rbs):
        def step(i, carry):
            body(i)
            return carry

        lax.fori_loop(0, count, step, 0)

    def segment(position):
        ends, seg_now = 0, jnp.zeros(position.shape, jnp.int32)
        for i in range(lengths.shape[1]):
            ends = ends + lengths[0, i]
            seg_now = seg_now + (position >= ends).astype(jnp.int32)
        return seg_now

    seg[...] = segment(lax.broadcasted_iota(jnp.int32, (tokens, LANES), 0))
    sg[...] = jnp.zeros_like(sg)

    loads[0].wait()

    def first_norm(rb):
        at = rows_at(rb, BLK)
        x_hat, _ = normalise(tok[at, :].astype(F32))
        norm[at, :] = (x_hat * gain1[...][None, :] + shift1[...][None, :]).astype(BF16)

    each(first_norm)
    loads[1].wait()

    def project(rb):
        at = rows_at(rb, BLK)
        x = norm[at, :]
        qs[at, :] = (mm(x, qkvw[0]) + qvb[0:1, :]).astype(BF16) * BF16(HEAD**-0.5)
        ks[at, :] = mm(x, qkvw[1]).astype(BF16)
        vs[at, :] = (mm(x, qkvw[2]) + qvb[1:2, :]).astype(BF16)

    each(project)
    loads[2].wait()
    pl.semaphore_wait(bar, bits + 1)

    def attend(rb):
        at = rows_at(rb, BLK)
        seg_row = segment(lax.broadcasted_iota(jnp.int32, (1, tokens), 1))
        same = jnp.concatenate([seg[at, :]] * (tokens // LANES), axis=1) == seg_row
        for pair in range(head_cols // LANES):
            sides = []
            for side in range(2):
                cols = slice(pair * LANES + side * HEAD, pair * LANES + (side + 1) * HEAD)
                scores = jnp.where(same, mm_t(qs[at, cols], ks[:, cols]), -1000000000.0)
                e = jnp.exp(scores - jnp.max(scores, axis=-1, keepdims=True))
                inverse = 1.0 / jnp.sum(e, axis=-1, keepdims=True)
                sides.append(mm((e * inverse).astype(BF16), vs[:, cols]))
            ctx[at, pair * LANES : (pair + 1) * LANES] = jnp.concatenate(sides, axis=1).astype(BF16)
        t1[at, :] = mm(ctx[at, :], outw[...])
        swap(0, t1, rb).start()

    each(attend)
    loads[3].wait()
    loads[4].wait()
    loads[5].wait()

    def second_norm(rb):
        at = rows_at(rb, BLK)
        swap(0, t1, rb).wait()
        hidden = tok[at, :].astype(F32) + (t1[at, :] + v[at, :]) + obias[...][None, :]
        t1[at, :] = hidden
        x_hat, _ = normalise(hidden)
        norm[at, :] = (x_hat * gain2[...][None, :] + shift2[...][None, :]).astype(BF16)
        t2[at, :] = jnp.zeros((BLK, features), F32)
        t3[at, :] = jnp.zeros((BLK, features), F32)

    each(second_norm)
    freed()

    def feed_forward(u):
        ucols = rows_at(u, BLK)

        def upper(rb):
            at = rows_at(rb, BLK)
            up = mm(norm[at, :], upw[:, ucols]) + ubias[ucols][None, :]
            cdf = 0.5 * (1.0 + lax.erf(up * 0.7071067811865476))
            act[at, :] = (up * cdf).astype(BF16)
            slope[at, :] = cdf + up * (jnp.exp(-0.5 * up * up) * 0.3989422804014327)

        each(upper)
        act_t[...] = act[...].T
        for p in range(PARTS):
            g[2 * u, p] = mm(act_t[...], cot[:, p * BLK : (p + 1) * BLK])
        big.tick(u + jnp.minimum(u, 1))

        @pl.when(u == 0)
        def _():
            norm_t[...] = norm[...].T

        def lower(rb, sums):
            at = rows_at(rb, BLK)
            down_rows = dnw[ucols, :]
            grad = (mm_t(cot[at, :], down_rows) * slope[at, :]).astype(BF16)
            gu[at, :] = grad
            t2[at, :] = t2[at, :] + mm(act[at, :], down_rows)
            t3[at, :] = t3[at, :] + mm_t(grad, upw[:, ucols])
            return sums + total(grad)

        sums = lax.fori_loop(0, rbs, lower, jnp.zeros((1, BLK), F32))
        row = plan["ubias"][0] + u * (BLK // LANES)
        for i in range(BLK // LANES):
            sg[0, 0, pl.ds(row + i, 1), :] = sums[:, i * LANES : (i + 1) * LANES]
        for p in range(PARTS):
            g[2 * u + 1, p] = mm(norm_t[p * BLK : (p + 1) * BLK, :], gu[...])

        @pl.when(u == 0)
        def _():
            big.tick(1)

    each(feed_forward, units // BLK)
    tau = units // BLK + 1

    pl.semaphore_wait(vfree, 1)
    each(lambda rb: swap(1, t3, rb).start())
    big.tick(tau)
    tau += 1

    def second_norm_back(rb):
        at = rows_at(rb, BLK)
        swap(1, t3, rb).wait()
        grad = t3[at, :] + v[at, :]
        x_hat, scale = normalise(t1[at, :])
        add_rows(sg, plan["gain2"][0], total(grad * x_hat))
        add_rows(sg, plan["shift2"][0], total(grad))
        given = cot[at, :].astype(F32)
        add_rows(sg, plan["dbias"][0], total(given))
        grad = given + norm_back(x_hat, scale, grad * gain2[...][None, :])
        t3[at, :] = grad
        norm[at, :] = grad.astype(BF16)
        add_rows(sg, plan["obias"][0], total(norm[at, :]))
        dctx[at, :] = mm_t(norm[at, :], outw[...]).astype(BF16)

    each(second_norm_back)
    freed()
    pl.semaphore_wait(vfree, 1)
    each(lambda rb: swap(2, t2, rb).start())

    x_t[...] = ctx[...].T
    for p in range(PARTS):
        branch = norm[:, p * BLK : (p + 1) * BLK]
        g[12, p] = mm(x_t[:BLK, :], branch)
        rest = mm(x_t[BLK:, :], branch)
        if p < 2:
            g[17, 1, p * LANES : (p + 1) * LANES] = rest
        else:
            g[17, 2, :LANES] = rest
    big.tick(tau)
    tau += 1

    def result(rb):
        at = rows_at(rb, BLK)
        swap(2, t2, rb).wait()
        norm[at, :] = (t1[at, :] + (t2[at, :] + v[at, :]) + dbias[...][None, :]).astype(BF16)

    each(result)
    freed()
    to_out = pltpu.make_async_copy(norm, out_h, lsem.at[0])
    to_out.start()

    x_t[...] = ks[...].T

    def attend_back(step):
        pair, qb = lax.div(step, rbs), lax.rem(step, rbs)
        at = rows_at(qb, BLK)
        cols = rows_at(pair, LANES)
        position = lax.broadcasted_iota(jnp.int32, (1, BLK), 1) + qb * BLK
        seg_row = segment(position)
        same = jnp.concatenate([seg[...]] * (BLK // LANES), axis=1) == seg_row
        dks, dvs = [], []
        for side in range(2):
            lanes = slice(side * HEAD, (side + 1) * HEAD)
            q_now, d_now = qs[at, cols][:, lanes], dctx[at, cols][:, lanes]
            scores = jnp.where(same, mm_t(ks[:, cols][:, lanes], q_now), -1000000000.0)
            e = jnp.exp(scores - jnp.max(scores, axis=0, keepdims=True))
            probs = e * (1.0 / jnp.sum(e, axis=0, keepdims=True))
            grad = mm_t(vs[:, cols][:, lanes], d_now)
            inner = jnp.sum(probs * grad, axis=0, keepdims=True)
            grad = (probs * (grad - inner)).astype(BF16)
            dvs.append(mm(probs.astype(BF16), d_now))
            dks.append(mm(grad, q_now))
            hrows = pl.ds(pl.multiple_of(pair * LANES + side * HEAD, HEAD), HEAD)
            dq_t[hrows, at] = (mm(x_t[hrows, :], grad) * HEAD**-0.5).astype(BF16)
        dk_now, dv_now = jnp.concatenate(dks, axis=1), jnp.concatenate(dvs, axis=1)

        @pl.when(qb == 0)
        def _():
            dk_sum[...] = dk_now
            dv_sum[...] = dv_now

        @pl.when(qb > 0)
        def _():
            dk_sum[...] = dk_sum[...] + dk_now
            dv_sum[...] = dv_sum[...] + dv_now

        @pl.when(qb == rbs - 1)
        def _():
            ks[:, cols] = dk_sum[...].astype(BF16)
            vs[:, cols] = dv_sum[...].astype(BF16)

        @pl.when(lax.rem(step, 3) == 1)
        def _():
            big.tick(tau + lax.div(step, 3))

    steps = rbs * (head_cols // LANES)
    each(attend_back, steps)
    tau += steps // 3

    qs[...] = dq_t[...].T
    put_rows(sg, plan["qbias"][0], total(qs[...]))
    put_rows(sg, plan["vbias"][0], total(vs[...]))
    to_out.wait()
    each(first_norm)
    norm_t[...] = norm[...].T
    for i, grads in enumerate((qs, ks, vs)):
        for j in range(PARTS):
            made = mm(norm_t[j * BLK : (j + 1) * BLK, :], grads[...])
            g[13 + i, j] = made[:, :BLK]
            if i * 3 + j < 8:
                c, p, side = leftover(i * 3 + j)
                g[c, p, :, side * LANES : (side + 1) * LANES] = made[:, BLK:]
            else:
                g[17, 2, LANES:, :LANES] = made[:LANES, BLK:]
                g[17, 2, LANES:, LANES:] = made[LANES:, BLK:]
    big.tick(tau)
    tau += 1

    pl.semaphore_wait(vfree, 1)

    def to_norm(rb):
        at = rows_at(rb, BLK)
        t2[at, :] = mm_t(qs[at, :], qkvw[0]) + mm_t(ks[at, :], qkvw[1]) + mm_t(vs[at, :], qkvw[2])
        swap(3, t2, rb).start()

    each(to_norm)

    def first_norm_back(rb):
        at = rows_at(rb, BLK)
        swap(3, t2, rb).wait()
        grad = t2[at, :] + v[at, :]
        x_hat, scale = normalise(tok[at, :].astype(F32))
        add_rows(sg, plan["gain1"][0], total(grad * x_hat))
        add_rows(sg, plan["shift1"][0], total(grad))
        norm[at, :] = (t3[at, :] + norm_back(x_hat, scale, grad * gain1[...][None, :])).astype(BF16)

    each(first_norm_back)
    to_ing = pltpu.make_async_copy(norm, ing_h, lsem.at[1])
    to_ing.start()

    rows = plan["genes"][1]
    local = genes[...][None, :] - core * plan["genes"][2]
    high = lax.shift_right_arithmetic(local, 7)
    low = local - high * LANES
    high = (lax.broadcasted_iota(jnp.int32, (rows, tokens), 0) == high).astype(F32).astype(BF16)
    low = (lax.broadcasted_iota(jnp.int32, (LANES, tokens), 0) == low).astype(F32).astype(BF16)
    sg[0, 0, :rows, :] = mm_t(high, low)

    def finish(i, carry):
        big.tick(tau + i)
        small.tick(i)
        return carry

    left = g.shape[0] + big.stages - tau
    lax.fori_loop(0, max(left, small.stages + 1), finish, 0)
    to_ing.wait()


def run_layer(n_dp, plan, small_rows, *args):
    (lengths, genes, tok, cot, gain1, shift1, qkvw, qvb, outw, obias, gain2, shift2, upw, ubias, dnw, dbias) = args
    tokens, features = tok.shape
    units, head_cols = dnw.shape[0], outw.shape[0]
    chunks = (features * (2 * units + 4 * head_cols)) // (PARTS * BLK * BLK)
    _, _, stages = stage_counts(n_dp)
    vmem = pl.BlockSpec(memory_space=pltpu.VMEM)
    smem = pl.BlockSpec(memory_space=pltpu.SMEM)
    hbm = pl.BlockSpec(memory_space=pl.ANY)
    dma = pltpu.SemaphoreType.DMA
    wide = (tokens, features)
    return pl.pallas_call(
        functools.partial(layer, n_dp, plan),
        out_shape=(
            jax.ShapeDtypeStruct(wide, BF16),
            jax.ShapeDtypeStruct(wide, BF16),
            jax.ShapeDtypeStruct((chunks, PARTS, BLK, BLK), F32),
            jax.ShapeDtypeStruct((1, 1, small_rows, LANES), F32),
        ),
        in_specs=[smem, vmem, hbm, hbm, vmem, vmem, hbm, vmem, hbm, vmem, vmem, vmem, hbm, vmem, hbm, vmem],
        out_specs=(hbm, hbm, hbm, hbm),
        scratch_shapes=[
            pltpu.VMEM(wide, BF16),
            pltpu.VMEM(wide, BF16),
            pltpu.VMEM(qkvw.shape, BF16),
            pltpu.VMEM(outw.shape, BF16),
            pltpu.VMEM(upw.shape, BF16),
            pltpu.VMEM(dnw.shape, BF16),
            pltpu.VMEM(wide, BF16),
            pltpu.VMEM((features, tokens), BF16),
            pltpu.VMEM((tokens, head_cols), BF16),
            pltpu.VMEM((tokens, head_cols), BF16),
            pltpu.VMEM((tokens, head_cols), BF16),
            pltpu.VMEM((head_cols, tokens), BF16),
            pltpu.VMEM((tokens, head_cols), BF16),
            pltpu.VMEM((tokens, head_cols), BF16),
            pltpu.VMEM((head_cols, tokens), BF16),
            pltpu.VMEM(wide, F32),
            pltpu.VMEM(wide, F32),
            pltpu.VMEM(wide, F32),
            pltpu.VMEM(wide, F32),
            pltpu.VMEM((chunks, PARTS, BLK, BLK), F32),
            pltpu.VMEM((SLOTS, PARTS, slot_rows(n_dp, BLK), BLK), F32),
            pltpu.VMEM((tokens, BLK), BF16),
            pltpu.VMEM((BLK, tokens), BF16),
            pltpu.VMEM((tokens, BLK), BF16),
            pltpu.VMEM((tokens, BLK), F32),
            pltpu.VMEM((tokens, LANES), F32),
            pltpu.VMEM((tokens, LANES), F32),
            pltpu.VMEM((tokens, LANES), jnp.int32),
            pltpu.VMEM((1, 1, small_rows, LANES), F32),
            pltpu.VMEM((1, 1, slot_rows(n_dp, small_rows), LANES), F32),
            dma((6,)),
            dma((4, tokens // BLK)),
            dma((4, tokens // BLK)),
            dma((chunks, PARTS, stages)),
            dma((chunks, PARTS, stages)),
            dma((chunks, PARTS)),
            dma((1, 1, stages)),
            dma((1, 1, stages)),
            dma((1, 1)),
            pltpu.SemaphoreType.REGULAR,
        ],
        compiler_params=pltpu.CompilerParams(
            collective_id=0, has_side_effects=True, vmem_limit_bytes=63 << 20
        ),
    )(*args)


def hand_out(plan, packed_h, sums, out_h, ing_h, *refs):
    (output, input_grad, gain1, shift1, qkv, qv, out, obias, gain2, shift2, up, ubias, down, dbias, genes) = refs[:15]
    packed, wide, loaded, sem = refs[15:]
    chunks = packed.shape[0]
    loads = [pltpu.make_async_copy(packed_h.at[c], packed.at[c], loaded.at[c]) for c in range(chunks)]
    loads.append(pltpu.make_async_copy(out_h, wide.at[0], loaded.at[chunks]))
    loads.append(pltpu.make_async_copy(ing_h, wide.at[1], loaded.at[chunks + 1]))
    for load in loads:
        load.start()
    moves = [[] for load in loads]
    moves[chunks].append((wide.at[0], output))
    moves[chunks + 1].append((wide.at[1], input_grad))
    for u in range(down.shape[0] // BLK):
        for p in range(PARTS):
            units, cols = pl.ds(u * BLK, BLK), pl.ds(p * BLK, BLK)
            moves[2 * u].append((packed.at[2 * u, p], down.at[units, cols]))
            moves[2 * u + 1].append((packed.at[2 * u + 1, p], up.at[cols, units]))
    half = pl.ds(0, LANES), pl.ds(LANES, LANES)
    for p in range(PARTS):
        cols = pl.ds(p * BLK, BLK)
        moves[12].append((packed.at[12, p], out.at[pl.ds(0, BLK), cols]))
        rest = packed.at[17, 1 + p // 2, half[p % 2]]
        moves[17].append((rest, out.at[pl.ds(BLK, LANES), cols]))
    for i in range(3):
        for j in range(PARTS):
            rows, tail = pl.ds(j * BLK, BLK), pl.ds(BLK, LANES)
            moves[13 + i].append((packed.at[13 + i, j], qkv.at[i, rows, pl.ds(0, BLK)]))
            if i * 3 + j < 8:
                c, p, side = leftover(i * 3 + j)
                moves[c].append((packed.at[c, p, pl.ds(0, BLK), half[side]], qkv.at[i, rows, tail]))
            else:
                for side in range(2):
                    rows = pl.ds(j * BLK + side * LANES, LANES)
                    moves[17].append((packed.at[17, 2, half[1], half[side]], qkv.at[i, rows, tail]))
    copies = []
    for load, group in zip(loads, moves):
        load.wait()
        for src, dst in group:
            copy = pltpu.make_async_copy(src, dst, sem.at[len(copies)])
            copy.start()
            copies.append(copy)

    def vector(name, ref, *index):
        at, count, _ = plan[name]
        for i in range(count):
            ref[(*index, pl.ds(i * LANES, LANES))] = sums[0, 0, at + i]

    for name, ref in (
        ("gain1", gain1),
        ("shift1", shift1),
        ("obias", obias),
        ("gain2", gain2),
        ("shift2", shift2),
        ("ubias", ubias),
        ("dbias", dbias),
    ):
        vector(name, ref)
    vector("qbias", qv, 0)
    vector("vbias", qv, 1)
    size = plan["genes"][2]
    for i in range(-(-size // LANES)):
        part = min(LANES, size - i * LANES)
        genes[pl.ds(i * LANES, part)] = sums[0, 0, i, :part].astype(jnp.int32)
    for copy in copies:
        copy.wait()


def results(plan, features, head_cols, units, packed, sums, output, input_grad):
    vmem = pl.BlockSpec(memory_space=pltpu.VMEM)
    hbm = pl.BlockSpec(memory_space=pl.ANY)
    size = lambda name: (plan[name][2],)
    shapes = (
        output.shape,
        input_grad.shape,
        size("gain1"),
        size("shift1"),
        (3, features, head_cols),
        (2, head_cols),
        (head_cols, features),
        size("obias"),
        size("gain2"),
        size("shift2"),
        (features, units),
        size("ubias"),
        (units, features),
        size("dbias"),
        size("genes"),
    )
    types = [BF16, BF16] + [F32] * 12 + [jnp.int32]
    large = (0, 1, 4, 6, 10, 12)
    return pl.pallas_call(
        functools.partial(hand_out, plan),
        out_shape=tuple(jax.ShapeDtypeStruct(shape, kind) for shape, kind in zip(shapes, types)),
        in_specs=[hbm, vmem, hbm, hbm],
        out_specs=tuple(hbm if i in large else vmem for i in range(15)),
        scratch_shapes=[
            pltpu.VMEM(packed.shape, F32),
            pltpu.VMEM((2, *output.shape), BF16),
            pltpu.SemaphoreType.DMA((packed.shape[0] + 2,)),
            pltpu.SemaphoreType.DMA((80,)),
        ],
        compiler_params=pltpu.CompilerParams(vmem_limit_bytes=60 << 20),
    )(packed, sums, output, input_grad)


def on_device(
    n_dp,
    tokens,
    lengths,
    gene_ids,
    norm1_gain,
    norm1_shift,
    qkv_weight,
    qv_bias,
    out_weight,
    out_bias,
    norm2_gain,
    norm2_shift,
    up_weight,
    up_bias,
    down_weight,
    down_bias,
    cotangent,
):
    features = tokens.shape[1]
    head_cols, units = out_weight.shape[0], down_weight.shape[0]
    plan, small_rows = small_plan(features, head_cols, units, VOCAB // lax.axis_size("tensor"))
    output, input_grad, packed, sums = run_layer(
        n_dp,
        plan,
        small_rows,
        lengths,
        gene_ids,
        tokens,
        cotangent,
        norm1_gain,
        norm1_shift,
        qkv_weight.transpose(1, 0, 2),
        qv_bias,
        out_weight,
        out_bias,
        norm2_gain,
        norm2_shift,
        up_weight,
        up_bias,
        down_weight,
        down_bias,
    )
    made = list(results(plan, features, head_cols, units, packed, sums, output, input_grad))
    made[4] = made[4].transpose(1, 0, 2)
    return tuple(made)


def solution(mesh):
    return jax.shard_map(
        functools.partial(on_device, mesh.shape["dp"]),
        mesh=mesh,
        in_specs=(
            P("dp", None),
            P("dp", None),
            P("dp"),
            P(),
            P(),
            P(None, None, "tensor"),
            P(None, "tensor"),
            P("tensor", None),
            P(),
            P(),
            P(),
            P(None, "tensor"),
            P("tensor"),
            P("tensor", None),
            P(),
            P("dp", None),
        ),
        out_specs=(
            P("dp", None),
            P("dp", None),
            P(),
            P(),
            P(None, None, "tensor"),
            P(None, "tensor"),
            P("tensor", None),
            P(),
            P(),
            P(),
            P(None, "tensor"),
            P("tensor"),
            P("tensor", None),
            P(),
            P("tensor"),
        ),
        check_vma=False,
    )
```

```python
import functools

import jax
import jax.numpy as jnp
from jax import lax
from jax.experimental import pallas as pl
from jax.experimental.pallas import tpu as pltpu
from jax.sharding import PartitionSpec as P

HEAD = 64
VOCAB = 36000
MESH = pl.DeviceIdType.MESH
F32, BF16 = jnp.float32, jnp.bfloat16
BLK = 256
PARTS = 3
SLOTS = 4
HELD = 14
LANES = 128


def mm(left, right):
    return jnp.dot(left, right, preferred_element_type=F32)


def mm_t(left, right):
    return lax.dot_general(left, right, (((1,), (1,)), ((), ())), preferred_element_type=F32)


def bit_of(index, mask):
    return lax.rem(lax.div(index, mask), 2)


def rows_at(index, size):
    return pl.ds(pl.multiple_of(index * size, size), size)


class Exchange:
    def __init__(self, n_dp, chunks, parts, slots, g, r, o, ssem, rsem, osem):
        self.chunks, self.parts, self.slots = chunks, parts, slots
        self.g, self.r, self.o = g, r, o
        self.ssem, self.rsem, self.osem = ssem, rsem, osem
        self.rows = g.shape[2]
        self.bits, self.half, self.stages = stage_counts(n_dp)
        self.dp, self.core = lax.axis_index("dp"), lax.axis_index("tensor")

    def mask(self, c, p, k):
        if k >= 3 or self.bits < 3 or p == 0:
            return 1 << k
        if p == 1:
            return 1 << (1, 0, 2)[k]
        if k == 0:
            return 4
        odd = lax.rem(c, 2)
        return 1 + odd if k == 1 else 2 - odd

    def first(self, c, p, depth):
        at = 0
        for k in range(depth):
            at = at + bit_of(self.dp, self.mask(c, p, k)) * (self.rows >> (k + 1))
        return at

    def held(self, c):
        return lax.rem(c, self.g.shape[0])

    def slot(self, s):
        if s < self.half:
            return pl.ds(self.rows - (self.rows >> s), self.rows >> (s + 1))
        size = self.rows >> self.half
        return pl.ds(self.rows - size + (s - self.half) * size, size)

    def own(self, c, p, depth):
        return pl.ds(pl.multiple_of(self.first(c, p, depth), 8), self.rows >> depth)

    def copy(self, c, p, s):
        flat_end = self.stages - self.half
        k = s if s < flat_end else self.stages - 1 - s
        mask = self.mask(c, p, k)
        bit = bit_of(self.dp, mask)
        if s < self.half:
            size = self.rows >> (s + 1)
            away = pl.ds(pl.multiple_of(self.first(c, p, s) + (1 - bit) * size, 8), size)
            src = self.g.at[self.held(c), p, away]
        elif s < flat_end:
            src = self.g.at[self.held(c), p, self.own(c, p, self.half)]
        if s < flat_end:
            dst = self.r.at[lax.rem(c, self.slots), p, self.slot(s)]
        else:
            mine = self.own(c, p, k + 1)
            dst = self.o.at[c, p, mine]
            src = self.g.at[self.held(c), p, mine] if s == flat_end else dst
        return pltpu.make_async_remote_copy(
            src,
            dst,
            self.ssem.at[c, p, s],
            self.rsem.at[c, p, s],
            device_id=(self.dp + mask * (1 - 2 * bit), self.core),
            device_id_type=MESH,
        )

    def keep(self, c, p):
        mine = self.own(c, p, self.half)
        return pltpu.make_async_copy(self.g.at[self.held(c), p, mine], self.o.at[c, p, mine], self.osem.at[c, p])

    def tick(self, tau):
        flat_end = self.stages - self.half
        for s in range(self.stages + 1):
            c = tau - s

            @pl.when((c >= 0) & (c < self.chunks))
            def _():
                for p in range(self.parts):
                    if s > 0:
                        self.copy(c, p, s - 1).wait()
                    if 0 < s <= flat_end:
                        mine = self.own(c, p, min(s, self.half))
                        got = self.r[lax.rem(c, self.slots), p, self.slot(s - 1)]
                        at = self.held(c)
                        self.g[at, p, mine] = self.g[at, p, mine] + got
                    if s == flat_end:
                        self.keep(c, p).start()
                    if s == flat_end + 1:
                        self.keep(c, p).wait()
                    if s < self.stages:
                        self.copy(c, p, s).start()


def stage_counts(n_dp):
    bits = n_dp.bit_length() - 1
    half = min(bits, 4)
    return bits, half, bits + half


def slot_rows(n_dp, rows):
    bits, half, _ = stage_counts(n_dp)
    return rows - (rows >> half) + (bits - half) * (rows >> half)


def normalise(x):
    c = x - jnp.mean(x, axis=-1, keepdims=True)
    scale = lax.rsqrt(jnp.mean(c * c, axis=-1, keepdims=True) + 1e-05)
    return c * scale, scale


def norm_back(x_hat, scale, grad):
    middle = jnp.mean(grad, axis=-1, keepdims=True)
    along = jnp.mean(grad * x_hat, axis=-1, keepdims=True)
    return (grad - middle - x_hat * along) * scale


def total(x):
    return jnp.sum(x.astype(F32), axis=0, keepdims=True)


def put_rows(ref, row, vector):
    for i in range(vector.shape[1] // LANES):
        ref[0, 0, row + i : row + i + 1, :] = vector[:, i * LANES : (i + 1) * LANES]


def add_rows(ref, row, vector):
    for i in range(vector.shape[1] // LANES):
        at = slice(row + i, row + i + 1)
        ref[0, 0, at, :] = ref[0, 0, at, :] + vector[:, i * LANES : (i + 1) * LANES]


def small_plan(features, head_cols, units, vocab_local):
    plan, at = {}, 0
    for name, size in (
        ("genes", vocab_local),
        ("gain1", features),
        ("shift1", features),
        ("qbias", head_cols),
        ("vbias", head_cols),
        ("obias", features),
        ("gain2", features),
        ("shift2", features),
        ("ubias", units),
        ("dbias", features),
    ):
        count = -(-size // LANES)
        if name == "genes":
            count = -(-count // 8) * 8
        plan[name] = (at, count, size)
        at += count
    return plan, -(-at // 128) * 128


def leftover(j):
    block = 9 + j // 2
    return (17, 13)[block // 3 - 3], block % 3, j % 2


def layer(
    n_dp,
    plan,
    lengths,
    genes,
    tok_h,
    cot_h,
    gain1,
    shift1,
    qkvw_h,
    qvb,
    outw_h,
    obias,
    gain2,
    shift2,
    upw_h,
    ubias,
    dnw_h,
    dbias,
    out_ref,
    ing_ref,
    o,
    o_small,
    tok,
    cot,
    qkvw,
    outw,
    upw,
    dnw,
    norm_t,
    qs,
    ks,
    vs,
    ctx,
    t1,
    t2,
    t3,
    v,
    g,
    r,
    act,
    act_t,
    gu,
    slope,
    seg,
    sg,
    sr,
    lsem,
    esend,
    erecv,
    ssem,
    rsem,
    osem,
    sssem,
    srsem,
    sosem,
    vfree,
):
    tokens, features = tok.shape
    head_cols = qs.shape[1]
    units = dnw.shape[0]
    rbs = tokens // BLK
    dq_t, x_t = norm_t.at[:head_cols], norm_t.at[head_cols : 2 * head_cols]
    dctx, norm = ctx, ing_ref
    dk_sum, dv_sum = slope.at[:, :LANES], slope.at[:, LANES:]
    dp, core = lax.axis_index("dp"), lax.axis_index("tensor")
    other = (dp, 1 - core)

    loads = [
        pltpu.make_async_copy(src, dst, lsem.at[i])
        for i, (src, dst) in enumerate(
            ((tok_h, tok), (qkvw_h, qkvw), (outw_h, outw), (upw_h, upw), (cot_h, cot), (dnw_h, dnw))
        )
    ]
    for load in loads:
        load.start()

    bar = pltpu.get_barrier_semaphore()
    bits = n_dp.bit_length() - 1
    for k in range(bits):
        bit = bit_of(dp, 1 << k)
        to = (dp + (1 << k) * (1 - 2 * bit), core)
        pl.semaphore_signal(bar, inc=1, device_id=to, device_id_type=MESH)
    pl.semaphore_signal(bar, inc=1, device_id=other, device_id_type=MESH)

    big = Exchange(n_dp, o.shape[0], PARTS, SLOTS, g, r, o, ssem, rsem, osem)
    small = Exchange(n_dp, 1, 1, 1, sg, sr, o_small, sssem, srsem, sosem)

    def swap(e, src, rb):
        at = rows_at(rb, BLK)
        return pltpu.make_async_remote_copy(
            src.at[at], v.at[at], esend.at[e, rb], erecv.at[e, rb], device_id=other, device_id_type=MESH
        )

    def freed():
        pl.semaphore_signal(vfree, inc=1, device_id=other, device_id_type=MESH)

    def each(body, count=rbs):
        def step(i, carry):
            body(i)
            return carry

        lax.fori_loop(0, count, step, 0)

    def segment(position):
        ends, seg_now = 0, jnp.zeros(position.shape, jnp.int32)
        for i in range(lengths.shape[1]):
            ends = ends + lengths[0, i]
            seg_now = seg_now + (position >= ends).astype(jnp.int32)
        return seg_now

    seg[...] = segment(lax.broadcasted_iota(jnp.int32, (tokens, LANES), 0))
    sg[...] = jnp.zeros_like(sg)

    loads[0].wait()

    def first_norm(rb):
        at = rows_at(rb, BLK)
        x_hat, _ = normalise(tok[at, :].astype(F32))
        norm[at, :] = (x_hat * gain1[...][None, :] + shift1[...][None, :]).astype(BF16)

    each(first_norm)
    loads[1].wait()

    def project(rb):
        at = rows_at(rb, BLK)
        x = norm[at, :]
        qs[at, :] = (mm(x, qkvw[0]) + qvb[0:1, :]).astype(BF16) * BF16(HEAD**-0.5)
        ks[at, :] = mm(x, qkvw[1]).astype(BF16)
        vs[at, :] = (mm(x, qkvw[2]) + qvb[1:2, :]).astype(BF16)

    each(project)
    loads[2].wait()
    pl.semaphore_wait(bar, bits + 1)

    def attend(rb):
        at = rows_at(rb, BLK)
        seg_row = segment(lax.broadcasted_iota(jnp.int32, (1, tokens), 1))
        same = jnp.concatenate([seg[at, :]] * (tokens // LANES), axis=1) == seg_row
        for pair in range(head_cols // LANES):
            sides = []
            for side in range(2):
                cols = slice(pair * LANES + side * HEAD, pair * LANES + (side + 1) * HEAD)
                scores = jnp.where(same, mm_t(qs[at, cols], ks[:, cols]), -1000000000.0)
                e = jnp.exp(scores - jnp.max(scores, axis=-1, keepdims=True))
                inverse = 1.0 / jnp.sum(e, axis=-1, keepdims=True)
                sides.append(mm((e * inverse).astype(BF16), vs[:, cols]))
            ctx[at, pair * LANES : (pair + 1) * LANES] = jnp.concatenate(sides, axis=1).astype(BF16)
        t1[at, :] = mm(ctx[at, :], outw[...])
        swap(0, t1, rb).start()

    each(attend)
    loads[3].wait()
    loads[4].wait()
    loads[5].wait()

    def second_norm(rb):
        at = rows_at(rb, BLK)
        swap(0, t1, rb).wait()
        hidden = tok[at, :].astype(F32) + (t1[at, :] + v[at, :]) + obias[...][None, :]
        t1[at, :] = hidden
        x_hat, _ = normalise(hidden)
        norm[at, :] = (x_hat * gain2[...][None, :] + shift2[...][None, :]).astype(BF16)
        t2[at, :] = jnp.zeros((BLK, features), F32)
        t3[at, :] = jnp.zeros((BLK, features), F32)

    each(second_norm)
    freed()

    def feed_forward(u):
        ucols = rows_at(u, BLK)

        def upper(rb):
            at = rows_at(rb, BLK)
            up = mm(norm[at, :], upw[:, ucols]) + ubias[ucols][None, :]
            cdf = 0.5 * (1.0 + lax.erf(up * 0.7071067811865476))
            act[at, :] = (up * cdf).astype(BF16)
            slope[at, :] = cdf + up * (jnp.exp(-0.5 * up * up) * 0.3989422804014327)

        each(upper)
        act_t[...] = act[...].T
        for p in range(PARTS):
            g[2 * u, p] = mm(act_t[...], cot[:, p * BLK : (p + 1) * BLK])
        big.tick(u + jnp.minimum(u, 1))

        @pl.when(u == 0)
        def _():
            norm_t[...] = norm[...].T

        def lower(rb, sums):
            at = rows_at(rb, BLK)
            down_rows = dnw[ucols, :]
            grad = (mm_t(cot[at, :], down_rows) * slope[at, :]).astype(BF16)
            gu[at, :] = grad
            t2[at, :] = t2[at, :] + mm(act[at, :], down_rows)
            t3[at, :] = t3[at, :] + mm_t(grad, upw[:, ucols])
            return sums + total(grad)

        sums = lax.fori_loop(0, rbs, lower, jnp.zeros((1, BLK), F32))
        row = plan["ubias"][0] + u * (BLK // LANES)
        for i in range(BLK // LANES):
            sg[0, 0, pl.ds(row + i, 1), :] = sums[:, i * LANES : (i + 1) * LANES]
        for p in range(PARTS):
            g[2 * u + 1, p] = mm(norm_t[p * BLK : (p + 1) * BLK, :], gu[...])

        @pl.when(u == 0)
        def _():
            big.tick(1)

    each(feed_forward, units // BLK)
    tau = units // BLK + 1

    pl.semaphore_wait(vfree, 1)
    each(lambda rb: swap(1, t3, rb).start())
    big.tick(tau)
    tau += 1

    x_t[...] = ctx[...].T

    def second_norm_back(rb):
        at = rows_at(rb, BLK)
        swap(1, t3, rb).wait()
        grad = t3[at, :] + v[at, :]
        x_hat, scale = normalise(t1[at, :])
        add_rows(sg, plan["gain2"][0], total(grad * x_hat))
        add_rows(sg, plan["shift2"][0], total(grad))
        given = cot[at, :].astype(F32)
        add_rows(sg, plan["dbias"][0], total(given))
        grad = given + norm_back(x_hat, scale, grad * gain2[...][None, :])
        t3[at, :] = grad
        norm[at, :] = grad.astype(BF16)
        add_rows(sg, plan["obias"][0], total(norm[at, :]))
        dctx[at, :] = mm_t(norm[at, :], outw[...]).astype(BF16)

    each(second_norm_back)
    freed()
    pl.semaphore_wait(vfree, 1)
    each(lambda rb: swap(2, t2, rb).start())

    for p in range(PARTS):
        branch = norm[:, p * BLK : (p + 1) * BLK]
        g[12, p] = mm(x_t[:BLK, :], branch)
        rest = mm(x_t[BLK:, :], branch)
        if p < 2:
            g[13, 1, p * LANES : (p + 1) * LANES] = rest
        else:
            g[13, 2, :LANES] = rest
    big.tick(tau)
    tau += 1

    def result(rb):
        at = rows_at(rb, BLK)
        swap(2, t2, rb).wait()
        out_ref[at, :] = (t1[at, :] + (t2[at, :] + v[at, :]) + dbias[...][None, :]).astype(BF16)

    each(result)
    freed()

    x_t[...] = ks[...].T

    def attend_back(step):
        pair, qb = lax.div(step, rbs), lax.rem(step, rbs)
        at = rows_at(qb, BLK)
        cols = rows_at(pair, LANES)
        position = lax.broadcasted_iota(jnp.int32, (1, BLK), 1) + qb * BLK
        seg_row = segment(position)
        same = jnp.concatenate([seg[...]] * (BLK // LANES), axis=1) == seg_row
        dks, dvs = [], []
        for side in range(2):
            lanes = slice(side * HEAD, (side + 1) * HEAD)
            q_now, d_now = qs[at, cols][:, lanes], dctx[at, cols][:, lanes]
            scores = jnp.where(same, mm_t(ks[:, cols][:, lanes], q_now), -1000000000.0)
            e = jnp.exp(scores - jnp.max(scores, axis=0, keepdims=True))
            probs = e * (1.0 / jnp.sum(e, axis=0, keepdims=True))
            grad = mm_t(vs[:, cols][:, lanes], d_now)
            inner = jnp.sum(probs * grad, axis=0, keepdims=True)
            grad = (probs * (grad - inner)).astype(BF16)
            dvs.append(mm(probs.astype(BF16), d_now))
            dks.append(mm(grad, q_now))
            hrows = pl.ds(pl.multiple_of(pair * LANES + side * HEAD, HEAD), HEAD)
            dq_t[hrows, at] = (mm(x_t[hrows, :], grad) * HEAD**-0.5).astype(BF16)
        dk_now, dv_now = jnp.concatenate(dks, axis=1), jnp.concatenate(dvs, axis=1)

        @pl.when(qb == 0)
        def _():
            dk_sum[...] = dk_now
            dv_sum[...] = dv_now

        @pl.when(qb > 0)
        def _():
            dk_sum[...] = dk_sum[...] + dk_now
            dv_sum[...] = dv_sum[...] + dv_now

        @pl.when(qb == rbs - 1)
        def _():
            ks[:, cols] = dk_sum[...].astype(BF16)
            vs[:, cols] = dv_sum[...].astype(BF16)

        @pl.when(lax.rem(step, 3) == 1)
        def _():
            big.tick(tau + lax.div(step, 3))

    steps = rbs * (head_cols // LANES)
    each(attend_back, steps)
    tau += steps // 3

    qs[...] = dq_t[...].T
    put_rows(sg, plan["qbias"][0], total(qs[...]))
    put_rows(sg, plan["vbias"][0], total(vs[...]))
    each(first_norm)
    norm_t[...] = norm[...].T
    for i, grads in enumerate((qs, ks, vs)):
        for j in range(PARTS):
            made = mm(norm_t[j * BLK : (j + 1) * BLK, :], grads[...])
            g[(14 + i) % HELD, j] = made[:, :BLK]
            if i * 3 + j < 8:
                c, p, side = leftover(i * 3 + j)
                g[c % HELD, p, :, side * LANES : (side + 1) * LANES] = made[:, BLK:]
            else:
                g[13, 2, LANES:, :LANES] = made[:LANES, BLK:]
                g[13, 2, LANES:, LANES:] = made[LANES:, BLK:]
    big.tick(tau)
    tau += 1

    pl.semaphore_wait(vfree, 1)

    def to_norm(rb):
        at = rows_at(rb, BLK)
        t2[at, :] = mm_t(qs[at, :], qkvw[0]) + mm_t(ks[at, :], qkvw[1]) + mm_t(vs[at, :], qkvw[2])
        swap(3, t2, rb).start()

    each(to_norm)

    def first_norm_back(rb):
        at = rows_at(rb, BLK)
        swap(3, t2, rb).wait()
        grad = t2[at, :] + v[at, :]
        x_hat, scale = normalise(tok[at, :].astype(F32))
        add_rows(sg, plan["gain1"][0], total(grad * x_hat))
        add_rows(sg, plan["shift1"][0], total(grad))
        ing_ref[at, :] = (t3[at, :] + norm_back(x_hat, scale, grad * gain1[...][None, :])).astype(BF16)

    each(first_norm_back)

    rows = plan["genes"][1]
    local = genes[...][None, :] - core * plan["genes"][2]
    high = lax.shift_right_arithmetic(local, 7)
    low = local - high * LANES
    high = (lax.broadcasted_iota(jnp.int32, (rows, tokens), 0) == high).astype(F32).astype(BF16)
    low = (lax.broadcasted_iota(jnp.int32, (LANES, tokens), 0) == low).astype(F32).astype(BF16)
    sg[0, 0, :rows, :] = mm_t(high, low)

    def finish(i, carry):
        big.tick(tau + i)
        small.tick(i)
        return carry

    left = big.chunks + big.stages - tau
    lax.fori_loop(0, max(left, small.stages + 1), finish, 0)


def run_layer(n_dp, plan, small_rows, *args):
    (lengths, genes, tok, cot, gain1, shift1, qkvw, qvb, outw, obias, gain2, shift2, upw, ubias, dnw, dbias) = args
    tokens, features = tok.shape
    units, head_cols = dnw.shape[0], outw.shape[0]
    chunks = (features * (2 * units + 4 * head_cols)) // (PARTS * BLK * BLK)
    _, _, stages = stage_counts(n_dp)
    vmem = pl.BlockSpec(memory_space=pltpu.VMEM)
    smem = pl.BlockSpec(memory_space=pltpu.SMEM)
    hbm = pl.BlockSpec(memory_space=pl.ANY)
    dma = pltpu.SemaphoreType.DMA
    wide = (tokens, features)
    return pl.pallas_call(
        functools.partial(layer, n_dp, plan),
        out_shape=(
            pltpu.VMEM(wide, BF16),
            pltpu.VMEM(wide, BF16),
            pltpu.VMEM((chunks, PARTS, BLK, BLK), F32),
            pltpu.VMEM((1, 1, small_rows, LANES), F32),
        ),
        in_specs=[smem, vmem, hbm, hbm, vmem, vmem, hbm, vmem, hbm, vmem, vmem, vmem, hbm, vmem, hbm, vmem],
        out_specs=(vmem, vmem, vmem, vmem),
        scratch_shapes=[
            pltpu.VMEM(wide, BF16),
            pltpu.VMEM(wide, BF16),
            pltpu.VMEM(qkvw.shape, BF16),
            pltpu.VMEM(outw.shape, BF16),
            pltpu.VMEM(upw.shape, BF16),
            pltpu.VMEM(dnw.shape, BF16),
            pltpu.VMEM((features, tokens), BF16),
            pltpu.VMEM((tokens, head_cols), BF16),
            pltpu.VMEM((tokens, head_cols), BF16),
            pltpu.VMEM((tokens, head_cols), BF16),
            pltpu.VMEM((tokens, head_cols), BF16),
            pltpu.VMEM(wide, F32),
            pltpu.VMEM(wide, F32),
            pltpu.VMEM(wide, F32),
            pltpu.VMEM(wide, F32),
            pltpu.VMEM((HELD, PARTS, BLK, BLK), F32),
            pltpu.VMEM((SLOTS, PARTS, slot_rows(n_dp, BLK), BLK), F32),
            pltpu.VMEM((tokens, BLK), BF16),
            pltpu.VMEM((BLK, tokens), BF16),
            pltpu.VMEM((tokens, BLK), BF16),
            pltpu.VMEM((tokens, BLK), F32),
            pltpu.VMEM((tokens, LANES), jnp.int32),
            pltpu.VMEM((1, 1, small_rows, LANES), F32),
            pltpu.VMEM((1, 1, slot_rows(n_dp, small_rows), LANES), F32),
            dma((6,)),
            dma((4, tokens // BLK)),
            dma((4, tokens // BLK)),
            dma((chunks, PARTS, stages)),
            dma((chunks, PARTS, stages)),
            dma((chunks, PARTS)),
            dma((1, 1, stages)),
            dma((1, 1, stages)),
            dma((1, 1)),
            pltpu.SemaphoreType.REGULAR,
        ],
        compiler_params=pltpu.CompilerParams(
            collective_id=0, has_side_effects=True, vmem_limit_bytes=47 << 20
        ),
    )(*args)


def hand_out(plan, packed, sums, out_ref, ing_ref, *refs):
    (output, input_grad, gain1, shift1, qkv, qv, out, obias, gain2, shift2, up, ubias, down, dbias, genes) = refs[:15]
    sem = refs[15]
    moves = [(out_ref, output), (ing_ref, input_grad)]
    for u in range(down.shape[0] // BLK):
        for p in range(PARTS):
            units, cols = pl.ds(u * BLK, BLK), pl.ds(p * BLK, BLK)
            moves.append((packed.at[2 * u, p], down.at[units, cols]))
            moves.append((packed.at[2 * u + 1, p], up.at[cols, units]))
    half = pl.ds(0, LANES), pl.ds(LANES, LANES)
    for p in range(PARTS):
        cols = pl.ds(p * BLK, BLK)
        moves.append((packed.at[12, p], out.at[pl.ds(0, BLK), cols]))
        rest = packed.at[13, 1 + p // 2, half[p % 2]]
        moves.append((rest, out.at[pl.ds(BLK, LANES), cols]))
    for i in range(3):
        for j in range(PARTS):
            rows, tail = pl.ds(j * BLK, BLK), pl.ds(BLK, LANES)
            moves.append((packed.at[14 + i, j], qkv.at[i, rows, pl.ds(0, BLK)]))
            if i * 3 + j < 8:
                c, p, side = leftover(i * 3 + j)
                moves.append((packed.at[c, p, pl.ds(0, BLK), half[side]], qkv.at[i, rows, tail]))
            else:
                for side in range(2):
                    rows = pl.ds(j * BLK + side * LANES, LANES)
                    moves.append((packed.at[13, 2, half[1], half[side]], qkv.at[i, rows, tail]))
    copies = [pltpu.make_async_copy(src, dst, sem.at[i]) for i, (src, dst) in enumerate(moves)]
    for copy in copies:
        copy.start()

    def vector(name, ref, *index):
        at, count, _ = plan[name]
        for i in range(count):
            ref[(*index, pl.ds(i * LANES, LANES))] = sums[0, 0, at + i]

    for name, ref in (
        ("gain1", gain1),
        ("shift1", shift1),
        ("obias", obias),
        ("gain2", gain2),
        ("shift2", shift2),
        ("ubias", ubias),
        ("dbias", dbias),
    ):
        vector(name, ref)
    vector("qbias", qv, 0)
    vector("vbias", qv, 1)
    size = plan["genes"][2]
    for i in range(-(-size // LANES)):
        part = min(LANES, size - i * LANES)
        genes[pl.ds(i * LANES, part)] = sums[0, 0, i, :part].astype(jnp.int32)
    for copy in copies:
        copy.wait()


def results(plan, features, head_cols, units, packed, sums, output, input_grad):
    vmem = pl.BlockSpec(memory_space=pltpu.VMEM)
    hbm = pl.BlockSpec(memory_space=pl.ANY)
    size = lambda name: (plan[name][2],)
    shapes = (
        output.shape,
        input_grad.shape,
        size("gain1"),
        size("shift1"),
        (3, features, head_cols),
        (2, head_cols),
        (head_cols, features),
        size("obias"),
        size("gain2"),
        size("shift2"),
        (features, units),
        size("ubias"),
        (units, features),
        size("dbias"),
        size("genes"),
    )
    types = [BF16, BF16] + [F32] * 12 + [jnp.int32]
    large = (0, 1, 4, 6, 10, 12)
    return pl.pallas_call(
        functools.partial(hand_out, plan),
        out_shape=tuple(jax.ShapeDtypeStruct(shape, kind) for shape, kind in zip(shapes, types)),
        in_specs=[vmem, vmem, vmem, vmem],
        out_specs=tuple(hbm if i in large else vmem for i in range(15)),
        scratch_shapes=[
            pltpu.SemaphoreType.DMA((80,)),
        ],
        compiler_params=pltpu.CompilerParams(vmem_limit_bytes=16 << 20),
    )(packed, sums, output, input_grad)


def on_device(
    n_dp,
    tokens,
    lengths,
    gene_ids,
    norm1_gain,
    norm1_shift,
    qkv_weight,
    qv_bias,
    out_weight,
    out_bias,
    norm2_gain,
    norm2_shift,
    up_weight,
    up_bias,
    down_weight,
    down_bias,
    cotangent,
):
    features = tokens.shape[1]
    head_cols, units = out_weight.shape[0], down_weight.shape[0]
    plan, small_rows = small_plan(features, head_cols, units, VOCAB // lax.axis_size("tensor"))
    output, input_grad, packed, sums = run_layer(
        n_dp,
        plan,
        small_rows,
        lengths,
        gene_ids,
        tokens,
        cotangent,
        norm1_gain,
        norm1_shift,
        qkv_weight.transpose(1, 0, 2),
        qv_bias,
        out_weight,
        out_bias,
        norm2_gain,
        norm2_shift,
        up_weight,
        up_bias,
        down_weight,
        down_bias,
    )
    made = list(results(plan, features, head_cols, units, packed, sums, output, input_grad))
    made[4] = made[4].transpose(1, 0, 2)
    return tuple(made)


def solution(mesh):
    return jax.shard_map(
        functools.partial(on_device, mesh.shape["dp"]),
        mesh=mesh,
        in_specs=(
            P("dp", None),
            P("dp", None),
            P("dp"),
            P(),
            P(),
            P(None, None, "tensor"),
            P(None, "tensor"),
            P("tensor", None),
            P(),
            P(),
            P(),
            P(None, "tensor"),
            P("tensor"),
            P("tensor", None),
            P(),
            P("dp", None),
        ),
        out_specs=(
            P("dp", None),
            P("dp", None),
            P(),
            P(),
            P(None, None, "tensor"),
            P(None, "tensor"),
            P("tensor", None),
            P(),
            P(),
            P(),
            P(None, "tensor"),
            P("tensor"),
            P("tensor", None),
            P(),
            P("tensor"),
        ),
        check_vma=False,
    )
```

```python
import functools

import jax
import jax.numpy as jnp
from jax import lax
from jax.experimental import pallas as pl
from jax.experimental.pallas import tpu as pltpu
from jax.sharding import PartitionSpec as P

HEAD = 64
VOCAB = 36000
MESH = pl.DeviceIdType.MESH
F32, BF16 = jnp.float32, jnp.bfloat16
BLK = 256
PARTS = 3
SLOTS = 4
HELD = 14
LANES = 128


def mm(left, right):
    return jnp.dot(left, right, preferred_element_type=F32)


def mm_t(left, right):
    return lax.dot_general(left, right, (((1,), (1,)), ((), ())), preferred_element_type=F32)


def bit_of(index, mask):
    return lax.rem(lax.div(index, mask), 2)


def rows_at(index, size):
    return pl.ds(pl.multiple_of(index * size, size), size)


class Exchange:
    def __init__(self, n_dp, chunks, parts, slots, g, r, o, ssem, rsem, osem):
        self.chunks, self.parts, self.slots = chunks, parts, slots
        self.g, self.r, self.o = g, r, o
        self.ssem, self.rsem, self.osem = ssem, rsem, osem
        self.rows = g.shape[2]
        self.bits, self.half, self.stages = stage_counts(n_dp)
        self.dp, self.core = lax.axis_index("dp"), lax.axis_index("tensor")

    def mask(self, c, p, k):
        if k >= 3 or self.bits < 3 or p == 0:
            return 1 << k
        if p == 1:
            return 1 << (1, 0, 2)[k]
        if k == 0:
            return 4
        odd = lax.rem(c, 2)
        return 1 + odd if k == 1 else 2 - odd

    def first(self, c, p, depth):
        at = 0
        for k in range(depth):
            at = at + bit_of(self.dp, self.mask(c, p, k)) * (self.rows >> (k + 1))
        return at

    def held(self, c):
        return lax.rem(c, self.g.shape[0])

    def slot(self, s):
        if s < self.half:
            return pl.ds(self.rows - (self.rows >> s), self.rows >> (s + 1))
        size = self.rows >> self.half
        return pl.ds(self.rows - size + (s - self.half) * size, size)

    def own(self, c, p, depth):
        return pl.ds(pl.multiple_of(self.first(c, p, depth), 8), self.rows >> depth)

    def copy(self, c, p, s):
        flat_end = self.stages - self.half
        k = s if s < flat_end else self.stages - 1 - s
        mask = self.mask(c, p, k)
        bit = bit_of(self.dp, mask)
        if s < self.half:
            size = self.rows >> (s + 1)
            away = pl.ds(pl.multiple_of(self.first(c, p, s) + (1 - bit) * size, 8), size)
            src = self.g.at[self.held(c), p, away]
        elif s < flat_end:
            src = self.g.at[self.held(c), p, self.own(c, p, self.half)]
        if s < flat_end:
            dst = self.r.at[lax.rem(c, self.slots), p, self.slot(s)]
        else:
            mine = self.own(c, p, k + 1)
            dst = self.o.at[c, p, mine]
            src = self.g.at[self.held(c), p, mine] if s == flat_end else dst
        return pltpu.make_async_remote_copy(
            src,
            dst,
            self.ssem.at[lax.rem(c, self.slots), p, s],
            self.rsem.at[lax.rem(c, self.slots), p, s],
            device_id=(self.dp + mask * (1 - 2 * bit), self.core),
            device_id_type=MESH,
        )

    def keep(self, c, p):
        mine = self.own(c, p, self.half)
        return pltpu.make_async_copy(self.g.at[self.held(c), p, mine], self.o.at[c, p, mine], self.osem.at[lax.rem(c, self.slots), p])

    def tick(self, tau):
        flat_end = self.stages - self.half
        for s in range(self.stages + 1):
            c = tau - s

            @pl.when((c >= 0) & (c < self.chunks))
            def _():
                for p in range(self.parts):
                    if s > 0:
                        self.copy(c, p, s - 1).wait()
                    if 0 < s <= flat_end:
                        mine = self.own(c, p, min(s, self.half))
                        got = self.r[lax.rem(c, self.slots), p, self.slot(s - 1)]
                        at = self.held(c)
                        self.g[at, p, mine] = self.g[at, p, mine] + got
                    if s == flat_end:
                        self.keep(c, p).start()
                    if s == flat_end + 1:
                        self.keep(c, p).wait()
                    if s < self.stages:
                        self.copy(c, p, s).start()


def stage_counts(n_dp):
    bits = n_dp.bit_length() - 1
    half = min(bits, 4)
    return bits, half, bits + half


def slot_rows(n_dp, rows):
    bits, half, _ = stage_counts(n_dp)
    return rows - (rows >> half) + (bits - half) * (rows >> half)


def normalise(x):
    c = x - jnp.mean(x, axis=-1, keepdims=True)
    scale = lax.rsqrt(jnp.mean(c * c, axis=-1, keepdims=True) + 1e-05)
    return c * scale, scale


def norm_back(x_hat, scale, grad):
    middle = jnp.mean(grad, axis=-1, keepdims=True)
    along = jnp.mean(grad * x_hat, axis=-1, keepdims=True)
    return (grad - middle - x_hat * along) * scale


def total(x):
    return jnp.sum(x.astype(F32), axis=0, keepdims=True)


def put_rows(ref, row, vector):
    for i in range(vector.shape[1] // LANES):
        ref[0, 0, row + i : row + i + 1, :] = vector[:, i * LANES : (i + 1) * LANES]


def add_rows(ref, row, vector):
    for i in range(vector.shape[1] // LANES):
        at = slice(row + i, row + i + 1)
        ref[0, 0, at, :] = ref[0, 0, at, :] + vector[:, i * LANES : (i + 1) * LANES]


def small_plan(features, head_cols, units, vocab_local):
    plan, at = {}, 0
    for name, size in (
        ("genes", vocab_local),
        ("gain1", features),
        ("shift1", features),
        ("qbias", head_cols),
        ("vbias", head_cols),
        ("obias", features),
        ("gain2", features),
        ("shift2", features),
        ("ubias", units),
        ("dbias", features),
    ):
        count = -(-size // LANES)
        if name == "genes":
            count = -(-count // 8) * 8
        plan[name] = (at, count, size)
        at += count
    return plan, -(-at // 128) * 128


def leftover(j):
    block = 9 + j // 2
    return (17, 13)[block // 3 - 3], block % 3, j % 2


def layer(
    n_dp,
    plan,
    lengths_h,
    genes_h,
    tok_h,
    cot_h,
    gain1_h,
    shift1_h,
    qkvw_h,
    qvb_h,
    outw_h,
    obias_h,
    gain2_h,
    shift2_h,
    upw_h,
    ubias_h,
    dnw_h,
    dbias_h,
    out_ref,
    ing_ref,
    o,
    o_small,
    tok,
    cot,
    qkvw,
    outw,
    upw,
    dnw,
    norm_t,
    qs,
    ks,
    vs,
    ctx,
    t1,
    t2,
    t3,
    v,
    g,
    r,
    act,
    act_t,
    gu,
    seg,
    sg,
    sr,
    lsem,
    esend,
    erecv,
    ssem,
    rsem,
    osem,
    sssem,
    srsem,
    sosem,
    vfree,
    lengths,
    genes,
    gain1,
    shift1,
    qvb,
    obias,
    gain2,
    shift2,
    ubias,
    dbias,
):
    tokens, features = tok.shape
    head_cols = qs.shape[1]
    units = dnw.shape[0]
    rbs = tokens // BLK
    dq_t, x_t = norm_t.at[:head_cols], norm_t.at[head_cols : 2 * head_cols]
    dctx, norm = ctx, ing_ref
    slope, dk_sum, dv_sum = v.at[:, :BLK], v.at[:, :LANES], v.at[:, LANES:BLK]
    dp, core = lax.axis_index("dp"), lax.axis_index("tensor")
    other = (dp, 1 - core)

    loads = [
        pltpu.make_async_copy(src, dst, lsem.at[i])
        for i, (src, dst) in enumerate(
            (
                (tok_h, tok),
                (lengths_h, lengths),
                (gain1_h, gain1),
                (shift1_h, shift1),
                (qkvw_h, qkvw),
                (qvb_h, qvb),
                (outw_h, outw),
                (obias_h, obias),
                (gain2_h, gain2),
                (shift2_h, shift2),
                (upw_h, upw),
                (ubias_h, ubias),
                (cot_h, cot),
                (dnw_h, dnw),
                (dbias_h, dbias),
                (genes_h, genes),
            )
        )
    ]
    for load in loads:
        load.start()

    bar = pltpu.get_barrier_semaphore()
    bits = n_dp.bit_length() - 1
    for k in range(bits):
        bit = bit_of(dp, 1 << k)
        to = (dp + (1 << k) * (1 - 2 * bit), core)
        pl.semaphore_signal(bar, inc=1, device_id=to, device_id_type=MESH)
    pl.semaphore_signal(bar, inc=1, device_id=other, device_id_type=MESH)

    big = Exchange(n_dp, o.shape[0], PARTS, SLOTS, g, r, o, ssem, rsem, osem)
    small = Exchange(n_dp, 1, 1, 1, sg, sr, o_small, sssem, srsem, sosem)

    def swap(e, src, rb):
        at = rows_at(rb, BLK)
        return pltpu.make_async_remote_copy(
            src.at[at], v.at[at], esend.at[e, rb], erecv.at[e, rb], device_id=other, device_id_type=MESH
        )

    def freed():
        pl.semaphore_signal(vfree, inc=1, device_id=other, device_id_type=MESH)

    def each(body, count=rbs):
        def step(i, carry):
            body(i)
            return carry

        lax.fori_loop(0, count, step, 0)

    def segment(position):
        ends, seg_now = 0, jnp.zeros(position.shape, jnp.int32)
        for i in range(lengths.shape[1]):
            ends = ends + lengths[0, i]
            seg_now = seg_now + (position >= ends).astype(jnp.int32)
        return seg_now

    loads[1].wait()
    seg[...] = segment(lax.broadcasted_iota(jnp.int32, (tokens, LANES), 0))
    sg[...] = jnp.zeros_like(sg)

    for i in (0, 2, 3):
        loads[i].wait()

    def first_norm(rb):
        at = rows_at(rb, BLK)
        x_hat, _ = normalise(tok[at, :].astype(F32))
        norm[at, :] = (x_hat * gain1[...][None, :] + shift1[...][None, :]).astype(BF16)

    each(first_norm)
    for load in loads[4:6]:
        load.wait()

    def project(rb):
        at = rows_at(rb, BLK)
        x = norm[at, :]
        qs[at, :] = (mm(x, qkvw[0]) + qvb[0:1, :]).astype(BF16) * BF16(HEAD**-0.5)
        ks[at, :] = mm(x, qkvw[1]).astype(BF16)
        vs[at, :] = (mm(x, qkvw[2]) + qvb[1:2, :]).astype(BF16)

    each(project)
    loads[6].wait()
    pl.semaphore_wait(bar, bits + 1)

    def attend(rb):
        at = rows_at(rb, BLK)
        seg_row = segment(lax.broadcasted_iota(jnp.int32, (1, tokens), 1))
        same = jnp.concatenate([seg[at, :]] * (tokens // LANES), axis=1) == seg_row
        for pair in range(head_cols // LANES):
            sides = []
            for side in range(2):
                cols = slice(pair * LANES + side * HEAD, pair * LANES + (side + 1) * HEAD)
                scores = jnp.where(same, mm_t(qs[at, cols], ks[:, cols]), -1000000000.0)
                e = jnp.exp(scores - jnp.max(scores, axis=-1, keepdims=True))
                inverse = 1.0 / jnp.sum(e, axis=-1, keepdims=True)
                sides.append(mm(e.astype(BF16), vs[:, cols]) * inverse)
            ctx[at, pair * LANES : (pair + 1) * LANES] = jnp.concatenate(sides, axis=1).astype(BF16)
        t1[at, :] = mm(ctx[at, :], outw[...])
        swap(0, t1, rb).start()

    each(attend)
    for load in loads[7:]:
        load.wait()

    def second_norm(rb):
        at = rows_at(rb, BLK)
        swap(0, t1, rb).wait()
        hidden = tok[at, :].astype(F32) + (t1[at, :] + v[at, :]) + obias[...][None, :]
        t1[at, :] = hidden
        x_hat, _ = normalise(hidden)
        norm[at, :] = (x_hat * gain2[...][None, :] + shift2[...][None, :]).astype(BF16)
        t2[at, :] = jnp.zeros((BLK, features), F32)
        t3[at, :] = jnp.zeros((BLK, features), F32)

    each(second_norm)

    def feed_forward(u):
        ucols = rows_at(u, BLK)

        def upper(rb):
            at = rows_at(rb, BLK)
            up = mm(norm[at, :], upw[:, ucols]) + ubias[ucols][None, :]
            cdf = 0.5 * (1.0 + lax.erf(up * 0.7071067811865476))
            act[at, :] = (up * cdf).astype(BF16)
            slope[at, :] = cdf + up * (jnp.exp(-0.5 * up * up) * 0.3989422804014327)

        each(upper)
        act_t[...] = act[...].T
        for p in range(PARTS):
            g[2 * u, p] = mm(act_t[...], cot[:, p * BLK : (p + 1) * BLK])
        big.tick(u + jnp.minimum(u, 1))

        @pl.when(u == 0)
        def _():
            norm_t[...] = norm[...].T

        def lower(rb, sums):
            at = rows_at(rb, BLK)
            down_rows = dnw[ucols, :]
            grad = (mm_t(cot[at, :], down_rows) * slope[at, :]).astype(BF16)
            gu[at, :] = grad
            t2[at, :] = t2[at, :] + mm(act[at, :], down_rows)
            t3[at, :] = t3[at, :] + mm_t(grad, upw[:, ucols])
            return sums + total(grad)

        sums = lax.fori_loop(0, rbs, lower, jnp.zeros((1, BLK), F32))
        row = plan["ubias"][0] + u * (BLK // LANES)
        for i in range(BLK // LANES):
            sg[0, 0, pl.ds(row + i, 1), :] = sums[:, i * LANES : (i + 1) * LANES]
        for p in range(PARTS):
            g[2 * u + 1, p] = mm(norm_t[p * BLK : (p + 1) * BLK, :], gu[...])

        @pl.when(u == 0)
        def _():
            big.tick(1)

    each(feed_forward, units // BLK)
    freed()
    tau = units // BLK + 1

    pl.semaphore_wait(vfree, 1)
    each(lambda rb: swap(1, t3, rb).start())
    big.tick(tau)
    tau += 1

    x_t[...] = ctx[...].T

    def second_norm_back(rb):
        at = rows_at(rb, BLK)
        swap(1, t3, rb).wait()
        grad = t3[at, :] + v[at, :]
        x_hat, scale = normalise(t1[at, :])
        add_rows(sg, plan["gain2"][0], total(grad * x_hat))
        add_rows(sg, plan["shift2"][0], total(grad))
        given = cot[at, :].astype(F32)
        add_rows(sg, plan["dbias"][0], total(given))
        grad = given + norm_back(x_hat, scale, grad * gain2[...][None, :])
        t3[at, :] = grad
        norm[at, :] = grad.astype(BF16)
        add_rows(sg, plan["obias"][0], total(norm[at, :]))
        dctx[at, :] = mm_t(norm[at, :], outw[...]).astype(BF16)

    each(second_norm_back)
    freed()
    pl.semaphore_wait(vfree, 1)
    each(lambda rb: swap(2, t2, rb).start())

    for p in range(PARTS):
        branch = norm[:, p * BLK : (p + 1) * BLK]
        g[12, p] = mm(x_t[:BLK, :], branch)
        rest = mm(x_t[BLK:, :], branch)
        if p < 2:
            g[13, 1, p * LANES : (p + 1) * LANES] = rest
        else:
            g[13, 2, :LANES] = rest
    big.tick(tau)
    tau += 1

    def result(rb):
        at = rows_at(rb, BLK)
        swap(2, t2, rb).wait()
        out_ref[at, :] = (t1[at, :] + (t2[at, :] + v[at, :]) + dbias[...][None, :]).astype(BF16)

    each(result)

    x_t[...] = ks[...].T

    def attend_back(step):
        pair, qb = lax.div(step, rbs), lax.rem(step, rbs)
        at = rows_at(qb, BLK)
        cols = rows_at(pair, LANES)
        position = lax.broadcasted_iota(jnp.int32, (1, BLK), 1) + qb * BLK
        seg_row = segment(position)
        same = jnp.concatenate([seg[...]] * (BLK // LANES), axis=1) == seg_row
        dks, dvs = [], []
        for side in range(2):
            lanes = slice(side * HEAD, (side + 1) * HEAD)
            q_now, d_now = qs[at, cols][:, lanes], dctx[at, cols][:, lanes]
            scores = jnp.where(same, mm_t(ks[:, cols][:, lanes], q_now), -1000000000.0)
            e = jnp.exp(scores - jnp.max(scores, axis=0, keepdims=True))
            probs = e * (1.0 / jnp.sum(e, axis=0, keepdims=True))
            grad = mm_t(vs[:, cols][:, lanes], d_now)
            inner = jnp.sum(probs * grad, axis=0, keepdims=True)
            grad = (probs * (grad - inner)).astype(BF16)
            dvs.append(mm(probs.astype(BF16), d_now))
            dks.append(mm(grad, q_now))
            hrows = pl.ds(pl.multiple_of(pair * LANES + side * HEAD, HEAD), HEAD)
            dq_t[hrows, at] = (mm(x_t[hrows, :], grad) * HEAD**-0.5).astype(BF16)
        dk_now, dv_now = jnp.concatenate(dks, axis=1), jnp.concatenate(dvs, axis=1)

        @pl.when(qb == 0)
        def _():
            dk_sum[...] = dk_now
            dv_sum[...] = dv_now

        @pl.when(qb > 0)
        def _():
            dk_sum[...] = dk_sum[...] + dk_now
            dv_sum[...] = dv_sum[...] + dv_now

        @pl.when(qb == rbs - 1)
        def _():
            ks[:, cols] = dk_sum[...].astype(BF16)
            vs[:, cols] = dv_sum[...].astype(BF16)

        @pl.when(lax.rem(step, 3) == 1)
        def _():
            big.tick(tau + lax.div(step, 3))

    steps = rbs * (head_cols // LANES)
    each(attend_back, steps)
    freed()
    tau += steps // 3

    qs[...] = dq_t[...].T
    put_rows(sg, plan["qbias"][0], total(qs[...]))
    put_rows(sg, plan["vbias"][0], total(vs[...]))
    each(first_norm)
    norm_t[...] = norm[...].T
    for i, grads in enumerate((qs, ks, vs)):
        for j in range(PARTS):
            made = mm(norm_t[j * BLK : (j + 1) * BLK, :], grads[...])
            g[(14 + i) % HELD, j] = made[:, :BLK]
            if i * 3 + j < 8:
                c, p, side = leftover(i * 3 + j)
                g[c % HELD, p, :, side * LANES : (side + 1) * LANES] = made[:, BLK:]
            else:
                g[13, 2, LANES:, :LANES] = made[:LANES, BLK:]
                g[13, 2, LANES:, LANES:] = made[LANES:, BLK:]
    big.tick(tau)
    tau += 1

    pl.semaphore_wait(vfree, 1)

    def to_norm(rb):
        at = rows_at(rb, BLK)
        t2[at, :] = mm_t(qs[at, :], qkvw[0]) + mm_t(ks[at, :], qkvw[1]) + mm_t(vs[at, :], qkvw[2])
        swap(3, t2, rb).start()

    each(to_norm)

    def first_norm_back(rb):
        at = rows_at(rb, BLK)
        swap(3, t2, rb).wait()
        grad = t2[at, :] + v[at, :]
        x_hat, scale = normalise(tok[at, :].astype(F32))
        add_rows(sg, plan["gain1"][0], total(grad * x_hat))
        add_rows(sg, plan["shift1"][0], total(grad))
        ing_ref[at, :] = (t3[at, :] + norm_back(x_hat, scale, grad * gain1[...][None, :])).astype(BF16)

    each(first_norm_back)

    rows = plan["genes"][1]
    local = genes[...][None, :] - core * plan["genes"][2]
    high = lax.shift_right_arithmetic(local, 7)
    low = local - high * LANES
    high = (lax.broadcasted_iota(jnp.int32, (rows, tokens), 0) == high).astype(F32).astype(BF16)
    low = (lax.broadcasted_iota(jnp.int32, (LANES, tokens), 0) == low).astype(F32).astype(BF16)
    sg[0, 0, :rows, :] = mm_t(high, low)

    def finish(i, carry):
        big.tick(tau + i)
        small.tick(i)
        return carry

    left = big.chunks + big.stages - tau
    lax.fori_loop(0, max(left, small.stages + 1), finish, 0)


def run_layer(n_dp, plan, small_rows, *args):
    (lengths, genes, tok, cot, gain1, shift1, qkvw, qvb, outw, obias, gain2, shift2, upw, ubias, dnw, dbias) = args
    tokens, features = tok.shape
    units, head_cols = dnw.shape[0], outw.shape[0]
    chunks = (features * (2 * units + 4 * head_cols)) // (PARTS * BLK * BLK)
    _, _, stages = stage_counts(n_dp)
    vmem = pl.BlockSpec(memory_space=pltpu.VMEM)
    hbm = pl.BlockSpec(memory_space=pl.ANY)
    dma = pltpu.SemaphoreType.DMA
    wide = (tokens, features)
    return pl.pallas_call(
        functools.partial(layer, n_dp, plan),
        out_shape=(
            pltpu.VMEM(wide, BF16),
            pltpu.VMEM(wide, BF16),
            pltpu.VMEM((chunks, PARTS, BLK, BLK), F32),
            pltpu.VMEM((1, 1, small_rows, LANES), F32),
        ),
        in_specs=[hbm] * 16,
        out_specs=(vmem, vmem, vmem, vmem),
        scratch_shapes=[
            pltpu.VMEM(wide, BF16),
            pltpu.VMEM(wide, BF16),
            pltpu.VMEM(qkvw.shape, BF16),
            pltpu.VMEM(outw.shape, BF16),
            pltpu.VMEM(upw.shape, BF16),
            pltpu.VMEM(dnw.shape, BF16),
            pltpu.VMEM((features, tokens), BF16),
            pltpu.VMEM((tokens, head_cols), BF16),
            pltpu.VMEM((tokens, head_cols), BF16),
            pltpu.VMEM((tokens, head_cols), BF16),
            pltpu.VMEM((tokens, head_cols), BF16),
            pltpu.VMEM(wide, F32),
            pltpu.VMEM(wide, F32),
            pltpu.VMEM(wide, F32),
            pltpu.VMEM(wide, F32),
            pltpu.VMEM((HELD, PARTS, BLK, BLK), F32),
            pltpu.VMEM((SLOTS, PARTS, slot_rows(n_dp, BLK), BLK), F32),
            pltpu.VMEM((tokens, BLK), BF16),
            pltpu.VMEM((BLK, tokens), BF16),
            pltpu.VMEM((tokens, BLK), BF16),
            pltpu.VMEM((tokens, LANES), jnp.int32),
            pltpu.VMEM((1, 1, small_rows, LANES), F32),
            pltpu.VMEM((1, 1, slot_rows(n_dp, small_rows), LANES), F32),
            dma((16,)),
            dma((4, tokens // BLK)),
            dma((4, tokens // BLK)),
            dma((SLOTS, PARTS, stages)),
            dma((SLOTS, PARTS, stages)),
            dma((SLOTS, PARTS)),
            dma((1, 1, stages)),
            dma((1, 1, stages)),
            dma((1, 1)),
            pltpu.SemaphoreType.REGULAR,
            pltpu.SMEM(lengths.shape, jnp.int32),
            pltpu.VMEM(genes.shape, jnp.int32),
            *(pltpu.VMEM(x.shape, F32) for x in (gain1, shift1, qvb, obias, gain2, shift2, ubias, dbias)),
        ],
        compiler_params=pltpu.CompilerParams(
            collective_id=0, has_side_effects=True, vmem_limit_bytes=47 << 20
        ),
    )(*args)


def hand_out(plan, packed, sums, out_ref, ing_ref, *refs):
    (output, input_grad, gain1, shift1, qkv, qv, out, obias, gain2, shift2, up, ubias, down, dbias, genes) = refs[:15]
    sem = refs[15]
    moves = [(out_ref, output), (ing_ref, input_grad)]
    for u in range(down.shape[0] // BLK):
        for p in range(PARTS):
            units, cols = pl.ds(u * BLK, BLK), pl.ds(p * BLK, BLK)
            moves.append((packed.at[2 * u, p], down.at[units, cols]))
            moves.append((packed.at[2 * u + 1, p], up.at[cols, units]))
    half = pl.ds(0, LANES), pl.ds(LANES, LANES)
    for p in range(PARTS):
        cols = pl.ds(p * BLK, BLK)
        moves.append((packed.at[12, p], out.at[pl.ds(0, BLK), cols]))
        rest = packed.at[13, 1 + p // 2, half[p % 2]]
        moves.append((rest, out.at[pl.ds(BLK, LANES), cols]))
    for i in range(3):
        for j in range(PARTS):
            rows, tail = pl.ds(j * BLK, BLK), pl.ds(BLK, LANES)
            moves.append((packed.at[14 + i, j], qkv.at[i, rows, pl.ds(0, BLK)]))
            if i * 3 + j < 8:
                c, p, side = leftover(i * 3 + j)
                moves.append((packed.at[c, p, pl.ds(0, BLK), half[side]], qkv.at[i, rows, tail]))
            else:
                for side in range(2):
                    rows = pl.ds(j * BLK + side * LANES, LANES)
                    moves.append((packed.at[13, 2, half[1], half[side]], qkv.at[i, rows, tail]))
    copies = [pltpu.make_async_copy(src, dst, sem.at[i]) for i, (src, dst) in enumerate(moves)]
    for copy in copies:
        copy.start()

    def vector(name, ref, *index):
        at, count, _ = plan[name]
        for i in range(count):
            ref[(*index, pl.ds(i * LANES, LANES))] = sums[0, 0, at + i]

    for name, ref in (
        ("gain1", gain1),
        ("shift1", shift1),
        ("obias", obias),
        ("gain2", gain2),
        ("shift2", shift2),
        ("ubias", ubias),
        ("dbias", dbias),
    ):
        vector(name, ref)
    vector("qbias", qv, 0)
    vector("vbias", qv, 1)
    size = plan["genes"][2]
    for i in range(-(-size // LANES)):
        part = min(LANES, size - i * LANES)
        genes[pl.ds(i * LANES, part)] = sums[0, 0, i, :part].astype(jnp.int32)
    for copy in copies:
        copy.wait()


def results(plan, features, head_cols, units, packed, sums, output, input_grad):
    vmem = pl.BlockSpec(memory_space=pltpu.VMEM)
    hbm = pl.BlockSpec(memory_space=pl.ANY)
    size = lambda name: (plan[name][2],)
    shapes = (
        output.shape,
        input_grad.shape,
        size("gain1"),
        size("shift1"),
        (3, features, head_cols),
        (2, head_cols),
        (head_cols, features),
        size("obias"),
        size("gain2"),
        size("shift2"),
        (features, units),
        size("ubias"),
        (units, features),
        size("dbias"),
        size("genes"),
    )
    types = [BF16, BF16] + [F32] * 12 + [jnp.int32]
    large = (0, 1, 4, 6, 10, 12)
    return pl.pallas_call(
        functools.partial(hand_out, plan),
        out_shape=tuple(jax.ShapeDtypeStruct(shape, kind) for shape, kind in zip(shapes, types)),
        in_specs=[vmem, vmem, vmem, vmem],
        out_specs=tuple(hbm if i in large else vmem for i in range(15)),
        scratch_shapes=[
            pltpu.SemaphoreType.DMA((80,)),
        ],
        compiler_params=pltpu.CompilerParams(vmem_limit_bytes=16 << 20),
    )(packed, sums, output, input_grad)


def on_device(
    n_dp,
    tokens,
    lengths,
    gene_ids,
    norm1_gain,
    norm1_shift,
    qkv_weight,
    qv_bias,
    out_weight,
    out_bias,
    norm2_gain,
    norm2_shift,
    up_weight,
    up_bias,
    down_weight,
    down_bias,
    cotangent,
):
    features = tokens.shape[1]
    head_cols, units = out_weight.shape[0], down_weight.shape[0]
    plan, small_rows = small_plan(features, head_cols, units, VOCAB // lax.axis_size("tensor"))
    output, input_grad, packed, sums = run_layer(
        n_dp,
        plan,
        small_rows,
        lengths,
        gene_ids,
        tokens,
        cotangent,
        norm1_gain,
        norm1_shift,
        qkv_weight.transpose(1, 0, 2),
        qv_bias,
        out_weight,
        out_bias,
        norm2_gain,
        norm2_shift,
        up_weight,
        up_bias,
        down_weight,
        down_bias,
    )
    made = list(results(plan, features, head_cols, units, packed, sums, output, input_grad))
    made[4] = made[4].transpose(1, 0, 2)
    return tuple(made)


def solution(mesh):
    return jax.shard_map(
        functools.partial(on_device, mesh.shape["dp"]),
        mesh=mesh,
        in_specs=(
            P("dp", None),
            P("dp", None),
            P("dp"),
            P(),
            P(),
            P(None, None, "tensor"),
            P(None, "tensor"),
            P("tensor", None),
            P(),
            P(),
            P(),
            P(None, "tensor"),
            P("tensor"),
            P("tensor", None),
            P(),
            P("dp", None),
        ),
        out_specs=(
            P("dp", None),
            P("dp", None),
            P(),
            P(),
            P(None, None, "tensor"),
            P(None, "tensor"),
            P("tensor", None),
            P(),
            P(),
            P(),
            P(None, "tensor"),
            P("tensor"),
            P("tensor", None),
            P(),
            P("tensor"),
        ),
        check_vma=False,
    )
```

```python
import functools

import jax
import jax.numpy as jnp
from jax import lax
from jax.experimental import pallas as pl
from jax.experimental.pallas import tpu as pltpu
from jax.sharding import PartitionSpec as P

HEAD = 64
VOCAB = 36000
MESH = pl.DeviceIdType.MESH
F32, BF16 = jnp.float32, jnp.bfloat16
BLK = 256
PARTS = 3
SLOTS = 4
HELD = 14
LANES = 128


def mm(left, right):
    return jnp.dot(left, right, preferred_element_type=F32)


def mm_t(left, right):
    return lax.dot_general(left, right, (((1,), (1,)), ((), ())), preferred_element_type=F32)


def bit_of(index, mask):
    return lax.rem(lax.div(index, mask), 2)


def rows_at(index, size):
    return pl.ds(pl.multiple_of(index * size, size), size)


class Exchange:
    def __init__(self, n_dp, chunks, parts, slots, g, r, o, ssem, rsem, osem):
        self.chunks, self.parts, self.slots = chunks, parts, slots
        self.g, self.r, self.o = g, r, o
        self.ssem, self.rsem, self.osem = ssem, rsem, osem
        self.rows = g.shape[2]
        self.bits, self.half, self.stages = stage_counts(n_dp)
        self.dp, self.core = lax.axis_index("dp"), lax.axis_index("tensor")

    def mask(self, c, p, k):
        if k >= 3 or self.bits < 3 or p == 0:
            return 1 << k
        if p == 1:
            return 1 << (1, 0, 2)[k]
        if k == 0:
            return 4
        odd = lax.rem(c, 2)
        return 1 + odd if k == 1 else 2 - odd

    def first(self, c, p, depth):
        at = 0
        for k in range(depth):
            at = at + bit_of(self.dp, self.mask(c, p, k)) * (self.rows >> (k + 1))
        return at

    def held(self, c):
        return lax.rem(c, self.g.shape[0])

    def slot(self, s):
        if s < self.half:
            return pl.ds(self.rows - (self.rows >> s), self.rows >> (s + 1))
        size = self.rows >> self.half
        return pl.ds(self.rows - size + (s - self.half) * size, size)

    def own(self, c, p, depth):
        return pl.ds(pl.multiple_of(self.first(c, p, depth), 8), self.rows >> depth)

    def copy(self, c, p, s):
        flat_end = self.stages - self.half
        k = s if s < flat_end else self.stages - 1 - s
        mask = self.mask(c, p, k)
        bit = bit_of(self.dp, mask)
        if s < self.half:
            size = self.rows >> (s + 1)
            away = pl.ds(pl.multiple_of(self.first(c, p, s) + (1 - bit) * size, 8), size)
            src = self.g.at[self.held(c), p, away]
        elif s < flat_end:
            src = self.g.at[self.held(c), p, self.own(c, p, self.half)]
        if s < flat_end:
            dst = self.r.at[lax.rem(c, self.slots), p, self.slot(s)]
        else:
            mine = self.own(c, p, k + 1)
            dst = self.o.at[c, p, mine]
            src = self.g.at[self.held(c), p, mine] if s == flat_end else dst
        return pltpu.make_async_remote_copy(
            src,
            dst,
            self.ssem.at[lax.rem(c, self.ssem.shape[0]), p, s],
            self.rsem.at[lax.rem(c, self.slots), p, s],
            device_id=(self.dp + mask * (1 - 2 * bit), self.core),
            device_id_type=MESH,
        )

    def keep(self, c, p):
        mine = self.own(c, p, self.half)
        return pltpu.make_async_copy(self.g.at[self.held(c), p, mine], self.o.at[c, p, mine], self.osem.at[lax.rem(c, self.osem.shape[0]), p])

    def tick(self, tau):
        flat_end = self.stages - self.half
        for s in range(self.stages + 1):
            c = tau - s

            @pl.when((c >= 0) & (c < self.chunks))
            def _():
                for p in range(self.parts):
                    if s > 0:
                        self.copy(c, p, s - 1).wait()
                    if 0 < s <= flat_end:
                        mine = self.own(c, p, min(s, self.half))
                        got = self.r[lax.rem(c, self.slots), p, self.slot(s - 1)]
                        at = self.held(c)
                        self.g[at, p, mine] = self.g[at, p, mine] + got
                    if s == flat_end:
                        self.keep(c, p).start()
                    if s == flat_end + 1:
                        self.keep(c, p).wait()
                    if s < self.stages:
                        self.copy(c, p, s).start()


def stage_counts(n_dp):
    bits = n_dp.bit_length() - 1
    half = min(bits, 4)
    return bits, half, bits + half


def slot_rows(n_dp, rows):
    bits, half, _ = stage_counts(n_dp)
    return rows - (rows >> half) + (bits - half) * (rows >> half)


def normalise(x):
    c = x - jnp.mean(x, axis=-1, keepdims=True)
    scale = lax.rsqrt(jnp.mean(c * c, axis=-1, keepdims=True) + 1e-05)
    return c * scale, scale


def norm_back(x_hat, scale, grad):
    middle = jnp.mean(grad, axis=-1, keepdims=True)
    along = jnp.mean(grad * x_hat, axis=-1, keepdims=True)
    return (grad - middle - x_hat * along) * scale


def total(x):
    return jnp.sum(x.astype(F32), axis=0, keepdims=True)


def put_rows(ref, row, vector):
    for i in range(vector.shape[1] // LANES):
        ref[0, 0, row + i : row + i + 1, :] = vector[:, i * LANES : (i + 1) * LANES]


def add_rows(ref, row, vector):
    for i in range(vector.shape[1] // LANES):
        at = slice(row + i, row + i + 1)
        ref[0, 0, at, :] = ref[0, 0, at, :] + vector[:, i * LANES : (i + 1) * LANES]


def small_plan(features, head_cols, units, vocab_local):
    plan, at = {}, 0
    for name, size in (
        ("genes", vocab_local),
        ("gain1", features),
        ("shift1", features),
        ("qbias", head_cols),
        ("vbias", head_cols),
        ("obias", features),
        ("gain2", features),
        ("shift2", features),
        ("ubias", units),
        ("dbias", features),
    ):
        count = -(-size // LANES)
        if name == "genes":
            count = -(-count // 8) * 8
        plan[name] = (at, count, size)
        at += count
    return plan, -(-at // 128) * 128


def leftover(j):
    block = 9 + j // 2
    return (17, 13)[block // 3 - 3], block % 3, j % 2


def layer(
    n_dp,
    plan,
    lengths_h,
    genes_h,
    tok_h,
    cot_h,
    gain1_h,
    shift1_h,
    qkvw_h,
    qvb_h,
    outw_h,
    obias_h,
    gain2_h,
    shift2_h,
    upw_h,
    ubias_h,
    dnw_h,
    dbias_h,
    out_ref,
    ing_ref,
    o,
    o_small,
    tok,
    cot,
    qkvw,
    outw,
    upw,
    dnw,
    norm_t,
    qs,
    ks,
    vs,
    ctx,
    t1,
    t2,
    t3,
    v,
    g,
    r,
    act_t,
    seg,
    sg,
    sr,
    lsem,
    esend,
    erecv,
    ssem,
    rsem,
    osem,
    sssem,
    srsem,
    sosem,
    vfree,
    lengths,
    genes,
    gain1,
    shift1,
    qvb,
    obias,
    gain2,
    shift2,
    ubias,
    dbias,
):
    tokens, features = tok.shape
    head_cols = qs.shape[1]
    units = dnw.shape[0]
    rbs = tokens // BLK
    dq_t, x_t = norm_t.at[:head_cols], norm_t.at[head_cols : 2 * head_cols]
    dctx, norm = ctx, ing_ref
    act, gu = out_ref.at[:, :BLK], out_ref.at[:, BLK : 2 * BLK]
    slope, dk_sum, dv_sum = v.at[:, :BLK], v.at[:, :LANES], v.at[:, LANES:BLK]
    dp, core = lax.axis_index("dp"), lax.axis_index("tensor")
    other = (dp, 1 - core)

    loads = [
        pltpu.make_async_copy(src, dst, lsem.at[i])
        for i, (src, dst) in enumerate(
            (
                (tok_h, tok),
                (lengths_h, lengths),
                (gain1_h, gain1),
                (shift1_h, shift1),
                (qkvw_h, qkvw),
                (qvb_h, qvb),
                (outw_h, outw),
                (obias_h, obias),
                (gain2_h, gain2),
                (shift2_h, shift2),
                (upw_h, upw),
                (ubias_h, ubias),
                (cot_h, cot),
                (dnw_h, dnw),
                (dbias_h, dbias),
                (genes_h, genes),
            )
        )
    ]
    for load in loads:
        load.start()

    bar = pltpu.get_barrier_semaphore()
    bits = n_dp.bit_length() - 1
    for k in range(bits):
        bit = bit_of(dp, 1 << k)
        to = (dp + (1 << k) * (1 - 2 * bit), core)
        pl.semaphore_signal(bar, inc=1, device_id=to, device_id_type=MESH)
    pl.semaphore_signal(bar, inc=1, device_id=other, device_id_type=MESH)

    big = Exchange(n_dp, o.shape[0], PARTS, SLOTS, g, r, o, ssem, rsem, osem)
    small = Exchange(n_dp, 1, 1, 1, sg, sr, o_small, sssem, srsem, sosem)

    def swap(e, src, rb):
        at = rows_at(rb, BLK)
        return pltpu.make_async_remote_copy(
            src.at[at], v.at[at], esend.at[e, rb], erecv.at[e, rb], device_id=other, device_id_type=MESH
        )

    def freed():
        pl.semaphore_signal(vfree, inc=1, device_id=other, device_id_type=MESH)

    def each(body, count=rbs):
        def step(i, carry):
            body(i)
            return carry

        lax.fori_loop(0, count, step, 0)

    def segment(position):
        ends, seg_now = 0, jnp.zeros(position.shape, jnp.int32)
        for i in range(lengths.shape[1]):
            ends = ends + lengths[0, i]
            seg_now = seg_now + (position >= ends).astype(jnp.int32)
        return seg_now

    loads[1].wait()
    seg[...] = segment(lax.broadcasted_iota(jnp.int32, (tokens, LANES), 0))
    sg[...] = jnp.zeros_like(sg)

    for i in (0, 2, 3):
        loads[i].wait()

    def first_norm(rb):
        at = rows_at(rb, BLK)
        x_hat, _ = normalise(tok[at, :].astype(F32))
        norm[at, :] = (x_hat * gain1[...][None, :] + shift1[...][None, :]).astype(BF16)

    each(first_norm)
    for load in loads[4:6]:
        load.wait()

    def project(rb):
        at = rows_at(rb, BLK)
        x = norm[at, :]
        qs[at, :] = (mm(x, qkvw[0]) + qvb[0:1, :]).astype(BF16) * BF16(HEAD**-0.5)
        ks[at, :] = mm(x, qkvw[1]).astype(BF16)
        vs[at, :] = (mm(x, qkvw[2]) + qvb[1:2, :]).astype(BF16)

    each(project)
    loads[6].wait()
    pl.semaphore_wait(bar, bits + 1)

    def attend(rb):
        at = rows_at(rb, BLK)
        seg_row = segment(lax.broadcasted_iota(jnp.int32, (1, tokens), 1))
        same = jnp.concatenate([seg[at, :]] * (tokens // LANES), axis=1) == seg_row
        heads = head_cols // HEAD

        def scores_of(h):
            cols = slice(h * HEAD, (h + 1) * HEAD)
            return jnp.where(same, mm_t(qs[at, cols], ks[:, cols]), -1000000000.0)

        ready, sides = scores_of(0), []
        for h in range(heads):
            scores = ready
            if h + 1 < heads:
                ready = scores_of(h + 1)
            e = jnp.exp(scores - jnp.max(scores, axis=-1, keepdims=True))
            inverse = 1.0 / jnp.sum(e, axis=-1, keepdims=True)
            sides.append(mm(e.astype(BF16), vs[:, h * HEAD : (h + 1) * HEAD]) * inverse)
            if h % 2:
                ctx[at, (h - 1) * HEAD : (h + 1) * HEAD] = jnp.concatenate(sides, axis=1).astype(BF16)
                sides = []
        t1[at, :] = mm(ctx[at, :], outw[...])
        swap(0, t1, rb).start()

    each(attend)
    for load in loads[7:]:
        load.wait()

    def second_norm(rb):
        at = rows_at(rb, BLK)
        swap(0, t1, rb).wait()
        hidden = tok[at, :].astype(F32) + (t1[at, :] + v[at, :]) + obias[...][None, :]
        t1[at, :] = hidden
        x_hat, _ = normalise(hidden)
        norm[at, :] = (x_hat * gain2[...][None, :] + shift2[...][None, :]).astype(BF16)
        t2[at, :] = jnp.zeros((BLK, features), F32)
        t3[at, :] = jnp.zeros((BLK, features), F32)

    each(second_norm)

    def feed_forward(u):
        ucols = rows_at(u, BLK)

        def upper(rb):
            at = rows_at(rb, BLK)
            up = mm(norm[at, :], upw[:, ucols]) + ubias[ucols][None, :]
            cdf = 0.5 * (1.0 + lax.erf(up * 0.7071067811865476))
            act[at, :] = (up * cdf).astype(BF16)
            slope[at, :] = cdf + up * (jnp.exp(-0.5 * up * up) * 0.3989422804014327)

        each(upper)
        act_t[...] = act[...].T
        for p in range(PARTS):
            g[2 * u, p] = mm(act_t[...], cot[:, p * BLK : (p + 1) * BLK])
        big.tick(u + jnp.minimum(u, 1))

        @pl.when(u == 0)
        def _():
            norm_t[...] = norm[...].T

        def lower(rb, sums):
            at = rows_at(rb, BLK)
            down_rows = dnw[ucols, :]
            grad = (mm_t(cot[at, :], down_rows) * slope[at, :]).astype(BF16)
            gu[at, :] = grad
            t2[at, :] = t2[at, :] + mm(act[at, :], down_rows)
            t3[at, :] = t3[at, :] + mm_t(grad, upw[:, ucols])
            return sums + total(grad)

        sums = lax.fori_loop(0, rbs, lower, jnp.zeros((1, BLK), F32))
        row = plan["ubias"][0] + u * (BLK // LANES)
        for i in range(BLK // LANES):
            sg[0, 0, pl.ds(row + i, 1), :] = sums[:, i * LANES : (i + 1) * LANES]
        for p in range(PARTS):
            g[2 * u + 1, p] = mm(norm_t[p * BLK : (p + 1) * BLK, :], gu[...])

        @pl.when(u == 0)
        def _():
            big.tick(1)

    each(feed_forward, units // BLK)
    freed()
    tau = units // BLK + 1

    pl.semaphore_wait(vfree, 1)
    each(lambda rb: swap(1, t3, rb).start())
    big.tick(tau)
    tau += 1

    x_t[...] = ctx[...].T

    def second_norm_back(rb):
        at = rows_at(rb, BLK)
        swap(1, t3, rb).wait()
        grad = t3[at, :] + v[at, :]
        x_hat, scale = normalise(t1[at, :])
        add_rows(sg, plan["gain2"][0], total(grad * x_hat))
        add_rows(sg, plan["shift2"][0], total(grad))
        given = cot[at, :].astype(F32)
        add_rows(sg, plan["dbias"][0], total(given))
        grad = given + norm_back(x_hat, scale, grad * gain2[...][None, :])
        t3[at, :] = grad
        norm[at, :] = grad.astype(BF16)
        add_rows(sg, plan["obias"][0], total(norm[at, :]))
        dctx[at, :] = mm_t(norm[at, :], outw[...]).astype(BF16)

    each(second_norm_back)
    freed()
    pl.semaphore_wait(vfree, 1)
    each(lambda rb: swap(2, t2, rb).start())

    for p in range(PARTS):
        branch = norm[:, p * BLK : (p + 1) * BLK]
        g[12, p] = mm(x_t[:BLK, :], branch)
        rest = mm(x_t[BLK:, :], branch)
        if p < 2:
            g[13, 1, p * LANES : (p + 1) * LANES] = rest
        else:
            g[13, 2, :LANES] = rest
    big.tick(tau)
    tau += 1

    def result(rb):
        at = rows_at(rb, BLK)
        swap(2, t2, rb).wait()
        out_ref[at, :] = (t1[at, :] + (t2[at, :] + v[at, :]) + dbias[...][None, :]).astype(BF16)

    each(result)

    x_t[...] = ks[...].T

    def attend_back(step):
        pair, qb = lax.div(step, rbs), lax.rem(step, rbs)
        at = rows_at(qb, BLK)
        cols = rows_at(pair, LANES)
        position = lax.broadcasted_iota(jnp.int32, (1, BLK), 1) + qb * BLK
        seg_row = segment(position)
        same = jnp.concatenate([seg[...]] * (BLK // LANES), axis=1) == seg_row
        dks, dvs = [], []
        for side in range(2):
            lanes = slice(side * HEAD, (side + 1) * HEAD)
            q_now, d_now = qs[at, cols][:, lanes], dctx[at, cols][:, lanes]
            scores = jnp.where(same, mm_t(ks[:, cols][:, lanes], q_now), -1000000000.0)
            e = jnp.exp(scores - jnp.max(scores, axis=0, keepdims=True))
            probs = e * (1.0 / jnp.sum(e, axis=0, keepdims=True))
            grad = mm_t(vs[:, cols][:, lanes], d_now)
            inner = jnp.sum(probs * grad, axis=0, keepdims=True)
            grad = (probs * (grad - inner)).astype(BF16)
            dvs.append(mm(probs.astype(BF16), d_now))
            dks.append(mm(grad, q_now))
            hrows = pl.ds(pl.multiple_of(pair * LANES + side * HEAD, HEAD), HEAD)
            dq_t[hrows, at] = (mm(x_t[hrows, :], grad) * HEAD**-0.5).astype(BF16)
        dk_now, dv_now = jnp.concatenate(dks, axis=1), jnp.concatenate(dvs, axis=1)

        @pl.when(qb == 0)
        def _():
            dk_sum[...] = dk_now
            dv_sum[...] = dv_now

        @pl.when(qb > 0)
        def _():
            dk_sum[...] = dk_sum[...] + dk_now
            dv_sum[...] = dv_sum[...] + dv_now

        @pl.when(qb == rbs - 1)
        def _():
            ks[:, cols] = dk_sum[...].astype(BF16)
            vs[:, cols] = dv_sum[...].astype(BF16)

        @pl.when(lax.rem(step, 3) == 1)
        def _():
            big.tick(tau + lax.div(step, 3))

    steps = rbs * (head_cols // LANES)
    each(attend_back, steps)
    freed()
    tau += steps // 3

    qs[...] = dq_t[...].T
    put_rows(sg, plan["qbias"][0], total(qs[...]))
    put_rows(sg, plan["vbias"][0], total(vs[...]))
    each(first_norm)
    norm_t[...] = norm[...].T
    for i, grads in enumerate((qs, ks, vs)):
        for j in range(PARTS):
            made = mm(norm_t[j * BLK : (j + 1) * BLK, :], grads[...])
            g[(14 + i) % HELD, j] = made[:, :BLK]
            if i * 3 + j < 8:
                c, p, side = leftover(i * 3 + j)
                g[c % HELD, p, :, side * LANES : (side + 1) * LANES] = made[:, BLK:]
            else:
                g[13, 2, LANES:, :LANES] = made[:LANES, BLK:]
                g[13, 2, LANES:, LANES:] = made[LANES:, BLK:]
    big.tick(tau)
    tau += 1

    pl.semaphore_wait(vfree, 1)

    def to_norm(rb):
        at = rows_at(rb, BLK)
        t2[at, :] = mm_t(qs[at, :], qkvw[0]) + mm_t(ks[at, :], qkvw[1]) + mm_t(vs[at, :], qkvw[2])
        swap(3, t2, rb).start()

    each(to_norm)

    def first_norm_back(rb):
        at = rows_at(rb, BLK)
        swap(3, t2, rb).wait()
        grad = t2[at, :] + v[at, :]
        x_hat, scale = normalise(tok[at, :].astype(F32))
        add_rows(sg, plan["gain1"][0], total(grad * x_hat))
        add_rows(sg, plan["shift1"][0], total(grad))
        ing_ref[at, :] = (t3[at, :] + norm_back(x_hat, scale, grad * gain1[...][None, :])).astype(BF16)

    each(first_norm_back)

    rows = plan["genes"][1]
    local = genes[...][None, :] - core * plan["genes"][2]
    high = lax.shift_right_arithmetic(local, 7)
    low = local - high * LANES
    high = (lax.broadcasted_iota(jnp.int32, (rows, tokens), 0) == high).astype(F32).astype(BF16)
    low = (lax.broadcasted_iota(jnp.int32, (LANES, tokens), 0) == low).astype(F32).astype(BF16)
    sg[0, 0, :rows, :] = mm_t(high, low)

    def finish(i, carry):
        big.tick(tau + i)
        small.tick(i)
        return carry

    left = big.chunks + big.stages - tau
    lax.fori_loop(0, max(left, small.stages + 1), finish, 0)


def run_layer(n_dp, plan, small_rows, *args):
    (lengths, genes, tok, cot, gain1, shift1, qkvw, qvb, outw, obias, gain2, shift2, upw, ubias, dnw, dbias) = args
    tokens, features = tok.shape
    units, head_cols = dnw.shape[0], outw.shape[0]
    chunks = (features * (2 * units + 4 * head_cols)) // (PARTS * BLK * BLK)
    _, _, stages = stage_counts(n_dp)
    vmem = pl.BlockSpec(memory_space=pltpu.VMEM)
    hbm = pl.BlockSpec(memory_space=pl.ANY)
    dma = pltpu.SemaphoreType.DMA
    wide = (tokens, features)
    return pl.pallas_call(
        functools.partial(layer, n_dp, plan),
        out_shape=(
            pltpu.VMEM(wide, BF16),
            pltpu.VMEM(wide, BF16),
            pltpu.VMEM((chunks, PARTS, BLK, BLK), F32),
            pltpu.VMEM((1, 1, small_rows, LANES), F32),
        ),
        in_specs=[hbm] * 16,
        out_specs=(vmem, vmem, vmem, vmem),
        scratch_shapes=[
            pltpu.VMEM(wide, BF16),
            pltpu.VMEM(wide, BF16),
            pltpu.VMEM(qkvw.shape, BF16),
            pltpu.VMEM(outw.shape, BF16),
            pltpu.VMEM(upw.shape, BF16),
            pltpu.VMEM(dnw.shape, BF16),
            pltpu.VMEM((features, tokens), BF16),
            pltpu.VMEM((tokens, head_cols), BF16),
            pltpu.VMEM((tokens, head_cols), BF16),
            pltpu.VMEM((tokens, head_cols), BF16),
            pltpu.VMEM((tokens, head_cols), BF16),
            pltpu.VMEM(wide, F32),
            pltpu.VMEM(wide, F32),
            pltpu.VMEM(wide, F32),
            pltpu.VMEM(wide, F32),
            pltpu.VMEM((HELD, PARTS, BLK, BLK), F32),
            pltpu.VMEM((SLOTS, PARTS, slot_rows(n_dp, BLK), BLK), F32),
            pltpu.VMEM((BLK, tokens), BF16),
            pltpu.VMEM((tokens, LANES), jnp.int32),
            pltpu.VMEM((1, 1, small_rows, LANES), F32),
            pltpu.VMEM((1, 1, slot_rows(n_dp, small_rows), LANES), F32),
            dma((16,)),
            dma((4, tokens // BLK)),
            dma((4, tokens // BLK)),
            dma((2, PARTS, stages)),
            dma((SLOTS, PARTS, stages)),
            dma((2, PARTS)),
            dma((1, 1, stages)),
            dma((1, 1, stages)),
            dma((1, 1)),
            pltpu.SemaphoreType.REGULAR,
            pltpu.SMEM(lengths.shape, jnp.int32),
            pltpu.VMEM(genes.shape, jnp.int32),
            *(pltpu.VMEM(x.shape, F32) for x in (gain1, shift1, qvb, obias, gain2, shift2, ubias, dbias)),
        ],
        compiler_params=pltpu.CompilerParams(
            collective_id=0, has_side_effects=True, vmem_limit_bytes=47 << 20
        ),
    )(*args)


def hand_out(plan, packed, sums, out_ref, ing_ref, *refs):
    (output, input_grad, gain1, shift1, qkv, qv, out, obias, gain2, shift2, up, ubias, down, dbias, genes) = refs[:15]
    sem = refs[15]
    moves = [(out_ref, output), (ing_ref, input_grad)]
    for u in range(down.shape[0] // BLK):
        for p in range(PARTS):
            units, cols = pl.ds(u * BLK, BLK), pl.ds(p * BLK, BLK)
            moves.append((packed.at[2 * u, p], down.at[units, cols]))
            moves.append((packed.at[2 * u + 1, p], up.at[cols, units]))
    half = pl.ds(0, LANES), pl.ds(LANES, LANES)
    for p in range(PARTS):
        cols = pl.ds(p * BLK, BLK)
        moves.append((packed.at[12, p], out.at[pl.ds(0, BLK), cols]))
        rest = packed.at[13, 1 + p // 2, half[p % 2]]
        moves.append((rest, out.at[pl.ds(BLK, LANES), cols]))
    for i in range(3):
        for j in range(PARTS):
            rows, tail = pl.ds(j * BLK, BLK), pl.ds(BLK, LANES)
            moves.append((packed.at[14 + i, j], qkv.at[i, rows, pl.ds(0, BLK)]))
            if i * 3 + j < 8:
                c, p, side = leftover(i * 3 + j)
                moves.append((packed.at[c, p, pl.ds(0, BLK), half[side]], qkv.at[i, rows, tail]))
            else:
                for side in range(2):
                    rows = pl.ds(j * BLK + side * LANES, LANES)
                    moves.append((packed.at[13, 2, half[1], half[side]], qkv.at[i, rows, tail]))
    copies = [pltpu.make_async_copy(src, dst, sem.at[i]) for i, (src, dst) in enumerate(moves)]
    for copy in copies:
        copy.start()

    def vector(name, ref, *index):
        at, count, _ = plan[name]
        for i in range(count):
            ref[(*index, pl.ds(i * LANES, LANES))] = sums[0, 0, at + i]

    for name, ref in (
        ("gain1", gain1),
        ("shift1", shift1),
        ("obias", obias),
        ("gain2", gain2),
        ("shift2", shift2),
        ("ubias", ubias),
        ("dbias", dbias),
    ):
        vector(name, ref)
    vector("qbias", qv, 0)
    vector("vbias", qv, 1)
    size = plan["genes"][2]
    for i in range(-(-size // LANES)):
        part = min(LANES, size - i * LANES)
        genes[pl.ds(i * LANES, part)] = sums[0, 0, i, :part].astype(jnp.int32)
    for copy in copies:
        copy.wait()


def results(plan, features, head_cols, units, packed, sums, output, input_grad):
    vmem = pl.BlockSpec(memory_space=pltpu.VMEM)
    hbm = pl.BlockSpec(memory_space=pl.ANY)
    size = lambda name: (plan[name][2],)
    shapes = (
        output.shape,
        input_grad.shape,
        size("gain1"),
        size("shift1"),
        (3, features, head_cols),
        (2, head_cols),
        (head_cols, features),
        size("obias"),
        size("gain2"),
        size("shift2"),
        (features, units),
        size("ubias"),
        (units, features),
        size("dbias"),
        size("genes"),
    )
    types = [BF16, BF16] + [F32] * 12 + [jnp.int32]
    large = (0, 1, 4, 6, 10, 12)
    return pl.pallas_call(
        functools.partial(hand_out, plan),
        out_shape=tuple(jax.ShapeDtypeStruct(shape, kind) for shape, kind in zip(shapes, types)),
        in_specs=[vmem, vmem, vmem, vmem],
        out_specs=tuple(hbm if i in large else vmem for i in range(15)),
        scratch_shapes=[
            pltpu.SemaphoreType.DMA((63,)),
        ],
        compiler_params=pltpu.CompilerParams(vmem_limit_bytes=16 << 20),
    )(packed, sums, output, input_grad)


def on_device(
    n_dp,
    tokens,
    lengths,
    gene_ids,
    norm1_gain,
    norm1_shift,
    qkv_weight,
    qv_bias,
    out_weight,
    out_bias,
    norm2_gain,
    norm2_shift,
    up_weight,
    up_bias,
    down_weight,
    down_bias,
    cotangent,
):
    features = tokens.shape[1]
    head_cols, units = out_weight.shape[0], down_weight.shape[0]
    plan, small_rows = small_plan(features, head_cols, units, VOCAB // lax.axis_size("tensor"))
    output, input_grad, packed, sums = run_layer(
        n_dp,
        plan,
        small_rows,
        lengths,
        gene_ids,
        tokens,
        cotangent,
        norm1_gain,
        norm1_shift,
        qkv_weight.transpose(1, 0, 2),
        qv_bias,
        out_weight,
        out_bias,
        norm2_gain,
        norm2_shift,
        up_weight,
        up_bias,
        down_weight,
        down_bias,
    )
    made = list(results(plan, features, head_cols, units, packed, sums, output, input_grad))
    made[4] = made[4].transpose(1, 0, 2)
    return tuple(made)


def solution(mesh):
    return jax.shard_map(
        functools.partial(on_device, mesh.shape["dp"]),
        mesh=mesh,
        in_specs=(
            P("dp", None),
            P("dp", None),
            P("dp"),
            P(),
            P(),
            P(None, None, "tensor"),
            P(None, "tensor"),
            P("tensor", None),
            P(),
            P(),
            P(),
            P(None, "tensor"),
            P("tensor"),
            P("tensor", None),
            P(),
            P("dp", None),
        ),
        out_specs=(
            P("dp", None),
            P("dp", None),
            P(),
            P(),
            P(None, None, "tensor"),
            P(None, "tensor"),
            P("tensor", None),
            P(),
            P(),
            P(),
            P(None, "tensor"),
            P("tensor"),
            P("tensor", None),
            P(),
            P("tensor"),
        ),
        check_vma=False,
    )
```

```python
import functools

import jax
import jax.numpy as jnp
from jax import lax
from jax.experimental import pallas as pl
from jax.experimental.pallas import tpu as pltpu
from jax.sharding import PartitionSpec as P

HEAD = 64
VOCAB = 36000
MESH = pl.DeviceIdType.MESH
F32, BF16 = jnp.float32, jnp.bfloat16
BLK = 256
PARTS = 3
SLOTS = 4
HELD = 14
LANES = 128


def mm(left, right):
    return jnp.dot(left, right, preferred_element_type=F32)


def mm_t(left, right):
    return lax.dot_general(left, right, (((1,), (1,)), ((), ())), preferred_element_type=F32)


def bit_of(index, mask):
    return lax.rem(lax.div(index, mask), 2)


def rows_at(index, size):
    return pl.ds(pl.multiple_of(index * size, size), size)


class Exchange:
    def __init__(self, n_dp, chunks, parts, slots, g, r, o, ssem, rsem, osem):
        self.chunks, self.parts, self.slots = chunks, parts, slots
        self.g, self.r, self.o = g, r, o
        self.ssem, self.rsem, self.osem = ssem, rsem, osem
        self.rows = g.shape[2]
        self.bits, self.half, self.stages = stage_counts(n_dp)
        self.dp, self.core = lax.axis_index("dp"), lax.axis_index("tensor")

    def mask(self, c, p, k):
        if k >= 3 or self.bits < 3 or p == 0:
            return 1 << k
        if p == 1:
            return 1 << (1, 0, 2)[k]
        if k == 0:
            return 4
        odd = lax.rem(c, 2)
        return 1 + odd if k == 1 else 2 - odd

    def first(self, c, p, depth):
        at = 0
        for k in range(depth):
            at = at + bit_of(self.dp, self.mask(c, p, k)) * (self.rows >> (k + 1))
        return at

    def held(self, c):
        return lax.rem(c, self.g.shape[0])

    def slot(self, s):
        if s < self.half:
            return pl.ds(self.rows - (self.rows >> s), self.rows >> (s + 1))
        size = self.rows >> self.half
        return pl.ds(self.rows - size + (s - self.half) * size, size)

    def own(self, c, p, depth):
        return pl.ds(pl.multiple_of(self.first(c, p, depth), 8), self.rows >> depth)

    def copy(self, c, p, s):
        flat_end = self.stages - self.half
        k = s if s < flat_end else self.stages - 1 - s
        mask = self.mask(c, p, k)
        bit = bit_of(self.dp, mask)
        if s < self.half:
            size = self.rows >> (s + 1)
            away = pl.ds(pl.multiple_of(self.first(c, p, s) + (1 - bit) * size, 8), size)
            src = self.g.at[self.held(c), p, away]
        elif s < flat_end:
            src = self.g.at[self.held(c), p, self.own(c, p, self.half)]
        if s < flat_end:
            dst = self.r.at[lax.rem(c, self.slots), p, self.slot(s)]
        else:
            mine = self.own(c, p, k + 1)
            dst = self.o.at[c, p, mine]
            src = self.g.at[self.held(c), p, mine] if s == flat_end else dst
        return pltpu.make_async_remote_copy(
            src,
            dst,
            self.ssem.at[lax.rem(c, self.ssem.shape[0]), p, s],
            self.rsem.at[lax.rem(c, self.slots), p, s],
            device_id=(self.dp + mask * (1 - 2 * bit), self.core),
            device_id_type=MESH,
        )

    def keep(self, c, p):
        mine = self.own(c, p, self.half)
        return pltpu.make_async_copy(self.g.at[self.held(c), p, mine], self.o.at[c, p, mine], self.osem.at[lax.rem(c, self.osem.shape[0]), p])

    def tick(self, tau):
        flat_end = self.stages - self.half
        for s in range(self.stages + 1):
            c = tau - s

            @pl.when((c >= 0) & (c < self.chunks))
            def _():
                for p in range(self.parts):
                    if s > 0:
                        self.copy(c, p, s - 1).wait()
                    if 0 < s <= flat_end:
                        mine = self.own(c, p, min(s, self.half))
                        got = self.r[lax.rem(c, self.slots), p, self.slot(s - 1)]
                        at = self.held(c)
                        self.g[at, p, mine] = self.g[at, p, mine] + got
                    if s == flat_end:
                        self.keep(c, p).start()
                    if s == flat_end + 1:
                        self.keep(c, p).wait()
                    if s < self.stages:
                        self.copy(c, p, s).start()


def stage_counts(n_dp):
    bits = n_dp.bit_length() - 1
    half = min(bits, 4)
    return bits, half, bits + half


def slot_rows(n_dp, rows):
    bits, half, _ = stage_counts(n_dp)
    return rows - (rows >> half) + (bits - half) * (rows >> half)


def normalise(x):
    c = x - jnp.mean(x, axis=-1, keepdims=True)
    scale = lax.rsqrt(jnp.mean(c * c, axis=-1, keepdims=True) + 1e-05)
    return c * scale, scale


def norm_back(x_hat, scale, grad):
    middle = jnp.mean(grad, axis=-1, keepdims=True)
    along = jnp.mean(grad * x_hat, axis=-1, keepdims=True)
    return (grad - middle - x_hat * along) * scale


def total(x):
    return jnp.sum(x.astype(F32), axis=0, keepdims=True)


def put_rows(ref, row, vector):
    for i in range(vector.shape[1] // LANES):
        ref[0, 0, row + i : row + i + 1, :] = vector[:, i * LANES : (i + 1) * LANES]


def add_rows(ref, row, vector):
    for i in range(vector.shape[1] // LANES):
        at = slice(row + i, row + i + 1)
        ref[0, 0, at, :] = ref[0, 0, at, :] + vector[:, i * LANES : (i + 1) * LANES]


def small_plan(features, head_cols, units, vocab_local):
    plan, at = {}, 0
    for name, size in (
        ("genes", vocab_local),
        ("gain1", features),
        ("shift1", features),
        ("qbias", head_cols),
        ("vbias", head_cols),
        ("obias", features),
        ("gain2", features),
        ("shift2", features),
        ("ubias", units),
        ("dbias", features),
    ):
        count = -(-size // LANES)
        if name == "genes":
            count = -(-count // 8) * 8
        plan[name] = (at, count, size)
        at += count
    return plan, -(-at // 128) * 128


def leftover(j):
    block = 9 + j // 2
    return (17, 13)[block // 3 - 3], block % 3, j % 2


def layer(
    n_dp,
    plan,
    lengths_h,
    genes_h,
    tok_h,
    cot_h,
    gain1_h,
    shift1_h,
    qkvw_h,
    qvb_h,
    outw_h,
    obias_h,
    gain2_h,
    shift2_h,
    upw_h,
    ubias_h,
    dnw_h,
    dbias_h,
    out_ref,
    ing_ref,
    o,
    o_small,
    tok,
    cot,
    qkvw,
    outw,
    upw,
    dnw,
    norm_t,
    qs,
    ks,
    vs,
    ctx,
    t1,
    t2,
    t3,
    v,
    g,
    r,
    act_t,
    seg,
    sg,
    sr,
    lsem,
    esend,
    erecv,
    ssem,
    rsem,
    osem,
    sssem,
    srsem,
    sosem,
    vfree,
    lengths,
    genes,
    gain1,
    shift1,
    qvb,
    obias,
    gain2,
    shift2,
    ubias,
    dbias,
):
    tokens, features = tok.shape
    head_cols = qs.shape[1]
    units = dnw.shape[0]
    rbs = tokens // BLK
    dq_t, x_t = norm_t.at[:head_cols], norm_t.at[head_cols : 2 * head_cols]
    dctx, norm = ctx, ing_ref
    act, gu = out_ref.at[:, :BLK], out_ref.at[:, BLK : 2 * BLK]
    slope, dk_sum, dv_sum = v.at[:, :BLK], v.at[:, :LANES], v.at[:, LANES:BLK]
    dp, core = lax.axis_index("dp"), lax.axis_index("tensor")
    other = (dp, 1 - core)

    loads = [
        pltpu.make_async_copy(src, dst, lsem.at[i])
        for i, (src, dst) in enumerate(
            (
                (tok_h, tok),
                (lengths_h, lengths),
                (gain1_h, gain1),
                (shift1_h, shift1),
                (qkvw_h, qkvw),
                (qvb_h, qvb),
                (outw_h, outw),
                (obias_h, obias),
                (gain2_h, gain2),
                (shift2_h, shift2),
                (upw_h, upw),
                (ubias_h, ubias),
                (cot_h, cot),
                (dnw_h, dnw),
                (dbias_h, dbias),
                (genes_h, genes),
            )
        )
    ]
    for load in loads:
        load.start()

    bar = pltpu.get_barrier_semaphore()
    bits = n_dp.bit_length() - 1
    for k in range(bits):
        bit = bit_of(dp, 1 << k)
        to = (dp + (1 << k) * (1 - 2 * bit), core)
        pl.semaphore_signal(bar, inc=1, device_id=to, device_id_type=MESH)
    pl.semaphore_signal(bar, inc=1, device_id=other, device_id_type=MESH)

    big = Exchange(n_dp, o.shape[0], PARTS, SLOTS, g, r, o, ssem, rsem, osem)
    small = Exchange(n_dp, 1, 1, 1, sg, sr, o_small, sssem, srsem, sosem)

    def swap(e, src, rb):
        at = rows_at(rb, BLK)
        return pltpu.make_async_remote_copy(
            src.at[at], v.at[at], esend.at[e, rb], erecv.at[e, rb], device_id=other, device_id_type=MESH
        )

    def freed():
        pl.semaphore_signal(vfree, inc=1, device_id=other, device_id_type=MESH)

    def each(body, count=rbs):
        def step(i, carry):
            body(i)
            return carry

        lax.fori_loop(0, count, step, 0)

    def segment(position):
        ends, seg_now = 0, jnp.zeros(position.shape, jnp.int32)
        for i in range(lengths.shape[1]):
            ends = ends + lengths[0, i]
            seg_now = seg_now + (position >= ends).astype(jnp.int32)
        return seg_now

    loads[1].wait()
    seg[...] = segment(lax.broadcasted_iota(jnp.int32, (tokens, LANES), 0))
    sg[...] = jnp.zeros_like(sg)

    for i in (0, 2, 3):
        loads[i].wait()

    def first_norm(rb):
        at = rows_at(rb, BLK)
        x_hat, _ = normalise(tok[at, :].astype(F32))
        norm[at, :] = (x_hat * gain1[...][None, :] + shift1[...][None, :]).astype(BF16)

    each(first_norm)
    for load in loads[4:6]:
        load.wait()

    def project(rb):
        at = rows_at(rb, BLK)
        x = norm[at, :]
        qs[at, :] = (mm(x, qkvw[0]) + qvb[0:1, :]).astype(BF16) * BF16(HEAD**-0.5)
        ks[at, :] = mm(x, qkvw[1]).astype(BF16)
        vs[at, :] = (mm(x, qkvw[2]) + qvb[1:2, :]).astype(BF16)

    each(project)
    loads[6].wait()
    pl.semaphore_wait(bar, bits + 1)

    def attend(rb):
        at = rows_at(rb, BLK)
        seg_row = segment(lax.broadcasted_iota(jnp.int32, (1, tokens), 1))
        same = jnp.concatenate([seg[at, :]] * (tokens // LANES), axis=1) == seg_row
        heads = head_cols // HEAD

        def scores_of(h):
            cols = slice(h * HEAD, (h + 1) * HEAD)
            return jnp.where(same, mm_t(qs[at, cols], ks[:, cols]), -1000000000.0)

        ready, sides = scores_of(0), []
        for h in range(heads):
            scores = ready
            if h + 1 < heads:
                ready = scores_of(h + 1)
            e = jnp.exp(scores - jnp.max(scores, axis=-1, keepdims=True))
            inverse = 1.0 / jnp.sum(e, axis=-1, keepdims=True)
            sides.append(mm(e.astype(BF16), vs[:, h * HEAD : (h + 1) * HEAD]) * inverse)
            if h % 2:
                ctx[at, (h - 1) * HEAD : (h + 1) * HEAD] = jnp.concatenate(sides, axis=1).astype(BF16)
                sides = []
        t1[at, :] = mm(ctx[at, :], outw[...])
        swap(0, t1, rb).start()

    each(attend)
    for load in loads[7:]:
        load.wait()

    def second_norm(rb):
        at = rows_at(rb, BLK)
        swap(0, t1, rb).wait()
        hidden = tok[at, :].astype(F32) + (t1[at, :] + v[at, :]) + obias[...][None, :]
        t1[at, :] = hidden
        x_hat, _ = normalise(hidden)
        norm[at, :] = (x_hat * gain2[...][None, :] + shift2[...][None, :]).astype(BF16)
        t2[at, :] = jnp.zeros((BLK, features), F32)
        t3[at, :] = jnp.zeros((BLK, features), F32)

    each(second_norm)

    def feed_forward(u):
        ucols = rows_at(u, BLK)

        def upper(rb):
            at = rows_at(rb, BLK)
            up = mm(norm[at, :], upw[:, ucols]) + ubias[ucols][None, :]
            cdf = 0.5 * (1.0 + lax.erf(up * 0.7071067811865476))
            act[at, :] = (up * cdf).astype(BF16)
            slope[at, :] = cdf + up * (jnp.exp(-0.5 * up * up) * 0.3989422804014327)

        each(upper)
        act_t[...] = act[...].T
        for p in range(PARTS):
            g[2 * u, p] = mm(act_t[...], cot[:, p * BLK : (p + 1) * BLK])
        big.tick(u + jnp.minimum(u, 1))

        @pl.when(u == 0)
        def _():
            norm_t[...] = norm[...].T

        def lower(rb, sums):
            at = rows_at(rb, BLK)
            down_rows = dnw[ucols, :]
            grad = (mm_t(cot[at, :], down_rows) * slope[at, :]).astype(BF16)
            gu[at, :] = grad
            t2[at, :] = t2[at, :] + mm(act[at, :], down_rows)
            t3[at, :] = t3[at, :] + mm_t(grad, upw[:, ucols])
            return sums + total(grad)

        sums = lax.fori_loop(0, rbs, lower, jnp.zeros((1, BLK), F32))
        row = plan["ubias"][0] + u * (BLK // LANES)
        for i in range(BLK // LANES):
            sg[0, 0, pl.ds(row + i, 1), :] = sums[:, i * LANES : (i + 1) * LANES]
        for p in range(PARTS):
            g[2 * u + 1, p] = mm(norm_t[p * BLK : (p + 1) * BLK, :], gu[...])

        @pl.when(u == 0)
        def _():
            big.tick(1)

    each(feed_forward, units // BLK)
    freed()
    tau = units // BLK + 1

    pl.semaphore_wait(vfree, 1)
    each(lambda rb: swap(1, t3, rb).start())
    big.tick(tau)
    tau += 1

    x_t[...] = ctx[...].T

    def second_norm_back(rb):
        at = rows_at(rb, BLK)
        swap(1, t3, rb).wait()
        grad = t3[at, :] + v[at, :]
        x_hat, scale = normalise(t1[at, :])
        add_rows(sg, plan["gain2"][0], total(grad * x_hat))
        add_rows(sg, plan["shift2"][0], total(grad))
        given = cot[at, :].astype(F32)
        add_rows(sg, plan["dbias"][0], total(given))
        grad = given + norm_back(x_hat, scale, grad * gain2[...][None, :])
        t3[at, :] = grad
        norm[at, :] = grad.astype(BF16)
        add_rows(sg, plan["obias"][0], total(norm[at, :]))
        dctx[at, :] = mm_t(norm[at, :], outw[...]).astype(BF16)

    each(second_norm_back)
    freed()
    pl.semaphore_wait(vfree, 1)
    each(lambda rb: swap(2, t2, rb).start())

    for p in range(PARTS):
        branch = norm[:, p * BLK : (p + 1) * BLK]
        g[12, p] = mm(x_t[:BLK, :], branch)
        rest = mm(x_t[BLK:, :], branch)
        if p < 2:
            g[13, 1, p * LANES : (p + 1) * LANES] = rest
        else:
            g[13, 2, :LANES] = rest
    big.tick(tau)
    tau += 1

    def result(rb):
        at = rows_at(rb, BLK)
        swap(2, t2, rb).wait()
        out_ref[at, :] = (t1[at, :] + (t2[at, :] + v[at, :]) + dbias[...][None, :]).astype(BF16)

    each(result)

    x_t[...] = ks[...].T

    def attend_back(step):
        pair, qb = lax.div(step, rbs), lax.rem(step, rbs)
        at = rows_at(qb, BLK)
        cols = rows_at(pair, LANES)
        position = lax.broadcasted_iota(jnp.int32, (1, BLK), 1) + qb * BLK
        seg_row = segment(position)
        same = jnp.concatenate([seg[...]] * (BLK // LANES), axis=1) == seg_row
        dks, dvs = [], []
        for side in range(2):
            lanes = slice(side * HEAD, (side + 1) * HEAD)
            q_now, d_now = qs[at, cols][:, lanes], dctx[at, cols][:, lanes]
            scores = jnp.where(same, mm_t(ks[:, cols][:, lanes], q_now), -1000000000.0)
            e = jnp.exp(scores - jnp.max(scores, axis=0, keepdims=True))
            probs = e * (1.0 / jnp.sum(e, axis=0, keepdims=True))
            grad = mm_t(vs[:, cols][:, lanes], d_now)
            inner = jnp.sum(probs * grad, axis=0, keepdims=True)
            grad = (probs * (grad - inner)).astype(BF16)
            dvs.append(mm(probs.astype(BF16), d_now))
            dks.append(mm(grad, q_now))
            hrows = pl.ds(pl.multiple_of(pair * LANES + side * HEAD, HEAD), HEAD)
            dq_t[hrows, at] = (mm(x_t[hrows, :], grad) * HEAD**-0.5).astype(BF16)
        dk_now, dv_now = jnp.concatenate(dks, axis=1), jnp.concatenate(dvs, axis=1)

        @pl.when(qb == 0)
        def _():
            dk_sum[...] = dk_now
            dv_sum[...] = dv_now

        @pl.when(qb > 0)
        def _():
            dk_sum[...] = dk_sum[...] + dk_now
            dv_sum[...] = dv_sum[...] + dv_now

        @pl.when(qb == rbs - 1)
        def _():
            ks[:, cols] = dk_sum[...].astype(BF16)
            vs[:, cols] = dv_sum[...].astype(BF16)

        @pl.when(lax.rem(step, 3) == 1)
        def _():
            big.tick(tau + lax.div(step, 3))

    steps = rbs * (head_cols // LANES)
    each(attend_back, steps)
    freed()
    tau += steps // 3

    qs[...] = dq_t[...].T
    put_rows(sg, plan["qbias"][0], total(qs[...]))
    put_rows(sg, plan["vbias"][0], total(vs[...]))
    each(first_norm)
    norm_t[...] = norm[...].T
    for i, grads in enumerate((qs, ks, vs)):
        for j in range(PARTS):
            made = mm(norm_t[j * BLK : (j + 1) * BLK, :], grads[...])
            g[(14 + i) % HELD, j] = made[:, :BLK]
            if i * 3 + j < 8:
                c, p, side = leftover(i * 3 + j)
                g[c % HELD, p, :, side * LANES : (side + 1) * LANES] = made[:, BLK:]
            else:
                g[13, 2, LANES:, :LANES] = made[:LANES, BLK:]
                g[13, 2, LANES:, LANES:] = made[LANES:, BLK:]
    big.tick(tau)
    tau += 1

    pl.semaphore_wait(vfree, 1)

    def to_norm(rb):
        at = rows_at(rb, BLK)
        t2[at, :] = mm_t(qs[at, :], qkvw[0]) + mm_t(ks[at, :], qkvw[1]) + mm_t(vs[at, :], qkvw[2])
        swap(3, t2, rb).start()

    each(to_norm)

    def first_norm_back(rb):
        at = rows_at(rb, BLK)
        swap(3, t2, rb).wait()
        grad = t2[at, :] + v[at, :]
        x_hat, scale = normalise(tok[at, :].astype(F32))
        add_rows(sg, plan["gain1"][0], total(grad * x_hat))
        add_rows(sg, plan["shift1"][0], total(grad))
        ing_ref[at, :] = (t3[at, :] + norm_back(x_hat, scale, grad * gain1[...][None, :])).astype(BF16)

    each(first_norm_back)

    rows = plan["genes"][1]
    local = genes[...][None, :] - core * plan["genes"][2]
    high = lax.shift_right_arithmetic(local, 7)
    low = local - high * LANES
    high = (lax.broadcasted_iota(jnp.int32, (rows, tokens), 0) == high).astype(F32).astype(BF16)
    low = (lax.broadcasted_iota(jnp.int32, (LANES, tokens), 0) == low).astype(F32).astype(BF16)
    sg[0, 0, :rows, :] = mm_t(high, low)

    def finish(i, carry):
        big.tick(tau + i)
        small.tick(i)
        return carry

    left = big.chunks + big.stages - tau
    lax.fori_loop(0, max(left, small.stages + 1), finish, 0)


def run_layer(n_dp, plan, small_rows, *args):
    (lengths, genes, tok, cot, gain1, shift1, qkvw, qvb, outw, obias, gain2, shift2, upw, ubias, dnw, dbias) = args
    tokens, features = tok.shape
    units, head_cols = dnw.shape[0], outw.shape[0]
    chunks = (features * (2 * units + 4 * head_cols)) // (PARTS * BLK * BLK)
    _, _, stages = stage_counts(n_dp)
    vmem = pl.BlockSpec(memory_space=pltpu.VMEM)
    hbm = pl.BlockSpec(memory_space=pl.ANY)
    dma = pltpu.SemaphoreType.DMA
    wide = (tokens, features)
    return pl.pallas_call(
        functools.partial(layer, n_dp, plan),
        out_shape=(
            pltpu.VMEM(wide, BF16),
            pltpu.VMEM(wide, BF16),
            pltpu.VMEM((chunks, PARTS, BLK, BLK), F32),
            pltpu.VMEM((1, 1, small_rows, LANES), F32),
        ),
        in_specs=[hbm] * 16,
        out_specs=(vmem, vmem, vmem, vmem),
        scratch_shapes=[
            pltpu.VMEM(wide, BF16),
            pltpu.VMEM(wide, BF16),
            pltpu.VMEM(qkvw.shape, BF16),
            pltpu.VMEM(outw.shape, BF16),
            pltpu.VMEM(upw.shape, BF16),
            pltpu.VMEM(dnw.shape, BF16),
            pltpu.VMEM((features, tokens), BF16),
            pltpu.VMEM((tokens, head_cols), BF16),
            pltpu.VMEM((tokens, head_cols), BF16),
            pltpu.VMEM((tokens, head_cols), BF16),
            pltpu.VMEM((tokens, head_cols), BF16),
            pltpu.VMEM(wide, F32),
            pltpu.VMEM(wide, F32),
            pltpu.VMEM(wide, F32),
            pltpu.VMEM(wide, F32),
            pltpu.VMEM((HELD, PARTS, BLK, BLK), F32),
            pltpu.VMEM((SLOTS, PARTS, slot_rows(n_dp, BLK), BLK), F32),
            pltpu.VMEM((BLK, tokens), BF16),
            pltpu.VMEM((tokens, LANES), jnp.int32),
            pltpu.VMEM((1, 1, small_rows, LANES), F32),
            pltpu.VMEM((1, 1, slot_rows(n_dp, small_rows), LANES), F32),
            dma((16,)),
            dma((4, tokens // BLK)),
            dma((4, tokens // BLK)),
            dma((2, PARTS, stages)),
            dma((SLOTS, PARTS, stages)),
            dma((2, PARTS)),
            dma((1, 1, stages)),
            dma((1, 1, stages)),
            dma((1, 1)),
            pltpu.SemaphoreType.REGULAR,
            pltpu.SMEM(lengths.shape, jnp.int32),
            pltpu.VMEM(genes.shape, jnp.int32),
            *(pltpu.VMEM(x.shape, F32) for x in (gain1, shift1, qvb, obias, gain2, shift2, ubias, dbias)),
        ],
        compiler_params=pltpu.CompilerParams(
            collective_id=0, has_side_effects=True, vmem_limit_bytes=47 << 20
        ),
    )(*args)


SMALL = (2, 3, 5, 7, 8, 9, 11, 13, 14)


def hand_out(plan, packed, sums, out_ref, ing_ref, *refs):
    output, input_grad, _, _, qkv, _, out, _, _, _, up, _, down, _, _ = refs[:15]
    sem, *staged = refs[15:]
    gain1, shift1, qv, obias, gain2, shift2, ubias, dbias, genes = staged
    moves = [(out_ref, output), (ing_ref, input_grad)]
    for u in range(down.shape[0] // BLK):
        for p in range(PARTS):
            units, cols = pl.ds(u * BLK, BLK), pl.ds(p * BLK, BLK)
            moves.append((packed.at[2 * u, p], down.at[units, cols]))
            moves.append((packed.at[2 * u + 1, p], up.at[cols, units]))
    half = pl.ds(0, LANES), pl.ds(LANES, LANES)
    for p in range(PARTS):
        cols = pl.ds(p * BLK, BLK)
        moves.append((packed.at[12, p], out.at[pl.ds(0, BLK), cols]))
        rest = packed.at[13, 1 + p // 2, half[p % 2]]
        moves.append((rest, out.at[pl.ds(BLK, LANES), cols]))
    for i in range(3):
        for j in range(PARTS):
            rows, tail = pl.ds(j * BLK, BLK), pl.ds(BLK, LANES)
            moves.append((packed.at[14 + i, j], qkv.at[i, rows, pl.ds(0, BLK)]))
            if i * 3 + j < 8:
                c, p, side = leftover(i * 3 + j)
                moves.append((packed.at[c, p, pl.ds(0, BLK), half[side]], qkv.at[i, rows, tail]))
            else:
                for side in range(2):
                    rows = pl.ds(j * BLK + side * LANES, LANES)
                    moves.append((packed.at[13, 2, half[1], half[side]], qkv.at[i, rows, tail]))
    copies = [pltpu.make_async_copy(src, dst, sem.at[i]) for i, (src, dst) in enumerate(moves)]
    for copy in copies:
        copy.start()

    def vector(name, ref, *index):
        at, count, _ = plan[name]
        for i in range(count):
            ref[(*index, pl.ds(i * LANES, LANES))] = sums[0, 0, at + i]

    for name, ref in (
        ("gain1", gain1),
        ("shift1", shift1),
        ("obias", obias),
        ("gain2", gain2),
        ("shift2", shift2),
        ("ubias", ubias),
        ("dbias", dbias),
    ):
        vector(name, ref)
    vector("qbias", qv, 0)
    vector("vbias", qv, 1)
    size = plan["genes"][2]
    for i in range(-(-size // LANES)):
        part = min(LANES, size - i * LANES)
        genes[pl.ds(i * LANES, part)] = sums[0, 0, i, :part].astype(jnp.int32)
    for src, at in zip(staged, SMALL):
        copies.append(pltpu.make_async_copy(src, refs[at], sem.at[len(copies)]))
        copies[-1].start()
    for copy in copies:
        copy.wait()


def results(plan, features, head_cols, units, packed, sums, output, input_grad):
    vmem = pl.BlockSpec(memory_space=pltpu.VMEM)
    hbm = pl.BlockSpec(memory_space=pl.ANY)
    size = lambda name: (plan[name][2],)
    shapes = (
        output.shape,
        input_grad.shape,
        size("gain1"),
        size("shift1"),
        (3, features, head_cols),
        (2, head_cols),
        (head_cols, features),
        size("obias"),
        size("gain2"),
        size("shift2"),
        (features, units),
        size("ubias"),
        (units, features),
        size("dbias"),
        size("genes"),
    )
    types = [BF16, BF16] + [F32] * 12 + [jnp.int32]
    return pl.pallas_call(
        functools.partial(hand_out, plan),
        out_shape=tuple(jax.ShapeDtypeStruct(shape, kind) for shape, kind in zip(shapes, types)),
        in_specs=[vmem, vmem, vmem, vmem],
        out_specs=(hbm,) * 15,
        scratch_shapes=[
            pltpu.SemaphoreType.DMA((72,)),
            *(pltpu.VMEM(shapes[i], types[i]) for i in SMALL),
        ],
        compiler_params=pltpu.CompilerParams(vmem_limit_bytes=16 << 20),
    )(packed, sums, output, input_grad)


def on_device(
    n_dp,
    tokens,
    lengths,
    gene_ids,
    norm1_gain,
    norm1_shift,
    qkv_weight,
    qv_bias,
    out_weight,
    out_bias,
    norm2_gain,
    norm2_shift,
    up_weight,
    up_bias,
    down_weight,
    down_bias,
    cotangent,
):
    features = tokens.shape[1]
    head_cols, units = out_weight.shape[0], down_weight.shape[0]
    plan, small_rows = small_plan(features, head_cols, units, VOCAB // lax.axis_size("tensor"))
    output, input_grad, packed, sums = run_layer(
        n_dp,
        plan,
        small_rows,
        lengths,
        gene_ids,
        tokens,
        cotangent,
        norm1_gain,
        norm1_shift,
        qkv_weight.transpose(1, 0, 2),
        qv_bias,
        out_weight,
        out_bias,
        norm2_gain,
        norm2_shift,
        up_weight,
        up_bias,
        down_weight,
        down_bias,
    )
    made = list(results(plan, features, head_cols, units, packed, sums, output, input_grad))
    made[4] = made[4].transpose(1, 0, 2)
    return tuple(made)


def solution(mesh):
    return jax.shard_map(
        functools.partial(on_device, mesh.shape["dp"]),
        mesh=mesh,
        in_specs=(
            P("dp", None),
            P("dp", None),
            P("dp"),
            P(),
            P(),
            P(None, None, "tensor"),
            P(None, "tensor"),
            P("tensor", None),
            P(),
            P(),
            P(),
            P(None, "tensor"),
            P("tensor"),
            P("tensor", None),
            P(),
            P("dp", None),
        ),
        out_specs=(
            P("dp", None),
            P("dp", None),
            P(),
            P(),
            P(None, None, "tensor"),
            P(None, "tensor"),
            P("tensor", None),
            P(),
            P(),
            P(),
            P(None, "tensor"),
            P("tensor"),
            P("tensor", None),
            P(),
            P("tensor"),
        ),
        check_vma=False,
    )
```

```python
import functools

import jax
import jax.numpy as jnp
from jax import lax
from jax.experimental import pallas as pl
from jax.experimental.pallas import tpu as pltpu
from jax.sharding import PartitionSpec as P

HEAD = 64
VOCAB = 36000
MESH = pl.DeviceIdType.MESH
F32, BF16 = jnp.float32, jnp.bfloat16
BLK = 256
PARTS = 3
SLOTS = 4
HELD = 14
LANES = 128


def mm(left, right):
    return jnp.dot(left, right, preferred_element_type=F32)


def mm_t(left, right):
    return lax.dot_general(left, right, (((1,), (1,)), ((), ())), preferred_element_type=F32)


def bit_of(index, mask):
    return lax.rem(lax.div(index, mask), 2)


def rows_at(index, size):
    return pl.ds(pl.multiple_of(index * size, size), size)


class Exchange:
    def __init__(self, n_dp, chunks, parts, slots, g, r, o, ssem, rsem, osem):
        self.chunks, self.parts, self.slots = chunks, parts, slots
        self.g, self.r, self.o = g, r, o
        self.ssem, self.rsem, self.osem = ssem, rsem, osem
        self.rows = g.shape[2]
        self.bits, self.half, self.stages = stage_counts(n_dp)
        self.dp, self.core = lax.axis_index("dp"), lax.axis_index("tensor")

    def mask(self, c, p, k):
        if k >= 3 or self.bits < 3 or p == 0:
            return 1 << k
        if p == 1:
            return 1 << (1, 0, 2)[k]
        if k == 0:
            return 4
        odd = lax.rem(c, 2)
        return 1 + odd if k == 1 else 2 - odd

    def first(self, c, p, depth):
        at = 0
        for k in range(depth):
            at = at + bit_of(self.dp, self.mask(c, p, k)) * (self.rows >> (k + 1))
        return at

    def held(self, c):
        return lax.rem(c, self.g.shape[0])

    def slot(self, s):
        if s < self.half:
            return pl.ds(self.rows - (self.rows >> s), self.rows >> (s + 1))
        size = self.rows >> self.half
        return pl.ds(self.rows - size + (s - self.half) * size, size)

    def own(self, c, p, depth):
        return pl.ds(pl.multiple_of(self.first(c, p, depth), 8), self.rows >> depth)

    def copy(self, c, p, s):
        flat_end = self.stages - self.half
        k = s if s < flat_end else self.stages - 1 - s
        mask = self.mask(c, p, k)
        bit = bit_of(self.dp, mask)
        if s < self.half:
            size = self.rows >> (s + 1)
            away = pl.ds(pl.multiple_of(self.first(c, p, s) + (1 - bit) * size, 8), size)
            src = self.g.at[self.held(c), p, away]
        elif s < flat_end:
            src = self.g.at[self.held(c), p, self.own(c, p, self.half)]
        if s < flat_end:
            dst = self.r.at[lax.rem(c, self.slots), p, self.slot(s)]
        else:
            mine = self.own(c, p, k + 1)
            dst = self.o.at[c, p, mine]
            src = self.g.at[self.held(c), p, mine] if s == flat_end else dst
        return pltpu.make_async_remote_copy(
            src,
            dst,
            self.ssem.at[lax.rem(c, self.ssem.shape[0]), p, s],
            self.rsem.at[lax.rem(c, self.slots), p, s],
            device_id=(self.dp + mask * (1 - 2 * bit), self.core),
            device_id_type=MESH,
        )

    def keep(self, c, p):
        mine = self.own(c, p, self.half)
        return pltpu.make_async_copy(self.g.at[self.held(c), p, mine], self.o.at[c, p, mine], self.osem.at[lax.rem(c, self.osem.shape[0]), p])

    def tick(self, tau):
        flat_end = self.stages - self.half
        for s in range(self.stages + 1):
            c = tau - s

            @pl.when((c >= 0) & (c < self.chunks))
            def _():
                for p in (2, 0, 1) if self.parts == 3 else range(self.parts):
                    if s > 0:
                        self.copy(c, p, s - 1).wait()
                    if 0 < s <= flat_end:
                        mine = self.own(c, p, min(s, self.half))
                        got = self.r[lax.rem(c, self.slots), p, self.slot(s - 1)]
                        at = self.held(c)
                        self.g[at, p, mine] = self.g[at, p, mine] + got
                    if s == flat_end:
                        self.keep(c, p).start()
                    if s == flat_end + 1:
                        self.keep(c, p).wait()
                    if s < self.stages:
                        self.copy(c, p, s).start()


def stage_counts(n_dp):
    bits = n_dp.bit_length() - 1
    half = min(bits, 4)
    return bits, half, bits + half


def slot_rows(n_dp, rows):
    bits, half, _ = stage_counts(n_dp)
    return rows - (rows >> half) + (bits - half) * (rows >> half)


def normalise(x):
    c = x - jnp.mean(x, axis=-1, keepdims=True)
    scale = lax.rsqrt(jnp.mean(c * c, axis=-1, keepdims=True) + 1e-05)
    return c * scale, scale


def norm_back(x_hat, scale, grad):
    middle = jnp.mean(grad, axis=-1, keepdims=True)
    along = jnp.mean(grad * x_hat, axis=-1, keepdims=True)
    return (grad - middle - x_hat * along) * scale


def total(x):
    return jnp.sum(x.astype(F32), axis=0, keepdims=True)


def put_rows(ref, row, vector):
    for i in range(vector.shape[1] // LANES):
        ref[0, 0, row + i : row + i + 1, :] = vector[:, i * LANES : (i + 1) * LANES]


def add_rows(ref, row, vector):
    for i in range(vector.shape[1] // LANES):
        at = slice(row + i, row + i + 1)
        ref[0, 0, at, :] = ref[0, 0, at, :] + vector[:, i * LANES : (i + 1) * LANES]


def small_plan(features, head_cols, units, vocab_local):
    plan, at = {}, 0
    for name, size in (
        ("genes", vocab_local),
        ("gain1", features),
        ("shift1", features),
        ("qbias", head_cols),
        ("vbias", head_cols),
        ("obias", features),
        ("gain2", features),
        ("shift2", features),
        ("ubias", units),
        ("dbias", features),
    ):
        count = -(-size // LANES)
        if name == "genes":
            count = -(-count // 8) * 8
        plan[name] = (at, count, size)
        at += count
    return plan, -(-at // 128) * 128


def leftover(j):
    block = 9 + j // 2
    return (17, 13)[block // 3 - 3], block % 3, j % 2


def layer(
    n_dp,
    plan,
    lengths_h,
    genes_h,
    tok_h,
    cot_h,
    gain1_h,
    shift1_h,
    qkvw_h,
    qvb_h,
    outw_h,
    obias_h,
    gain2_h,
    shift2_h,
    upw_h,
    ubias_h,
    dnw_h,
    dbias_h,
    out_ref,
    ing_ref,
    o,
    o_small,
    tok,
    cot,
    qkvw,
    outw,
    upw,
    dnw,
    norm_t,
    qs,
    ks,
    vs,
    ctx,
    t1,
    t2,
    t3,
    v,
    g,
    r,
    act_t,
    seg,
    sg,
    sr,
    lsem,
    esend,
    erecv,
    ssem,
    rsem,
    osem,
    sssem,
    srsem,
    sosem,
    vfree,
    lengths,
    genes,
    gain1,
    shift1,
    qvb,
    obias,
    gain2,
    shift2,
    ubias,
    dbias,
):
    tokens, features = tok.shape
    head_cols = qs.shape[1]
    units = dnw.shape[0]
    rbs = tokens // BLK
    dq_t, x_t = norm_t.at[:head_cols], norm_t.at[head_cols : 2 * head_cols]
    dctx, norm = ctx, ing_ref
    act, gu = out_ref.at[:, :BLK], out_ref.at[:, BLK : 2 * BLK]
    slope, dk_sum, dv_sum = v.at[:, :BLK], v.at[:, :LANES], v.at[:, LANES:BLK]
    dp, core = lax.axis_index("dp"), lax.axis_index("tensor")
    other = (dp, 1 - core)

    loads = [
        pltpu.make_async_copy(src, dst, lsem.at[i])
        for i, (src, dst) in enumerate(
            (
                (tok_h, tok),
                (lengths_h, lengths),
                (gain1_h, gain1),
                (shift1_h, shift1),
                (qkvw_h, qkvw),
                (qvb_h, qvb),
                (outw_h, outw),
                (obias_h, obias),
                (gain2_h, gain2),
                (shift2_h, shift2),
                (upw_h, upw),
                (ubias_h, ubias),
                (cot_h, cot),
                (dnw_h, dnw),
                (dbias_h, dbias),
                (genes_h, genes),
            )
        )
    ]
    for load in loads:
        load.start()

    bar = pltpu.get_barrier_semaphore()
    bits = n_dp.bit_length() - 1
    for k in range(bits):
        bit = bit_of(dp, 1 << k)
        to = (dp + (1 << k) * (1 - 2 * bit), core)
        pl.semaphore_signal(bar, inc=1, device_id=to, device_id_type=MESH)
    pl.semaphore_signal(bar, inc=1, device_id=other, device_id_type=MESH)

    big = Exchange(n_dp, o.shape[0], PARTS, SLOTS, g, r, o, ssem, rsem, osem)
    small = Exchange(n_dp, 1, 1, 1, sg, sr, o_small, sssem, srsem, sosem)

    def swap(e, src, rb):
        at = rows_at(rb, BLK)
        return pltpu.make_async_remote_copy(
            src.at[at], v.at[at], esend.at[e, rb], erecv.at[e, rb], device_id=other, device_id_type=MESH
        )

    def freed():
        pl.semaphore_signal(vfree, inc=1, device_id=other, device_id_type=MESH)

    def each(body, count=rbs):
        def step(i, carry):
            body(i)
            return carry

        lax.fori_loop(0, count, step, 0)

    def segment(position):
        ends, seg_now = 0, jnp.zeros(position.shape, jnp.int32)
        for i in range(lengths.shape[1]):
            ends = ends + lengths[0, i]
            seg_now = seg_now + (position >= ends).astype(jnp.int32)
        return seg_now

    loads[1].wait()
    seg[...] = segment(lax.broadcasted_iota(jnp.int32, (tokens, LANES), 0))
    sg[...] = jnp.zeros_like(sg)

    for i in (0, 2, 3):
        loads[i].wait()

    def first_norm(rb):
        at = rows_at(rb, BLK)
        x_hat, _ = normalise(tok[at, :].astype(F32))
        norm[at, :] = (x_hat * gain1[...][None, :] + shift1[...][None, :]).astype(BF16)

    each(first_norm)
    for load in loads[4:6]:
        load.wait()

    def project(rb):
        at = rows_at(rb, BLK)
        x = norm[at, :]
        qs[at, :] = (mm(x, qkvw[0]) + qvb[0:1, :]).astype(BF16) * BF16(HEAD**-0.5)
        ks[at, :] = mm(x, qkvw[1]).astype(BF16)
        vs[at, :] = (mm(x, qkvw[2]) + qvb[1:2, :]).astype(BF16)

    each(project)
    loads[6].wait()
    pl.semaphore_wait(bar, bits + 1)

    def attend(rb):
        at = rows_at(rb, BLK)
        seg_row = segment(lax.broadcasted_iota(jnp.int32, (1, tokens), 1))
        same = jnp.concatenate([seg[at, :]] * (tokens // LANES), axis=1) == seg_row
        heads = head_cols // HEAD

        def scores_of(h):
            cols = slice(h * HEAD, (h + 1) * HEAD)
            return jnp.where(same, mm_t(qs[at, cols], ks[:, cols]), -1000000000.0)

        ready, sides = scores_of(0), []
        for h in range(heads):
            scores = ready
            if h + 1 < heads:
                ready = scores_of(h + 1)
            e = jnp.exp(scores - jnp.max(scores, axis=-1, keepdims=True))
            inverse = 1.0 / jnp.sum(e, axis=-1, keepdims=True)
            sides.append(mm(e.astype(BF16), vs[:, h * HEAD : (h + 1) * HEAD]) * inverse)
            if h % 2:
                ctx[at, (h - 1) * HEAD : (h + 1) * HEAD] = jnp.concatenate(sides, axis=1).astype(BF16)
                sides = []
        t1[at, :] = mm(ctx[at, :], outw[...])
        swap(0, t1, rb).start()

    each(attend)
    for load in loads[7:]:
        load.wait()

    def second_norm(rb):
        at = rows_at(rb, BLK)
        swap(0, t1, rb).wait()
        hidden = tok[at, :].astype(F32) + (t1[at, :] + v[at, :]) + obias[...][None, :]
        t1[at, :] = hidden
        x_hat, _ = normalise(hidden)
        norm[at, :] = (x_hat * gain2[...][None, :] + shift2[...][None, :]).astype(BF16)
        t2[at, :] = jnp.zeros((BLK, features), F32)
        t3[at, :] = jnp.zeros((BLK, features), F32)

    each(second_norm)

    def feed_forward(u):
        ucols = rows_at(u, BLK)

        def upper(rb):
            at = rows_at(rb, BLK)
            up = mm(norm[at, :], upw[:, ucols]) + ubias[ucols][None, :]
            cdf = 0.5 * (1.0 + lax.erf(up * 0.7071067811865476))
            act[at, :] = (up * cdf).astype(BF16)
            slope[at, :] = cdf + up * (jnp.exp(-0.5 * up * up) * 0.3989422804014327)

        each(upper)
        act_t[...] = act[...].T
        for p in range(PARTS):
            g[2 * u, p] = mm(act_t[...], cot[:, p * BLK : (p + 1) * BLK])
        big.tick(u + jnp.minimum(u, 1))

        @pl.when(u == 0)
        def _():
            norm_t[...] = norm[...].T

        def lower(rb, sums):
            at = rows_at(rb, BLK)
            down_rows = dnw[ucols, :]
            grad = (mm_t(cot[at, :], down_rows) * slope[at, :]).astype(BF16)
            gu[at, :] = grad
            t2[at, :] = t2[at, :] + mm(act[at, :], down_rows)
            t3[at, :] = t3[at, :] + mm_t(grad, upw[:, ucols])
            return sums + total(grad)

        sums = lax.fori_loop(0, rbs, lower, jnp.zeros((1, BLK), F32))
        row = plan["ubias"][0] + u * (BLK // LANES)
        for i in range(BLK // LANES):
            sg[0, 0, pl.ds(row + i, 1), :] = sums[:, i * LANES : (i + 1) * LANES]
        for p in range(PARTS):
            g[2 * u + 1, p] = mm(norm_t[p * BLK : (p + 1) * BLK, :], gu[...])

        @pl.when(u == 0)
        def _():
            big.tick(1)

    each(feed_forward, units // BLK)
    freed()
    tau = units // BLK + 1

    pl.semaphore_wait(vfree, 1)
    each(lambda rb: swap(1, t3, rb).start())
    big.tick(tau)
    tau += 1

    x_t[...] = ctx[...].T

    def second_norm_back(rb):
        at = rows_at(rb, BLK)
        swap(1, t3, rb).wait()
        grad = t3[at, :] + v[at, :]
        x_hat, scale = normalise(t1[at, :])
        add_rows(sg, plan["gain2"][0], total(grad * x_hat))
        add_rows(sg, plan["shift2"][0], total(grad))
        given = cot[at, :].astype(F32)
        add_rows(sg, plan["dbias"][0], total(given))
        grad = given + norm_back(x_hat, scale, grad * gain2[...][None, :])
        t3[at, :] = grad
        norm[at, :] = grad.astype(BF16)
        add_rows(sg, plan["obias"][0], total(norm[at, :]))
        dctx[at, :] = mm_t(norm[at, :], outw[...]).astype(BF16)

    each(second_norm_back)
    freed()
    pl.semaphore_wait(vfree, 1)
    each(lambda rb: swap(2, t2, rb).start())

    for p in range(PARTS):
        branch = norm[:, p * BLK : (p + 1) * BLK]
        g[12, p] = mm(x_t[:BLK, :], branch)
        rest = mm(x_t[BLK:, :], branch)
        if p < 2:
            g[13, 1, p * LANES : (p + 1) * LANES] = rest
        else:
            g[13, 2, :LANES] = rest
    big.tick(tau)
    tau += 1

    def result(rb):
        at = rows_at(rb, BLK)
        swap(2, t2, rb).wait()
        out_ref[at, :] = (t1[at, :] + (t2[at, :] + v[at, :]) + dbias[...][None, :]).astype(BF16)

    each(result)

    x_t[...] = ks[...].T

    def attend_back(step):
        pair, qb = lax.div(step, rbs), lax.rem(step, rbs)
        at = rows_at(qb, BLK)
        cols = rows_at(pair, LANES)
        position = lax.broadcasted_iota(jnp.int32, (1, BLK), 1) + qb * BLK
        seg_row = segment(position)
        same = jnp.concatenate([seg[...]] * (BLK // LANES), axis=1) == seg_row
        dks, dvs = [], []
        for side in range(2):
            lanes = slice(side * HEAD, (side + 1) * HEAD)
            q_now, d_now = qs[at, cols][:, lanes], dctx[at, cols][:, lanes]
            scores = jnp.where(same, mm_t(ks[:, cols][:, lanes], q_now), -1000000000.0)
            e = jnp.exp(scores - jnp.max(scores, axis=0, keepdims=True))
            probs = e * (1.0 / jnp.sum(e, axis=0, keepdims=True))
            grad = mm_t(vs[:, cols][:, lanes], d_now)
            inner = jnp.sum(probs * grad, axis=0, keepdims=True)
            grad = (probs * (grad - inner)).astype(BF16)
            dvs.append(mm(probs.astype(BF16), d_now))
            dks.append(mm(grad, q_now))
            hrows = pl.ds(pl.multiple_of(pair * LANES + side * HEAD, HEAD), HEAD)
            dq_t[hrows, at] = (mm(x_t[hrows, :], grad) * HEAD**-0.5).astype(BF16)
        dk_now, dv_now = jnp.concatenate(dks, axis=1), jnp.concatenate(dvs, axis=1)

        @pl.when(qb == 0)
        def _():
            dk_sum[...] = dk_now
            dv_sum[...] = dv_now

        @pl.when(qb > 0)
        def _():
            dk_sum[...] = dk_sum[...] + dk_now
            dv_sum[...] = dv_sum[...] + dv_now

        @pl.when(qb == rbs - 1)
        def _():
            ks[:, cols] = dk_sum[...].astype(BF16)
            vs[:, cols] = dv_sum[...].astype(BF16)

        @pl.when(lax.rem(step, 3) == 1)
        def _():
            big.tick(tau + lax.div(step, 3))

    steps = rbs * (head_cols // LANES)
    each(attend_back, steps)
    freed()
    tau += steps // 3

    qs[...] = dq_t[...].T
    put_rows(sg, plan["qbias"][0], total(qs[...]))
    put_rows(sg, plan["vbias"][0], total(vs[...]))
    each(first_norm)
    norm_t[...] = norm[...].T
    for i, grads in enumerate((qs, ks, vs)):
        for j in range(PARTS):
            made = mm(norm_t[j * BLK : (j + 1) * BLK, :], grads[...])
            g[(14 + i) % HELD, j] = made[:, :BLK]
            if i * 3 + j < 8:
                c, p, side = leftover(i * 3 + j)
                g[c % HELD, p, :, side * LANES : (side + 1) * LANES] = made[:, BLK:]
            else:
                g[13, 2, LANES:, :LANES] = made[:LANES, BLK:]
                g[13, 2, LANES:, LANES:] = made[LANES:, BLK:]
    big.tick(tau)
    tau += 1

    pl.semaphore_wait(vfree, 1)

    def to_norm(rb):
        at = rows_at(rb, BLK)
        t2[at, :] = mm_t(qs[at, :], qkvw[0]) + mm_t(ks[at, :], qkvw[1]) + mm_t(vs[at, :], qkvw[2])
        swap(3, t2, rb).start()

    each(to_norm)

    def first_norm_back(rb):
        at = rows_at(rb, BLK)
        swap(3, t2, rb).wait()
        grad = t2[at, :] + v[at, :]
        x_hat, scale = normalise(tok[at, :].astype(F32))
        add_rows(sg, plan["gain1"][0], total(grad * x_hat))
        add_rows(sg, plan["shift1"][0], total(grad))
        ing_ref[at, :] = (t3[at, :] + norm_back(x_hat, scale, grad * gain1[...][None, :])).astype(BF16)

    each(first_norm_back)

    rows = plan["genes"][1]
    local = genes[...][None, :] - core * plan["genes"][2]
    high = lax.shift_right_arithmetic(local, 7)
    low = local - high * LANES
    high = (lax.broadcasted_iota(jnp.int32, (rows, tokens), 0) == high).astype(F32).astype(BF16)
    low = (lax.broadcasted_iota(jnp.int32, (LANES, tokens), 0) == low).astype(F32).astype(BF16)
    sg[0, 0, :rows, :] = mm_t(high, low)

    def finish(i, carry):
        big.tick(tau + i)
        small.tick(i)
        return carry

    left = big.chunks + big.stages - tau
    lax.fori_loop(0, max(left, small.stages + 1), finish, 0)


def run_layer(n_dp, plan, small_rows, *args):
    (lengths, genes, tok, cot, gain1, shift1, qkvw, qvb, outw, obias, gain2, shift2, upw, ubias, dnw, dbias) = args
    tokens, features = tok.shape
    units, head_cols = dnw.shape[0], outw.shape[0]
    chunks = (features * (2 * units + 4 * head_cols)) // (PARTS * BLK * BLK)
    _, _, stages = stage_counts(n_dp)
    vmem = pl.BlockSpec(memory_space=pltpu.VMEM)
    hbm = pl.BlockSpec(memory_space=pl.ANY)
    dma = pltpu.SemaphoreType.DMA
    wide = (tokens, features)
    return pl.pallas_call(
        functools.partial(layer, n_dp, plan),
        out_shape=(
            pltpu.VMEM(wide, BF16),
            pltpu.VMEM(wide, BF16),
            pltpu.VMEM((chunks, PARTS, BLK, BLK), F32),
            pltpu.VMEM((1, 1, small_rows, LANES), F32),
        ),
        in_specs=[hbm] * 16,
        out_specs=(vmem, vmem, vmem, vmem),
        scratch_shapes=[
            pltpu.VMEM(wide, BF16),
            pltpu.VMEM(wide, BF16),
            pltpu.VMEM(qkvw.shape, BF16),
            pltpu.VMEM(outw.shape, BF16),
            pltpu.VMEM(upw.shape, BF16),
            pltpu.VMEM(dnw.shape, BF16),
            pltpu.VMEM((features, tokens), BF16),
            pltpu.VMEM((tokens, head_cols), BF16),
            pltpu.VMEM((tokens, head_cols), BF16),
            pltpu.VMEM((tokens, head_cols), BF16),
            pltpu.VMEM((tokens, head_cols), BF16),
            pltpu.VMEM(wide, F32),
            pltpu.VMEM(wide, F32),
            pltpu.VMEM(wide, F32),
            pltpu.VMEM(wide, F32),
            pltpu.VMEM((HELD, PARTS, BLK, BLK), F32),
            pltpu.VMEM((SLOTS, PARTS, slot_rows(n_dp, BLK), BLK), F32),
            pltpu.VMEM((BLK, tokens), BF16),
            pltpu.VMEM((tokens, LANES), jnp.int32),
            pltpu.VMEM((1, 1, small_rows, LANES), F32),
            pltpu.VMEM((1, 1, slot_rows(n_dp, small_rows), LANES), F32),
            dma((16,)),
            dma((4, tokens // BLK)),
            dma((4, tokens // BLK)),
            dma((2, PARTS, stages)),
            dma((SLOTS, PARTS, stages)),
            dma((2, PARTS)),
            dma((1, 1, stages)),
            dma((1, 1, stages)),
            dma((1, 1)),
            pltpu.SemaphoreType.REGULAR,
            pltpu.SMEM(lengths.shape, jnp.int32),
            pltpu.VMEM(genes.shape, jnp.int32),
            *(pltpu.VMEM(x.shape, F32) for x in (gain1, shift1, qvb, obias, gain2, shift2, ubias, dbias)),
        ],
        compiler_params=pltpu.CompilerParams(
            collective_id=0, has_side_effects=True, vmem_limit_bytes=47 << 20
        ),
    )(*args)


SMALL = (2, 3, 5, 7, 8, 9, 11, 13, 14)


def hand_out(plan, packed, sums, out_ref, ing_ref, *refs):
    output, input_grad, _, _, qkv, _, out, _, _, _, up, _, down, _, _ = refs[:15]
    sem, *staged = refs[15:]
    gain1, shift1, qv, obias, gain2, shift2, ubias, dbias, genes = staged
    moves = [(out_ref, output), (ing_ref, input_grad)]
    for u in range(down.shape[0] // BLK):
        for p in range(PARTS):
            units, cols = pl.ds(u * BLK, BLK), pl.ds(p * BLK, BLK)
            moves.append((packed.at[2 * u, p], down.at[units, cols]))
            moves.append((packed.at[2 * u + 1, p], up.at[cols, units]))
    half = pl.ds(0, LANES), pl.ds(LANES, LANES)
    for p in range(PARTS):
        cols = pl.ds(p * BLK, BLK)
        moves.append((packed.at[12, p], out.at[pl.ds(0, BLK), cols]))
        rest = packed.at[13, 1 + p // 2, half[p % 2]]
        moves.append((rest, out.at[pl.ds(BLK, LANES), cols]))
    for i in range(3):
        for j in range(PARTS):
            rows, tail = pl.ds(j * BLK, BLK), pl.ds(BLK, LANES)
            moves.append((packed.at[14 + i, j], qkv.at[i, rows, pl.ds(0, BLK)]))
            if i * 3 + j < 8:
                c, p, side = leftover(i * 3 + j)
                moves.append((packed.at[c, p, pl.ds(0, BLK), half[side]], qkv.at[i, rows, tail]))
            else:
                for side in range(2):
                    rows = pl.ds(j * BLK + side * LANES, LANES)
                    moves.append((packed.at[13, 2, half[1], half[side]], qkv.at[i, rows, tail]))
    copies = [pltpu.make_async_copy(src, dst, sem.at[i]) for i, (src, dst) in enumerate(moves)]
    for copy in copies:
        copy.start()

    def vector(name, ref, *index):
        at, count, _ = plan[name]
        for i in range(count):
            ref[(*index, pl.ds(i * LANES, LANES))] = sums[0, 0, at + i]

    for name, ref in (
        ("gain1", gain1),
        ("shift1", shift1),
        ("obias", obias),
        ("gain2", gain2),
        ("shift2", shift2),
        ("ubias", ubias),
        ("dbias", dbias),
    ):
        vector(name, ref)
    vector("qbias", qv, 0)
    vector("vbias", qv, 1)
    size = plan["genes"][2]
    for i in range(-(-size // LANES)):
        part = min(LANES, size - i * LANES)
        genes[pl.ds(i * LANES, part)] = sums[0, 0, i, :part].astype(jnp.int32)
    for src, at in zip(staged, SMALL):
        copies.append(pltpu.make_async_copy(src, refs[at], sem.at[len(copies)]))
        copies[-1].start()
    for copy in copies:
        copy.wait()


def results(plan, features, head_cols, units, packed, sums, output, input_grad):
    vmem = pl.BlockSpec(memory_space=pltpu.VMEM)
    hbm = pl.BlockSpec(memory_space=pl.ANY)
    size = lambda name: (plan[name][2],)
    shapes = (
        output.shape,
        input_grad.shape,
        size("gain1"),
        size("shift1"),
        (3, features, head_cols),
        (2, head_cols),
        (head_cols, features),
        size("obias"),
        size("gain2"),
        size("shift2"),
        (features, units),
        size("ubias"),
        (units, features),
        size("dbias"),
        size("genes"),
    )
    types = [BF16, BF16] + [F32] * 12 + [jnp.int32]
    return pl.pallas_call(
        functools.partial(hand_out, plan),
        out_shape=tuple(jax.ShapeDtypeStruct(shape, kind) for shape, kind in zip(shapes, types)),
        in_specs=[vmem, vmem, vmem, vmem],
        out_specs=(hbm,) * 15,
        scratch_shapes=[
            pltpu.SemaphoreType.DMA((72,)),
            *(pltpu.VMEM(shapes[i], types[i]) for i in SMALL),
        ],
        compiler_params=pltpu.CompilerParams(vmem_limit_bytes=16 << 20),
    )(packed, sums, output, input_grad)


def on_device(
    n_dp,
    tokens,
    lengths,
    gene_ids,
    norm1_gain,
    norm1_shift,
    qkv_weight,
    qv_bias,
    out_weight,
    out_bias,
    norm2_gain,
    norm2_shift,
    up_weight,
    up_bias,
    down_weight,
    down_bias,
    cotangent,
):
    features = tokens.shape[1]
    head_cols, units = out_weight.shape[0], down_weight.shape[0]
    plan, small_rows = small_plan(features, head_cols, units, VOCAB // lax.axis_size("tensor"))
    output, input_grad, packed, sums = run_layer(
        n_dp,
        plan,
        small_rows,
        lengths,
        gene_ids,
        tokens,
        cotangent,
        norm1_gain,
        norm1_shift,
        qkv_weight.transpose(1, 0, 2),
        qv_bias,
        out_weight,
        out_bias,
        norm2_gain,
        norm2_shift,
        up_weight,
        up_bias,
        down_weight,
        down_bias,
    )
    made = list(results(plan, features, head_cols, units, packed, sums, output, input_grad))
    made[4] = made[4].transpose(1, 0, 2)
    return tuple(made)


def solution(mesh):
    return jax.shard_map(
        functools.partial(on_device, mesh.shape["dp"]),
        mesh=mesh,
        in_specs=(
            P("dp", None),
            P("dp", None),
            P("dp"),
            P(),
            P(),
            P(None, None, "tensor"),
            P(None, "tensor"),
            P("tensor", None),
            P(),
            P(),
            P(),
            P(None, "tensor"),
            P("tensor"),
            P("tensor", None),
            P(),
            P("dp", None),
        ),
        out_specs=(
            P("dp", None),
            P("dp", None),
            P(),
            P(),
            P(None, None, "tensor"),
            P(None, "tensor"),
            P("tensor", None),
            P(),
            P(),
            P(),
            P(None, "tensor"),
            P("tensor"),
            P("tensor", None),
            P(),
            P("tensor"),
        ),
        check_vma=False,
    )
```
